32 devices in a mesh: groups: 2 (over y), gx: 8 (over z, x), gy: 2 (over core).
Axes of the slice: x: 2, y: 2, z: 4, core: 2. Of those that a mesh axis runs over, the one named last changes fastest.
Arguments:
- positions: float32 [16, 2, 3, 384], P(('groups', 'gx'), 'gy'), parts along dimension 0, may hold values from -1 to 17, as said below
- species: int32 [16, 2, 384], P(('groups', 'gx'), 'gy'), parts along dimension 0, may hold values from 0 to 4
- neighbours: int32 [16, 2, 32, 384], P(('groups', 'gx'), 'gy'), parts along dimension 0, may hold values from 0 to 1440, as said below
- send_x: int32 [16, 2, 2, 384], P(('groups', 'gx'), 'gy'), parts along dimension 0, may hold values from 0 to 383
- send_y: int32 [16, 2, 2, 144], P(('groups', 'gx'), 'gy'), parts along dimension 0, may hold values from 0 to 1151, as said below
- two_weight: float32 [18, 128], replicated, may hold values from -1.5 to 1.5
- two_bias: float32 [128], replicated, may hold values from -3 to 3
- env_weight: float32 [2, 128, 32], replicated, may hold values from -0.5 to 0.5
- value_weight: float32 [2, 128, 32], replicated, may hold values from -0.5 to 0.5
- latent_weight: float32 [2, 224, 128], replicated, may hold values from -0.375 to 0.375
- latent_bias: float32 [2, 128], replicated, may hold values from -3 to 3
- out_weight: float32 [128], replicated, may hold values from -0.5 to 0.5
- species_shift: float32 [5], replicated, may hold values from -1 to 1
Outputs:
- atom_energy: float32 [16, 2, 384], P(('groups', 'gx'), 'gy'), parts along dimension 0
- forces: float32 [16, 2, 3, 384], P(('groups', 'gx'), 'gy'), parts along dimension 0
- mean_energy: float32 [2], P('groups'), parts along dimension 0
The draws below stay inside these ranges and needn't reach their ends.
There are 2 independent parts, one for each index of `groups`. The reference program is written for one: setup_inputs(seed, part) draws one part's arguments, and reference() takes and returns one part's arrays. A program takes and returns all parts, laid end to end along the dimension named above; an argument that names none is the same for every part. Nothing has to cross between parts.
Inputs may be any that keep to these rules, and one draw needn't show every extreme that they name: `neighbours`: entries equal to 1440 point to the padding slot. `send_y`: the two rows of a box hold distinct entries. `positions`: lattice sites jittered: two atoms of the extended list are at least 0.4 apart.
All inputs are finite; a program needn't handle non-finite values.
Results may differ from the reference program's by a relative error of at most 0.0003.
Values sent between devices are 32-bit elements; how exact they have to be, the bound alone decides.
No kernel may reach another device: no remote copies, remote signals or barrier semaphores. Data moves between devices by JAX's collectives and lax.ppermute only.
A program may use at most 256 MiB of HBM per device.

```python
import math
import jax
import jax.numpy as jnp
import numpy as np
from jax import lax

LATENT = 128
TENSORS = 32
BASIS = 8
SPECIES = 5
LAYERS = 2
NEIGHBOURS = 32
SITES_X = 2
SITES_Y = 16
SITES_Z = 12
ATOMS = 384
FACE_X = 384
FACE_Y = 144
EXTENDED = 1441
BOXES_X = 8
BOXES_Y = 2


def lattice_order(key):
    keys = jax.random.split(jax.random.fold_in(key, 101), BOXES_X * BOXES_Y)
    order = jax.vmap(lambda sub: jax.random.permutation(sub, ATOMS))(keys)
    return order.reshape(BOXES_X, BOXES_Y, ATOMS).astype(jnp.int32)


def site_coords(site):
    return (site // (SITES_Y * SITES_Z), site // SITES_Z % SITES_Y, site % SITES_Z)


def offset_table():
    found = []
    for step_x in range(-2, 3):
        for step_y in range(-2, 3):
            for step_z in range(-2, 3):
                square = step_x * step_x + step_y * step_y + step_z * step_z
                if 0 < square <= 4:
                    found.append([step_x, step_y, step_z])
    return np.array(found, dtype=np.int32)


def draw_positions(key, part):
    order = lattice_order(key)
    key = jax.random.fold_in(key, 1)
    site = jnp.argsort(order, axis=-1).astype(jnp.int32)
    first, second, third = site_coords(site)
    grid = jnp.stack([first, second, third], 2).astype(jnp.float32) + 0.5
    jitter = jax.random.uniform(key, grid.shape, jnp.float32, -0.25, 0.25)
    return grid + jitter


def draw_neighbours(key, part):
    order = lattice_order(key)
    key = jax.random.fold_in(key, 2)
    site = jnp.argsort(order, axis=-1).astype(jnp.int32)
    first, second, third = site_coords(site)
    table = offset_table()
    near_x = first[:, :, None, :] + jnp.asarray(table[:, 0])[:, None]
    near_y = second[:, :, None, :] + jnp.asarray(table[:, 1])[:, None]
    near_z = third[:, :, None, :] + jnp.asarray(table[:, 2])[:, None]
    inside_x = (near_x >= 0) & (near_x < SITES_X)
    inside_y = (near_y >= 0) & (near_y < SITES_Y)
    target = (jnp.clip(near_x, 0, SITES_X - 1) * SITES_Y + jnp.clip(near_y, 0, SITES_Y - 1)) * SITES_Z + jnp.clip(near_z, 0, SITES_Z - 1)
    own_slot = jnp.take_along_axis(order, target.reshape(BOXES_X, BOXES_Y, -1), axis=-1).reshape(target.shape)
    ghost_x = jnp.where(near_x < 0, ATOMS + ((near_x + 2) * SITES_Y + near_y) * SITES_Z + near_z, ATOMS + FACE_X + ((near_x - SITES_X) * SITES_Y + near_y) * SITES_Z + near_z)
    ghost_y = jnp.where(near_y < 0, ATOMS + 2 * FACE_X + ((near_x + 2) * 2 + near_y + 2) * SITES_Z + near_z, ATOMS + 2 * FACE_X + FACE_Y + ((near_x + 2) * 2 + near_y - SITES_Y) * SITES_Z + near_z)
    slot = jnp.where(inside_y, jnp.where(inside_x, own_slot, ghost_x), ghost_y)
    dropped = (near_z < 0) | (near_z >= SITES_Z) | (jax.random.randint(key, slot.shape, 0, 8) == 0)
    return jnp.where(dropped, EXTENDED - 1, slot).astype(jnp.int32)


def draw_send_x(key, part):
    order = lattice_order(key)
    counter = jnp.arange(FACE_X, dtype=jnp.int32)
    low = jnp.take(order, counter, axis=-1)
    high = jnp.take(order, (SITES_X - 2) * SITES_Y * SITES_Z + counter, axis=-1)
    return jnp.stack([low, high], 2).astype(jnp.int32)


def draw_send_y(key, part):
    order = lattice_order(key)
    counter = jnp.arange(FACE_Y, dtype=jnp.int32)
    along = counter // (2 * SITES_Z) - 2
    layer = counter // SITES_Z % 2
    height = counter % SITES_Z
    inside = (along >= 0) & (along < SITES_X)
    rows = []
    for which in range(2):
        across = layer + which * (SITES_Y - 2)
        target = (jnp.clip(along, 0, SITES_X - 1) * SITES_Y + across) * SITES_Z + height
        own = jnp.take(order, target, axis=-1)
        ghost = jnp.where(along < 0, ATOMS + ((along + 2) * SITES_Y + across) * SITES_Z + height, ATOMS + FACE_X + ((along - SITES_X) * SITES_Y + across) * SITES_Z + height)
        rows.append(jnp.where(inside[None, None], own, ghost[None, None]))
    return jnp.stack(rows, 2).astype(jnp.int32)


def touch_ends(drawn, key, least, high):
    longest = drawn.shape.index(max(drawn.shape))
    spots = []
    for shift in (0, 1):
        where = [jax.random.randint(jax.random.fold_in(key, axis), (), 0, length) for axis, length in enumerate(drawn.shape)]
        where[longest] = (where[longest] + shift) % drawn.shape[longest]
        spots.append(tuple(where))
    return drawn.at[spots[0]].set(least).at[spots[1]].set(high)


def bell_draw(rng, shape, scale, reach, kind=jnp.bfloat16):
    return jnp.clip(scale * jax.random.normal(rng, shape, jnp.float32), -reach, reach).astype(kind)


def setup_inputs(seed: int = 0, part: int = 0) -> dict:
    key_of = jax.random.split(jax.random.key(seed), 14)
    own_keys = jax.random.split(jax.random.fold_in(key_of[13], part), 14)
    return {
        "positions": draw_positions(jax.random.fold_in(jax.random.fold_in(key_of[13], part), 71), part),
        "species": touch_ends(jax.random.randint(own_keys[1], (BOXES_X, BOXES_Y, ATOMS), 0, SPECIES), jax.random.fold_in(own_keys[1], 1), 0, SPECIES - 1).astype(jnp.int32),
        "neighbours": draw_neighbours(jax.random.fold_in(jax.random.fold_in(key_of[13], part), 71), part),
        "send_x": draw_send_x(jax.random.fold_in(jax.random.fold_in(key_of[13], part), 71), part),
        "send_y": draw_send_y(jax.random.fold_in(jax.random.fold_in(key_of[13], part), 71), part),
        "two_weight": bell_draw(key_of[5], (2 * SPECIES + BASIS, LATENT), (2 * SPECIES + BASIS) ** -0.5, 1.5, jnp.float32),
        "two_bias": bell_draw(key_of[6], (LATENT,), 0.5, 3.0, jnp.float32),
        "env_weight": bell_draw(key_of[7], (LAYERS, LATENT, TENSORS), LATENT ** -0.5, 0.5, jnp.float32),
        "value_weight": bell_draw(key_of[8], (LAYERS, LATENT, TENSORS), LATENT ** -0.5, 0.5, jnp.float32),
        "latent_weight": bell_draw(key_of[9], (LAYERS, LATENT + 3 * TENSORS, LATENT), (LATENT + 3 * TENSORS) ** -0.5, 0.375, jnp.float32),
        "latent_bias": bell_draw(key_of[10], (LAYERS, LATENT), 0.5, 3.0, jnp.float32),
        "out_weight": bell_draw(key_of[11], (LATENT,), LATENT ** -0.5, 0.5, jnp.float32),
        "species_shift": jnp.clip(jax.random.uniform(key_of[12], (SPECIES,), jnp.float32, -1.0, 1.0), -1.0, 1.0),
    }


cutoff_radius = 2.5

def harmonics(unit):
    ux, uy, uz = (unit[0], unit[1], unit[2])
    root = math.sqrt(3.0)
    return jnp.stack([jnp.ones_like(ux), ux, uy, uz, root * ux * uy, root * uy * uz, 0.5 * (3.0 * uz * uz - 1.0), root * ux * uz, 0.5 * root * (ux * ux - uy * uy)])

def geometry(ext_pos, nbrs):
    count, atoms = nbrs.shape
    index = nbrs.reshape(-1)
    other = jnp.take(ext_pos, index, axis=1)
    centre = jnp.tile(ext_pos[:, :atoms], (1, count))
    vector = other - centre
    dist = jnp.sqrt(lax.optimization_barrier(jnp.sum(vector * vector, axis=0)))
    unit = vector / dist
    scaled = jnp.minimum(dist / cutoff_radius, 1.0)
    envelope = 1.0 - 28.0 * scaled ** 6 + 48.0 * scaled ** 7 - 21.0 * scaled ** 8
    orders = (jnp.arange(BASIS) + 1).astype(jnp.float32)[:, None]
    radial = math.sqrt(2.0 / cutoff_radius) * jnp.sin(orders * math.pi * dist / cutoff_radius) / dist * envelope
    return (harmonics(unit), envelope, radial)

def pair_latent(radial, ext_spec, nbrs, two_weight, two_bias):
    count, atoms = nbrs.shape
    kinds = jnp.arange(SPECIES).astype(jnp.float32)[:, None]
    spec_centre = jnp.tile(ext_spec[:atoms], (count,))
    spec_other = jnp.take(ext_spec, nbrs.reshape(-1))
    onehot_c = (spec_centre[None] == kinds).astype(jnp.float32)
    onehot_o = (spec_other[None] == kinds).astype(jnp.float32)
    features = jnp.concatenate([onehot_c, onehot_o, radial], 0)
    pre = jnp.dot(two_weight.T, features, precision=lax.Precision.HIGHEST) + two_bias[:, None]
    return jax.nn.silu(pre)

def environment(latent, sph, envelope, weight, count, atoms):
    embed = jnp.dot(weight.T, latent, precision=lax.Precision.HIGHEST) * envelope
    width = embed.shape[0]
    product = sph[:, None, :] * embed[None]
    return product.reshape(9 * width, count, atoms).sum(1) / math.sqrt(count)

def advance(latent, sph, env_own, ghost_env, nbrs, value_w, latent_w, latent_b):
    count, atoms = nbrs.shape
    width = value_w.shape[1]
    value = jnp.dot(value_w.T, latent, precision=lax.Precision.HIGHEST)
    ext_env = jnp.concatenate([env_own, ghost_env], 1)
    env_centre = jnp.tile(env_own, (1, count))
    env_other = jnp.take(ext_env, nbrs.reshape(-1), axis=1)
    mixed = (env_centre + env_other).reshape(9, width, -1) * sph[:, None, :] * value[None]
    scalars = jnp.concatenate([mixed[0], mixed[1:4].sum(0), mixed[4:9].sum(0)], 0)
    joined = jnp.concatenate([latent, scalars], 0)
    pre = jnp.dot(latent_w.T, joined, precision=lax.Precision.HIGHEST) + latent_b[:, None]
    return latent + jax.nn.silu(pre)

def readout(latent, envelope, own_spec, nbrs, out_weight, species_shift):
    count, atoms = nbrs.shape
    edge = jnp.dot(out_weight, latent, precision=lax.Precision.HIGHEST) * envelope / math.sqrt(count)
    kinds = jnp.arange(SPECIES).astype(jnp.float32)[:, None]
    onehot = (own_spec[None] == kinds).astype(jnp.float32)
    offset = jnp.dot(species_shift, onehot, precision=lax.Precision.HIGHEST)
    return edge.reshape(count, atoms).sum(0) + offset

def extend(rows, send_x, send_y, off_x, off_y, dummy):
    pick = jax.vmap(jax.vmap(lambda block, index: jnp.take(block, index, axis=1)))
    low = pick(rows, send_x[:, :, 0])
    high = pick(rows, send_x[:, :, 1])
    wide = jnp.concatenate([rows, jnp.roll(high, 1, axis=0) - off_x, jnp.roll(low, -1, axis=0) + off_x], 3)
    low_y = pick(wide, send_y[:, :, 0])
    high_y = pick(wide, send_y[:, :, 1])
    shape = (rows.shape[0], rows.shape[1], rows.shape[2], 1)
    padding = jnp.broadcast_to(dummy, shape)
    return jnp.concatenate([wide, jnp.roll(high_y, 1, axis=1) - off_y, jnp.roll(low_y, -1, axis=1) + off_y, padding], 3)

def reference(positions, species, neighbours, send_x, send_y, two_weight, two_bias, env_weight, value_weight, latent_weight, latent_bias, out_weight, species_shift):
    boxes = BOXES_X * BOXES_Y

    def total(coords):
        rows = jnp.concatenate([coords, species[:, :, None, :].astype(jnp.float32)], 2)
        off_x = jnp.array([SITES_X, 0.0, 0.0, 0.0], jnp.float32)[:, None]
        off_y = jnp.array([0.0, SITES_Y, 0.0, 0.0], jnp.float32)[:, None]
        dummy = jnp.array([0.0, 0.0, -1000.0, -1.0], jnp.float32)[:, None]
        ext = extend(rows, send_x, send_y, off_x, off_y, dummy)
        ext_pos = ext[:, :, :3].reshape(boxes, 3, EXTENDED)
        ext_spec = ext[:, :, 3].reshape(boxes, EXTENDED)
        nbrs = neighbours.reshape(boxes, NEIGHBOURS, ATOMS)

        def first(item):
            where, kinds, links = item
            sph, envelope, radial = geometry(where, links)
            latent = pair_latent(radial, kinds, links, two_weight, two_bias)
            env = environment(latent, sph, envelope, env_weight[0], NEIGHBOURS, ATOMS)
            return (sph, envelope, latent, env)
        sph, envelope, latent, env = lax.map(jax.checkpoint(first), (ext_pos, ext_spec, nbrs))
        zero = jnp.zeros((9 * TENSORS, 1), jnp.float32)
        energies = None
        for layer in range(LAYERS):
            grid = env.reshape(BOXES_X, BOXES_Y, 9 * TENSORS, ATOMS)
            ghost = extend(grid, send_x, send_y, zero, zero, zero)[..., ATOMS:].reshape(boxes, 9 * TENSORS, -1)
            if layer + 1 < LAYERS:

                def middle(item, layer=layer):
                    harm, cut, lat, own, far, links = item
                    fresh = advance(lat, harm, own, far, links, value_weight[layer], latent_weight[layer], latent_bias[layer])
                    return (fresh, environment(fresh, harm, cut, env_weight[layer + 1], NEIGHBOURS, ATOMS))
                latent, env = lax.map(jax.checkpoint(middle), (sph, envelope, latent, env, ghost, nbrs))
            else:

                def last(item, layer=layer):
                    harm, cut, lat, own, far, links, kinds = item
                    fresh = advance(lat, harm, own, far, links, value_weight[layer], latent_weight[layer], latent_bias[layer])
                    return readout(fresh, cut, kinds[:ATOMS], links, out_weight, species_shift)
                energies = lax.map(jax.checkpoint(last), (sph, envelope, latent, env, ghost, nbrs, ext_spec))
        energies = energies.reshape(BOXES_X, BOXES_Y, ATOMS)
        return (jnp.sum(energies), energies)
    grads, energies = jax.grad(total, has_aux=True)(positions)
    return (energies, -grads, jnp.mean(energies).reshape(1))
```

```python
from functools import partial
import math

import jax
import jax.numpy as jnp
from jax import lax
from jax.experimental import pallas as pl
from jax.experimental.pallas import tpu as pltpu
from jax.sharding import PartitionSpec as P

BASIS = 8
SPECIES = 5
SITES_X = 2
SITES_Y = 16
CUTOFF = 2.5
LATENT = 128
TENSORS = 32
HARM = 9
ROOT3 = math.sqrt(3.0)
DEGREE = (0, 1, 1, 1, 2, 2, 2, 2, 2)
F32 = jnp.float32
BF16 = jnp.bfloat16
WHOLE = pl.BlockSpec(memory_space=pltpu.VMEM)
SCALARS = pl.BlockSpec(memory_space=pltpu.SMEM)


def params():
    return pltpu.CompilerParams(vmem_limit_bytes=60 << 20)


def passed_along(value, axis, by):
    count = lax.axis_size(axis)
    return lax.ppermute(value, axis, [(i, (i + by) % count) for i in range(count)])


def dot(a, b):
    return jnp.dot(a, b, preferred_element_type=F32)


def dot_nt(a, b):
    return lax.dot_general(a, b, (((1,), (1,)), ((), ())), preferred_element_type=F32)


def halves(value):
    high = value.astype(BF16)
    return high, (value - high.astype(F32)).astype(BF16)


def stacked(value):
    return jnp.concatenate(halves(value), 0)


def product(weights, value):
    rows = weights.shape[0] // 2
    both = dot(weights, stacked(value))
    return both[:rows] + both[rows:]


def rounded(value):
    high = value.astype(BF16).astype(F32)
    return high, value - high


def weights_kernel(two, bias, env, val, lat, lat_bias, out_w, *outs):
    two_out, mix_out, s_out, back_out, ev_out, rad_out, cols = outs

    def depth_stack(piece):
        high, low = rounded(piece)
        top = jnp.concatenate([high, high], 0)
        bottom = jnp.concatenate([low, jnp.zeros_like(low)], 0)
        return top.T, bottom.T

    def join(pieces):
        tops, bottoms = zip(*[depth_stack(p) for p in pieces])
        return jnp.concatenate(list(tops) + list(bottoms), 0).astype(BF16)

    def wide_stack(piece):
        high, low = rounded(piece)
        top = jnp.concatenate([high, high], 1)
        bottom = jnp.concatenate([low, jnp.zeros_like(low)], 1)
        return jnp.concatenate([top, bottom], 0).astype(BF16)

    width = two.shape[1]
    first = jnp.concatenate(
        [
            two[0:SPECIES, :],
            bias[...],
            jnp.zeros((2, width), F32),
            two[SPECIES : 2 * SPECIES, :],
            jnp.zeros((3, width), F32),
            two[2 * SPECIES :, :],
        ],
        0,
    )
    two_out[...] = join([first])
    rad_out[...] = wide_stack(two[2 * SPECIES :, :])
    for layer in range(env.shape[0]):
        latent = lat[layer]
        mix_out[layer] = join([env[layer], val[layer], latent[:width]])
        s_out[layer] = join([latent[width:]])
        back_out[layer] = wide_stack(latent)
        high = [rounded(env[layer].T), rounded(val[layer].T)]
        top = jnp.concatenate([high[0][0], high[1][0]] * 2, 0).T
        bottom = jnp.concatenate([high[0][1], high[1][1]] + [jnp.zeros_like(high[0][1])] * 2, 0).T
        ev_out[layer] = jnp.concatenate([top, bottom], 0).astype(BF16)
    columns = jnp.concatenate(
        [lat_bias[...], out_w[...], jnp.zeros((8 - lat_bias.shape[0] - 1, width), F32)], 0
    )
    cols[...] = columns.T


def prepare_weights(two, bias, env, val, lat, lat_bias, out_w):
    layers = env.shape[0]
    shapes = [
        (2 * LATENT, 48),
        (layers, 2 * (LATENT + 2 * TENSORS), 2 * LATENT),
        (layers, 2 * LATENT, 6 * TENSORS),
        (layers, 2 * (LATENT + 3 * TENSORS), 2 * LATENT),
        (layers, 2 * LATENT, 4 * TENSORS),
        (2 * BASIS, 2 * LATENT),
    ]
    out_shape = [jax.ShapeDtypeStruct(s, BF16) for s in shapes]
    out_shape.append(jax.ShapeDtypeStruct((LATENT, 8), F32))
    return pl.pallas_call(
        weights_kernel,
        out_shape=out_shape,
        in_specs=[WHOLE] * 7,
        out_specs=[WHOLE] * 7,
        compiler_params=params(),
        name="prepare_weights",
    )(two, bias[None], env, val, lat, lat_bias, out_w[None])


def shifted(rows, by_x, by_y):
    lane_row = lax.broadcasted_iota(jnp.int32, rows.shape, 0)
    return rows + jnp.where(lane_row == 0, by_x, jnp.where(lane_row == 1, by_y, 0.0))


def lane_pick(table, row, index, blocks):
    low = index & 127
    high = lax.shift_right_arithmetic(index, 7)
    found = jnp.zeros(index.shape, F32)
    for block in range(blocks):
        span = slice(block * 128, block * 128 + 128)
        source = table[...][:, span] if row is None else table[row : row + 1, span]
        source = jnp.broadcast_to(source, index.shape)
        taken = jnp.take_along_axis(source, low, axis=1)
        found = jnp.where(high == block, taken, found)
    return found


def fill_wide(own, below, above, table, remap):
    atoms = own.shape[1]
    table[:, 0:atoms] = own[...]
    table[:, atoms : 2 * atoms] = shifted(below[...], -float(SITES_X), 0.0)
    table[:, 2 * atoms : 3 * atoms] = shifted(above[...], float(SITES_X), 0.0)
    lanes = lax.broadcasted_iota(jnp.int32, (1, atoms), 1).astype(F32)
    remap[:, 0:atoms] = lanes
    remap[:, atoms : 2 * atoms] = below[5:6, :] + float(atoms)
    remap[:, 2 * atoms : 3 * atoms] = above[4:5, :] + float(2 * atoms)


def lend_kernel(own, below, above, wanted, rows_out, wanted_out, table, remap):
    atoms = own.shape[1]
    blocks = 3 * atoms // 128
    fill_wide(own, below, above, table, remap)
    for tile in range(wanted.shape[1] // 128):
        span = slice(tile * 128, tile * 128 + 128)
        index = jnp.broadcast_to(wanted[:, span], (8, 128))
        place = lane_pick(remap, 0, index, blocks).astype(jnp.int32)
        place = jnp.where(index < 0, -1, place)
        wanted_out[:, span] = place[0:1]
        rows_out[:, span] = lane_pick(table, None, place, blocks)


def lend_rows(own, below, above, wanted):
    atoms = own.shape[1]
    return pl.pallas_call(
        lend_kernel,
        out_shape=[
            jax.ShapeDtypeStruct(wanted.shape[:0] + (8, wanted.shape[1]), F32),
            jax.ShapeDtypeStruct(wanted.shape, jnp.int32),
        ],
        in_specs=[WHOLE] * 4,
        out_specs=[WHOLE] * 2,
        scratch_shapes=[pltpu.VMEM((8, 3 * atoms), F32), pltpu.VMEM((1, 3 * atoms), F32)],
        compiler_params=params(),
        name="lend_rows",
    )(own, below, above, wanted)


def distances(vx, vy, vz):
    dist = jnp.sqrt(vx * vx + vy * vy + vz * vz)
    inverse = 1.0 / dist
    scaled = jnp.minimum(dist * (1.0 / CUTOFF), 1.0)
    second = scaled * scaled
    fourth = second * second
    sixth = fourth * second
    cut = 1.0 - 28.0 * sixth + 48.0 * (sixth * scaled) - 21.0 * (sixth * second)
    rest = 1.0 - scaled
    slope = (-168.0 / CUTOFF) * (fourth * scaled) * (rest * rest)
    angle = scaled * math.pi
    return inverse, cut, slope, jnp.sin(angle), jnp.cos(angle)


def geometry_kernel(
    own, below, above, across, nbrs, shift, vec_out, geo_out, nbr_out, base_out, table, remap, face
):
    atoms = own.shape[1]
    slots = nbrs.shape[0]
    blocks = table.shape[1] // 128
    fill_wide(own, below, above, table, remap)
    lanes = lax.broadcasted_iota(jnp.int32, (8, atoms), 1)
    rows = lax.broadcasted_iota(jnp.int32, (8, atoms), 0)
    moved = across[...] + jnp.where(
        rows == 1, jnp.where(lanes < face, -float(SITES_Y), float(SITES_Y)), 0.0
    )
    empty = jnp.where(rows == 2, -1000.0, jnp.where(rows == 3, -1.0, 0.0))
    table[:, 3 * atoms : 4 * atoms] = jnp.where(lanes < 2 * face, moved, empty)
    remap[:, 3 * atoms : 4 * atoms] = (
        lax.broadcasted_iota(jnp.int32, (1, atoms), 1) + 3 * atoms
    ).astype(F32)
    base = jnp.zeros((1, atoms), F32)
    for kind in range(SPECIES):
        base = base + jnp.where(own[3:4, :] == float(kind), shift[kind], 0.0)
    base_out[...] = base
    for group in range(slots // 8):
        for tile in range(atoms // 128):
            up = slice(group * 8, group * 8 + 8)
            span = slice(tile * 128, tile * 128 + 128)
            index = nbrs[up, span]
            index = lane_pick(remap, 0, index, blocks).astype(jnp.int32)
            nbr_out[up, span] = index
            vx = lane_pick(table, 0, index, blocks) - own[0:1, span]
            vy = lane_pick(table, 1, index, blocks) - own[1:2, span]
            vz = lane_pick(table, 2, index, blocks) - own[2:3, span]
            kind = lane_pick(table, 3, index, blocks)
            vec_out[0, up, span] = vx
            vec_out[1, up, span] = vy
            vec_out[2, up, span] = vz
            inverse, cut, _, sine, cosine = distances(vx, vy, vz)
            ux, uy, uz = vx * inverse, vy * inverse, vz * inverse
            harm = [
                ux,
                uy,
                uz,
                ROOT3 * ux * uy,
                ROOT3 * uy * uz,
                0.5 * (3.0 * uz * uz - 1.0),
                ROOT3 * ux * uz,
                0.5 * ROOT3 * (ux * ux - uy * uy),
            ]
            geo_out[0, up, span] = cut
            for number, value in enumerate(harm):
                geo_out[1 + number, up, span] = value
            scale = math.sqrt(2.0 / CUTOFF) * inverse * cut
            before, now = jnp.zeros_like(sine), sine
            for number in range(BASIS):
                geo_out[9 + number, up, span] = now * scale
                before, now = now, 2.0 * cosine * now - before
            geo_out[17, up, span] = kind


def geometry(own, below, above, across, nbrs, shift, face):
    slots, atoms = nbrs.shape
    return pl.pallas_call(
        partial(geometry_kernel, face=face),
        out_shape=[
            jax.ShapeDtypeStruct((3, slots, atoms), F32),
            jax.ShapeDtypeStruct((18, slots, atoms), F32),
            jax.ShapeDtypeStruct((slots, atoms), jnp.int32),
            jax.ShapeDtypeStruct((1, atoms), F32),
        ],
        in_specs=[WHOLE] * 5 + [SCALARS],
        out_specs=[WHOLE] * 4,
        scratch_shapes=[pltpu.VMEM((8, 4 * atoms), F32), pltpu.VMEM((1, 4 * atoms), F32)],
        compiler_params=params(),
        name="geometry",
    )(own, below, above, across, nbrs, shift)


def silu_pair(pre):
    gate = 1.0 / (1.0 + jnp.exp(-pre))
    value = pre * gate
    return value, gate + value * (1.0 - gate)


def first_kernel(
    geo, own, two_w, mix_w, cols, x_out, slope_out, emb_out, val_out, lx_out, env_out, *, group
):
    step = pl.program_id(0)
    atoms = own.shape[1]
    norm = 1.0 / math.sqrt(geo.shape[1])
    kinds = lax.broadcasted_iota(jnp.int32, (8, atoms), 0)
    kinds_f = kinds.astype(F32)
    centre = jnp.where((own[3:4, :] == kinds_f) & (kinds < SPECIES), 1.0, 0.0)
    centre = jnp.where(kinds == SPECIES, 1.0, centre)
    parts = []
    for q in range(group):
        k = step * group + q
        other = jnp.where(geo[17, pl.ds(k, 1), :] == kinds_f, 1.0, 0.0)
        radial = [geo[9 + n, pl.ds(k, 1), :] for n in range(BASIS)]
        parts.append(jnp.concatenate([centre, other] + radial, 0))
    features = jnp.concatenate(parts, 1)
    x, slope = silu_pair(product(two_w[...], features))
    x_out[...] = x
    slope_out[...] = slope
    mixed = product(mix_w[0], x)
    emb_out[...] = mixed[:TENSORS]
    val_out[...] = mixed[TENSORS : 2 * TENSORS]
    lx_out[...] = mixed[2 * TENSORS :] + cols[:, 0:1]

    @pl.when(step == 0)
    def _():
        env_out[...] = jnp.zeros_like(env_out)

    add_env(geo, step, group, mixed, env_out, atoms, norm)


def add_env(geo, step, group, embed, env_out, atoms, norm):
    for m in range(HARM):
        total = env_out[m * TENSORS : (m + 1) * TENSORS, :]
        for q in range(group):
            k = step * group + q
            cut = geo[0, pl.ds(k, 1), :] * norm
            factor = cut if m == 0 else cut * geo[m, pl.ds(k, 1), :]
            total = total + embed[:TENSORS, q * atoms : (q + 1) * atoms] * factor
        env_out[m * TENSORS : (m + 1) * TENSORS, :] = total


def edge_spec(rows, width):
    return pl.BlockSpec((rows, width), lambda i: (0, i))


def edge_shape(rows, edges):
    return jax.ShapeDtypeStruct((rows, edges), F32)


def first_pass(geo, own, two_w, mix_w, cols, group):
    _, slots, atoms = geo.shape
    width = group * atoms
    edges = slots * atoms
    rows = (LATENT, LATENT, TENSORS, TENSORS, LATENT)
    return pl.pallas_call(
        partial(first_kernel, group=group),
        grid=(slots // group,),
        out_shape=[edge_shape(r, edges) for r in rows] + [edge_shape(HARM * TENSORS, atoms)],
        in_specs=[WHOLE] * 5,
        out_specs=[edge_spec(r, width) for r in rows] + [WHOLE],
        compiler_params=params(),
        name="first_pass",
    )(geo, own, two_w, mix_w, cols)


def lend_env_kernel(own, below, above, wanted, out):
    atoms = own.shape[1]
    total = jnp.zeros(out.shape, F32)
    for number, block in enumerate((own, below, above)):
        rows = lax.broadcasted_iota(jnp.int32, (atoms, wanted.shape[1]), 0) + number * atoms
        chosen = (rows == wanted[...]).astype(F32).astype(BF16)
        both = dot(stacked(block[...]), chosen)
        total = total + both[: out.shape[0]] + both[out.shape[0] :]
    out[...] = total


def lend_env(own, below, above, wanted):
    return pl.pallas_call(
        lend_env_kernel,
        out_shape=jax.ShapeDtypeStruct(own.shape, F32),
        in_specs=[WHOLE] * 4,
        out_specs=WHOLE,
        compiler_params=params(),
        name="lend_env",
    )(own, below, above, wanted)


def take_back_kernel(returned, wanted, below, above, own, own_out, below_out, above_out):
    atoms = own.shape[1]
    rows_total = returned.shape[0]
    value = stacked(returned[...])
    for number, (block, out) in enumerate(((own, own_out), (below, below_out), (above, above_out))):
        rows = lax.broadcasted_iota(jnp.int32, (atoms, wanted.shape[1]), 0) + number * atoms
        chosen = (rows == wanted[...]).astype(F32).astype(BF16)
        both = dot_nt(value, chosen)
        out[...] = block[...] + both[:rows_total] + both[rows_total:]


def take_back(returned, wanted, own, below, above):
    return pl.pallas_call(
        take_back_kernel,
        out_shape=[jax.ShapeDtypeStruct(own.shape, F32)] * 3,
        in_specs=[WHOLE] * 5,
        out_specs=[WHOLE] * 3,
        compiler_params=params(),
        name="take_back",
    )(returned, wanted, below, above, own)


def chosen_columns(nbrs, step, group, columns):
    parts = []
    for q in range(group):
        index = nbrs[pl.ds(step * group + q, 1), :]
        rows = lax.broadcasted_iota(jnp.int32, (columns, index.shape[1]), 0)
        parts.append((rows == index).astype(F32).astype(BF16))
    return jnp.concatenate(parts, 1)


def fill_split(own, below, above, across, split):
    atoms = own.shape[1]
    rows = own.shape[0]
    for number, block in enumerate((own, below, above, across)):
        span = slice(number * atoms, (number + 1) * atoms)
        high, low = halves(block[...])
        split[:rows, span] = high
        split[rows:, span] = low


def gathered(split, chosen, own, g, group):
    rows = HARM * TENSORS
    atoms = own.shape[1]
    both = dot(split[...], chosen)
    for q in range(group):
        span = slice(q * atoms, (q + 1) * atoms)
        g[:, span] = both[:rows, span] + both[rows:, span] + own[...]


def contracted(geo, step, group, g, value, atoms):
    columns = []
    for q in range(group):
        k = step * group + q
        span = slice(q * atoms, (q + 1) * atoms)
        sums = [g[0:TENSORS, span], None, None]
        for m in range(1, HARM):
            term = g[m * TENSORS : (m + 1) * TENSORS, span] * geo[m, pl.ds(k, 1), :]
            d = DEGREE[m]
            sums[d] = term if sums[d] is None else sums[d] + term
        columns.append(jnp.concatenate(sums, 0))
    sums = jnp.concatenate(columns, 1)
    return sums, sums * jnp.concatenate([value] * 3, 0)


def middle_kernel(
    geo, nbrs, own, below, above, across, x, lx, val, s_w, mix_w, cols,
    g, slope_out, x_out, emb_out, val_out, lx_out, env_out, split, *, group,
):
    step = pl.program_id(0)
    atoms = own.shape[1]
    norm = 1.0 / math.sqrt(geo.shape[1])

    @pl.when(step == 0)
    def _():
        fill_split(own, below, above, across, split)
        env_out[...] = jnp.zeros_like(env_out)

    chosen = chosen_columns(nbrs, step, group, split.shape[1])
    gathered(split, chosen, own, g, group)
    _, s = contracted(geo, step, group, g, val[...], atoms)
    update, slope = silu_pair(lx[...] + product(s_w[0], s))
    slope_out[...] = slope
    fresh = x[...] + update
    x_out[...] = fresh
    mixed = product(mix_w[1], fresh)
    emb_out[...] = mixed[:TENSORS]
    val_out[...] = mixed[TENSORS : 2 * TENSORS]
    lx_out[...] = mixed[2 * TENSORS :] + cols[:, 1:2]
    add_env(geo, step, group, mixed, env_out, atoms, norm)


def middle_pass(geo, nbrs, blocks, x, lx, val, s_w, mix_w, cols, group):
    _, slots, atoms = geo.shape
    width = group * atoms
    edges = slots * atoms
    rows = (HARM * TENSORS, LATENT, LATENT, TENSORS, TENSORS, LATENT)
    return pl.pallas_call(
        partial(middle_kernel, group=group),
        grid=(slots // group,),
        out_shape=[edge_shape(r, edges) for r in rows] + [edge_shape(HARM * TENSORS, atoms)],
        in_specs=[WHOLE] * 6
        + [edge_spec(r, width) for r in (LATENT, LATENT, TENSORS)]
        + [WHOLE] * 3,
        out_specs=[edge_spec(r, width) for r in rows] + [WHOLE],
        scratch_shapes=[pltpu.VMEM((2 * HARM * TENSORS, 4 * atoms), BF16)],
        compiler_params=params(),
        name="middle_pass",
    )(geo, nbrs, *blocks, x, lx, val, s_w, mix_w, cols)


def pull_mixed(geo, step, group, g, value, ds, chosen, dgeo, d_own, d_wide, dg, atoms):
    columns = []
    for q in range(group):
        k = step * group + q
        span = slice(q * atoms, (q + 1) * atoms)
        part = value[:, span]
        pulled = [ds[d * TENSORS : (d + 1) * TENSORS, span] for d in range(3)]
        scaled = [p * part for p in pulled]
        total = None
        for m in range(HARM):
            rows = slice(m * TENSORS, (m + 1) * TENSORS)
            d = DEGREE[m]
            source = g[rows, span]
            if m == 0:
                total = source * pulled[0]
                grad = scaled[0]
            else:
                harm = geo[m, pl.ds(k, 1), :]
                total = total + source * pulled[d] * harm
                dgeo[m, pl.ds(k, 1), :] += jnp.sum(source * scaled[d], axis=0, keepdims=True)
                grad = scaled[d] * harm
            d_own[rows, :] += grad
            high, low = halves(grad)
            dg[rows, span] = high
            dg[slice(HARM * TENSORS + m * TENSORS, HARM * TENSORS + (m + 1) * TENSORS), span] = low
        columns.append(total)
    both = dot_nt(dg[...], chosen)
    rows = HARM * TENSORS
    for number, out in enumerate(d_wide):
        span = slice(number * atoms, (number + 1) * atoms)
        out[...] += both[:rows, span] + both[rows:, span]
    return jnp.concatenate(columns, 1)


def last_kernel(
    geo, nbrs, own, below, above, across, x, lx, val, s_w, back_w, cols, base,
    energy, dx_out, dval_out, dgeo, d_own, d_below, d_above, d_across, split, g, dg, *, group,
):
    step = pl.program_id(0)
    atoms = own.shape[1]
    norm = 1.0 / math.sqrt(geo.shape[1])

    @pl.when(step == 0)
    def _():
        fill_split(own, below, above, across, split)
        energy[...] = base[...]
        dgeo[...] = jnp.zeros_like(dgeo)
        for out in (d_own, d_below, d_above, d_across):
            out[...] = jnp.zeros_like(out)

    chosen = chosen_columns(nbrs, step, group, split.shape[1])
    gathered(split, chosen, own, g, group)
    value = val[...]
    _, s = contracted(geo, step, group, g, value, atoms)
    update, slope = silu_pair(lx[...] + product(s_w[1], s))
    fresh = x[...] + update
    weight = cols[:, 2:3]
    read = jnp.sum(fresh * weight, axis=0, keepdims=True) * norm
    cuts = []
    for q in range(group):
        k = step * group + q
        span = slice(q * atoms, (q + 1) * atoms)
        cut = geo[0, pl.ds(k, 1), :]
        cuts.append(cut)
        energy[...] += read[:, span] * cut
        dgeo[0, pl.ds(k, 1), :] = read[:, span]
    d_fresh = weight * (jnp.concatenate(cuts, 1) * norm)
    pulled = product(back_w[1], d_fresh * slope)
    dx_out[...] = d_fresh + pulled[:LATENT]
    dval_out[...] = pull_mixed(
        geo, step, group, g, value, pulled[LATENT:], chosen, dgeo, d_own,
        (d_own, d_below, d_above, d_across), dg, atoms,
    )


def last_pass(geo, nbrs, blocks, x, lx, val, s_w, back_w, cols, base, group):
    _, slots, atoms = geo.shape
    width = group * atoms
    edges = slots * atoms
    rows = HARM * TENSORS
    return pl.pallas_call(
        partial(last_kernel, group=group),
        grid=(slots // group,),
        out_shape=[
            jax.ShapeDtypeStruct((1, atoms), F32),
            edge_shape(LATENT, edges),
            edge_shape(TENSORS, edges),
            jax.ShapeDtypeStruct((HARM, slots, atoms), F32),
        ]
        + [edge_shape(rows, atoms)] * 4,
        in_specs=[WHOLE] * 6
        + [edge_spec(r, width) for r in (LATENT, LATENT, TENSORS)]
        + [WHOLE] * 4,
        out_specs=[WHOLE, edge_spec(LATENT, width), edge_spec(TENSORS, width)] + [WHOLE] * 5,
        scratch_shapes=[
            pltpu.VMEM((2 * rows, 4 * atoms), BF16),
            pltpu.VMEM((rows, width), F32),
            pltpu.VMEM((2 * rows, width), BF16),
        ],
        compiler_params=params(),
        name="last_pass",
    )(geo, nbrs, *blocks, x, lx, val, s_w, back_w, cols, base)


def pull_env(geo, step, group, total, emb, dgeo, atoms, norm):
    columns = []
    for q in range(group):
        k = step * group + q
        span = slice(q * atoms, (q + 1) * atoms)
        part = emb[:, span]
        cut = geo[0, pl.ds(k, 1), :] * norm
        grad = None
        for m in range(HARM):
            source = total[m * TENSORS : (m + 1) * TENSORS, :]
            if m == 0:
                grad = source
            else:
                grad = grad + source * geo[m, pl.ds(k, 1), :]
                dgeo[m, pl.ds(k, 1), :] += cut * jnp.sum(source * part, axis=0, keepdims=True)
        dgeo[0, pl.ds(k, 1), :] += norm * jnp.sum(grad * part, axis=0, keepdims=True)
        columns.append(grad * cut)
    return jnp.concatenate(columns, 1)


def middle_back_kernel(
    geo, nbrs, own, low, high, dgeo_in, dx, dval, emb, g, slope, val, ev_w, back_w,
    dx_out, dval_out, dgeo, d_own, d_below, d_above, d_across, total, dg, *, group,
):
    step = pl.program_id(0)
    atoms = own.shape[1]
    norm = 1.0 / math.sqrt(geo.shape[1])

    @pl.when(step == 0)
    def _():
        total[...] = own[...] + low[...] + high[...]
        dgeo[...] = dgeo_in[...]
        for out in (d_own, d_below, d_above, d_across):
            out[...] = jnp.zeros_like(out)

    chosen = chosen_columns(nbrs, step, group, 4 * atoms)
    demb = pull_env(geo, step, group, total, emb, dgeo, atoms, norm)
    d_fresh = dx[...] + product(ev_w[1], jnp.concatenate([demb, dval[...]], 0))
    pulled = product(back_w[0], d_fresh * slope[...])
    dx_out[...] = d_fresh + pulled[:LATENT]
    dval_out[...] = pull_mixed(
        geo, step, group, g, val[...], pulled[LATENT:], chosen, dgeo, d_own,
        (d_own, d_below, d_above, d_across), dg, atoms,
    )


def middle_back(geo, nbrs, grads, dgeo, dx, dval, emb, g, slope, val, ev_w, back_w, group):
    _, slots, atoms = geo.shape
    width = group * atoms
    edges = slots * atoms
    rows = HARM * TENSORS
    return pl.pallas_call(
        partial(middle_back_kernel, group=group),
        grid=(slots // group,),
        out_shape=[
            edge_shape(LATENT, edges),
            edge_shape(TENSORS, edges),
            jax.ShapeDtypeStruct((HARM, slots, atoms), F32),
        ]
        + [edge_shape(rows, atoms)] * 4,
        in_specs=[WHOLE] * 6
        + [edge_spec(r, width) for r in (LATENT, TENSORS, TENSORS, rows, LATENT, TENSORS)]
        + [WHOLE] * 2,
        out_specs=[edge_spec(LATENT, width), edge_spec(TENSORS, width)] + [WHOLE] * 5,
        scratch_shapes=[pltpu.VMEM((rows, atoms), F32), pltpu.VMEM((2 * rows, width), BF16)],
        compiler_params=params(),
        name="middle_back",
    )(geo, nbrs, *grads, dgeo, dx, dval, emb, g, slope, val, ev_w, back_w)


def first_back_kernel(
    geo, own, low, high, dgeo_in, dx, dval, emb, slope, ev_w, rad_w, dgeo, total, *, group
):
    step = pl.program_id(0)
    atoms = own.shape[1]
    norm = 1.0 / math.sqrt(geo.shape[1])

    @pl.when(step == 0)
    def _():
        total[...] = own[...] + low[...] + high[...]
        dgeo[0:HARM] = dgeo_in[...]

    demb = pull_env(geo, step, group, total, emb, dgeo, atoms, norm)
    d_fresh = dx[...] + product(ev_w[0], jnp.concatenate([demb, dval[...]], 0))
    radial = product(rad_w[...], d_fresh * slope[...])
    for q in range(group):
        k = step * group + q
        for n in range(BASIS):
            dgeo[HARM + n, pl.ds(k, 1), :] = radial[n : n + 1, q * atoms : (q + 1) * atoms]


def first_back(geo, grads, dgeo, dx, dval, emb, slope, ev_w, rad_w, group):
    _, slots, atoms = geo.shape
    width = group * atoms
    return pl.pallas_call(
        partial(first_back_kernel, group=group),
        grid=(slots // group,),
        out_shape=jax.ShapeDtypeStruct((HARM + BASIS, slots, atoms), F32),
        in_specs=[WHOLE] * 5
        + [edge_spec(r, width) for r in (LATENT, TENSORS, TENSORS, LATENT)]
        + [WHOLE] * 2,
        out_specs=WHOLE,
        scratch_shapes=[pltpu.VMEM((HARM * TENSORS, atoms), F32)],
        compiler_params=params(),
        name="first_back",
    )(geo, *grads, dgeo, dx, dval, emb, slope, ev_w, rad_w)


def geometry_back_kernel(vec, dgeo, nbrs, own_out, below_out, above_out, across_out, dvec):
    _, slots, atoms = vec.shape
    for group in range(slots // 8):
        for tile in range(atoms // 128):
            up = slice(group * 8, group * 8 + 8)
            span = slice(tile * 128, tile * 128 + 128)
            vx, vy, vz = (vec[axis, up, span] for axis in range(3))
            inverse, cut, slope, sine, cosine = distances(vx, vy, vz)
            ux, uy, uz = vx * inverse, vy * inverse, vz * inverse
            _, h1, h2, h3, h4, h5, h6, h7, h8 = (dgeo[m, up, span] for m in range(HARM))
            dux = h1 + ROOT3 * (uy * h4 + uz * h7 + ux * h8)
            duy = h2 + ROOT3 * (ux * h4 + uz * h5 - uy * h8)
            duz = h3 + ROOT3 * (uy * h5 + ux * h7) + 3.0 * uz * h6
            along = ux * dux + uy * duy + uz * duz
            scale = math.sqrt(2.0 / CUTOFF) * inverse
            by_wave = jnp.zeros_like(sine)
            by_angle = jnp.zeros_like(sine)
            before, now = jnp.zeros_like(sine), sine
            before_c, now_c = jnp.ones_like(sine), cosine
            for n in range(BASIS):
                pulled = dgeo[HARM + n, up, span]
                by_wave = by_wave + pulled * now
                by_angle = by_angle + (n + 1.0) * (pulled * now_c)
                before, now = now, 2.0 * cosine * now - before
                before_c, now_c = now_c, 2.0 * cosine * now_c - before_c
            d_dist = slope * dgeo[0, up, span] + scale * (
                (math.pi / CUTOFF) * by_angle * cut + by_wave * (slope - inverse * cut)
            )
            dvec[0, up, span] = (dux - ux * along) * inverse + ux * d_dist
            dvec[1, up, span] = (duy - uy * along) * inverse + uy * d_dist
            dvec[2, up, span] = (duz - uz * along) * inverse + uz * d_dist
    blocks = 4 * atoms // 128
    total = jnp.zeros((2 * 48, 128), F32)
    for k in range(slots):
        index = nbrs[k : k + 1, :]
        block = lax.shift_right_arithmetic(index, 7)
        rows = lax.broadcasted_iota(jnp.int32, (16, atoms), 0)
        here = rows == block
        spread = jnp.concatenate(
            [jnp.where(here, dvec[axis, k : k + 1, :], 0.0) for axis in range(3)], 0
        )
        lane = lax.broadcasted_iota(jnp.int32, (128, atoms), 0)
        chosen = (lane == (index & 127)).astype(F32).astype(BF16)
        total = total + dot_nt(stacked(spread), chosen)
    total = total[:48] + total[48:]
    outs = (own_out, below_out, above_out, across_out)
    for out in outs:
        out[...] = jnp.zeros_like(out)
    per = atoms // 128
    for axis in range(3):
        for block in range(blocks):
            row = axis * 16 + block
            span = slice(block % per * 128, block % per * 128 + 128)
            outs[block // per][axis : axis + 1, span] = total[row : row + 1]
        own_out[axis : axis + 1, :] -= jnp.sum(dvec[axis], axis=0, keepdims=True)


def geometry_back(vec, dgeo, nbrs):
    _, slots, atoms = vec.shape
    return pl.pallas_call(
        geometry_back_kernel,
        out_shape=[jax.ShapeDtypeStruct((8, atoms), F32)] * 4,
        in_specs=[WHOLE] * 3,
        out_specs=[WHOLE] * 4,
        scratch_shapes=[pltpu.VMEM((3, slots, atoms), F32)],
        compiler_params=params(),
        name="geometry_back",
    )(vec, dgeo, nbrs)


def swap_y(rows, face):
    if lax.axis_size("gy") == 2:
        return passed_along(rows, "gy", 1)
    up = passed_along(rows[:, :face], "gy", 1)
    down = passed_along(rows[:, face:], "gy", -1)
    return jnp.concatenate([up, down], 1)


def return_y(rows, face):
    if lax.axis_size("gy") == 2:
        return passed_along(rows, "gy", 1)
    up = passed_along(rows[:, :face], "gy", -1)
    down = passed_along(rows[:, face:], "gy", 1)
    return jnp.concatenate([up, down], 1)


def ghost_env(env, wanted, face):
    below = passed_along(env, "gx", 1)
    above = passed_along(env, "gx", -1)
    across = swap_y(lend_env(env, below, above, wanted), face)
    return env, below, above, across


def owned_grads(own, below, above, across, wanted, face):
    returned = return_y(across, face)
    own, below, above = take_back(returned, wanted, own, below, above)
    return own, passed_along(below, "gx", -1), passed_along(above, "gx", 1)


def per_device(
    positions,
    species,
    neighbours,
    send_x,
    send_y,
    two_weight,
    two_bias,
    env_weight,
    value_weight,
    latent_weight,
    latent_bias,
    out_weight,
    species_shift,
):
    group = 4
    nbrs = neighbours[0, 0]
    atoms = nbrs.shape[1]
    face = send_y.shape[3]
    rows = jnp.concatenate(
        [
            positions[0, 0],
            species[0, 0][None].astype(F32),
            send_x[0, 0].astype(F32),
            jnp.zeros((2, atoms), F32),
        ],
        0,
    )
    wanted = jnp.concatenate(
        [
            send_y[0, 0, 1],
            send_y[0, 0, 0],
            jnp.full((atoms - 2 * face,), -1, jnp.int32),
        ]
    )[None]
    below = passed_along(rows, "gx", 1)
    above = passed_along(rows, "gx", -1)
    two_w, mix_w, s_w, back_w, ev_w, rad_w, cols = prepare_weights(
        two_weight, two_bias, env_weight, value_weight, latent_weight, latent_bias, out_weight
    )
    lent, wanted = lend_rows(rows, below, above, wanted)
    across = swap_y(lent, face)
    vec, geo, nbrs, base = geometry(rows, below, above, across, nbrs, species_shift, face)
    x0, slope_a, emb0, val0, lx0, env0 = first_pass(geo, rows, two_w, mix_w, cols, group)
    blocks = ghost_env(env0, wanted, face)
    g0, slope0, x1, emb1, val1, lx1, env1 = middle_pass(
        geo, nbrs, blocks, x0, lx0, val0, s_w, mix_w, cols, group
    )
    blocks = ghost_env(env1, wanted, face)
    energy, dx, dval, dgeo, *grads = last_pass(
        geo, nbrs, blocks, x1, lx1, val1, s_w, back_w, cols, base, group
    )
    total = lax.psum(jnp.sum(energy), ("gx", "gy"))
    mean_energy = total / (atoms * lax.axis_size("gx") * lax.axis_size("gy"))
    grads = owned_grads(*grads, wanted, face)
    dx, dval, dgeo, *grads = middle_back(
        geo, nbrs, grads, dgeo, dx, dval, emb1, g0, slope0, val0, ev_w, back_w, group
    )
    grads = owned_grads(*grads, wanted, face)
    dgeo = first_back(geo, grads, dgeo, dx, dval, emb0, slope_a, ev_w, rad_w, group)
    grads = owned_grads(*geometry_back(vec, dgeo, nbrs), wanted, face)
    forces = -(grads[0] + grads[1] + grads[2])[:3]
    return (energy[None], forces[None, None], mean_energy.reshape(1))


def solution(mesh):
    placed = (
        P(("groups", "gx"), "gy", None, None),
        P(("groups", "gx"), "gy", None),
        P(("groups", "gx"), "gy", None, None),
        P(("groups", "gx"), "gy", None, None),
        P(("groups", "gx"), "gy", None, None),
        P(),
        P(),
        P(),
        P(),
        P(),
        P(),
        P(),
        P(),
    )
    return jax.shard_map(
        per_device,
        mesh=mesh,
        in_specs=placed,
        out_specs=(
            P(("groups", "gx"), "gy", None),
            P(("groups", "gx"), "gy", None, None),
            P("groups"),
        ),
        check_vma=False,
    )
```

```python
from functools import partial
import math

import jax
import jax.numpy as jnp
from jax import lax
from jax.experimental import pallas as pl
from jax.experimental.pallas import tpu as pltpu
from jax.sharding import PartitionSpec as P

BASIS = 8
SPECIES = 5
SITES_X = 2
SITES_Y = 16
CUTOFF = 2.5
LATENT = 128
TENSORS = 32
HARM = 9
ROOT3 = math.sqrt(3.0)
DEGREE = (0, 1, 1, 1, 2, 2, 2, 2, 2)
F32 = jnp.float32
BF16 = jnp.bfloat16
WHOLE = pl.BlockSpec(memory_space=pltpu.VMEM)
SCALARS = pl.BlockSpec(memory_space=pltpu.SMEM)


def params():
    return pltpu.CompilerParams(vmem_limit_bytes=60 << 20)


def passed_along(value, axis, by):
    count = lax.axis_size(axis)
    return lax.ppermute(value, axis, [(i, (i + by) % count) for i in range(count)])


def dot(a, b):
    return jnp.dot(a, b, preferred_element_type=F32)


def dot_nt(a, b):
    return lax.dot_general(a, b, (((1,), (1,)), ((), ())), preferred_element_type=F32)


def halves(value):
    high = value.astype(BF16)
    return high, (value - high.astype(F32)).astype(BF16)


def stacked(value):
    return jnp.concatenate(halves(value), 0)


def product(weights, value):
    rows = weights.shape[0] // 2
    both = dot(weights, stacked(value))
    return both[:rows] + both[rows:]


def rounded(value):
    high = value.astype(BF16).astype(F32)
    return high, value - high


def weights_kernel(two, bias, env, val, lat, lat_bias, out_w, *outs):
    two_out, mix_out, s_out, back_out, ev_out, rad_out, cols = outs

    def depth_stack(piece):
        high, low = rounded(piece)
        top = jnp.concatenate([high, high], 0)
        bottom = jnp.concatenate([low, jnp.zeros_like(low)], 0)
        return top.T, bottom.T

    def join(pieces):
        tops, bottoms = zip(*[depth_stack(p) for p in pieces])
        return jnp.concatenate(list(tops) + list(bottoms), 0).astype(BF16)

    def wide_stack(piece):
        high, low = rounded(piece)
        top = jnp.concatenate([high, high], 1)
        bottom = jnp.concatenate([low, jnp.zeros_like(low)], 1)
        return jnp.concatenate([top, bottom], 0).astype(BF16)

    width = two.shape[1]
    first = jnp.concatenate(
        [
            two[0:SPECIES, :],
            bias[...],
            jnp.zeros((2, width), F32),
            two[SPECIES : 2 * SPECIES, :],
            jnp.zeros((3, width), F32),
            two[2 * SPECIES :, :],
        ],
        0,
    )
    two_out[...] = join([first])
    rad_out[...] = wide_stack(two[2 * SPECIES :, :])
    for layer in range(env.shape[0]):
        latent = lat[layer]
        mix_out[layer] = join([env[layer], val[layer], latent[:width]])
        s_out[layer] = join([latent[width:]])
        back_out[layer] = wide_stack(latent)
        high = [rounded(env[layer].T), rounded(val[layer].T)]
        top = jnp.concatenate([high[0][0], high[1][0]] * 2, 0).T
        bottom = jnp.concatenate([high[0][1], high[1][1]] + [jnp.zeros_like(high[0][1])] * 2, 0).T
        ev_out[layer] = jnp.concatenate([top, bottom], 0).astype(BF16)
    columns = jnp.concatenate(
        [lat_bias[...], out_w[...], jnp.zeros((8 - lat_bias.shape[0] - 1, width), F32)], 0
    )
    cols[...] = columns.T


def prepare_weights(two, bias, env, val, lat, lat_bias, out_w):
    layers = env.shape[0]
    shapes = [
        (2 * LATENT, 48),
        (layers, 2 * (LATENT + 2 * TENSORS), 2 * LATENT),
        (layers, 2 * LATENT, 6 * TENSORS),
        (layers, 2 * (LATENT + 3 * TENSORS), 2 * LATENT),
        (layers, 2 * LATENT, 4 * TENSORS),
        (2 * BASIS, 2 * LATENT),
    ]
    out_shape = [jax.ShapeDtypeStruct(s, BF16) for s in shapes]
    out_shape.append(jax.ShapeDtypeStruct((LATENT, 8), F32))
    return pl.pallas_call(
        weights_kernel,
        out_shape=out_shape,
        in_specs=[WHOLE] * 7,
        out_specs=[WHOLE] * 7,
        compiler_params=params(),
        name="prepare_weights",
    )(two, bias[None], env, val, lat, lat_bias, out_w[None])


def shifted(rows, by_x, by_y):
    lane_row = lax.broadcasted_iota(jnp.int32, rows.shape, 0)
    return rows + jnp.where(lane_row == 0, by_x, jnp.where(lane_row == 1, by_y, 0.0))


def lane_pick(table, row, index, blocks):
    low = index & 127
    high = lax.shift_right_arithmetic(index, 7)
    found = jnp.zeros(index.shape, F32)
    for block in range(blocks):
        span = slice(block * 128, block * 128 + 128)
        source = table[...][:, span] if row is None else table[row : row + 1, span]
        source = jnp.broadcast_to(source, index.shape)
        taken = jnp.take_along_axis(source, low, axis=1)
        found = jnp.where(high == block, taken, found)
    return found


def fill_wide(own, below, above, table, remap):
    atoms = own.shape[1]
    table[:, 0:atoms] = own[...]
    table[:, atoms : 2 * atoms] = shifted(below[...], -float(SITES_X), 0.0)
    table[:, 2 * atoms : 3 * atoms] = shifted(above[...], float(SITES_X), 0.0)
    lanes = lax.broadcasted_iota(jnp.int32, (1, atoms), 1).astype(F32)
    remap[:, 0:atoms] = lanes
    remap[:, atoms : 2 * atoms] = below[5:6, :] + float(atoms)
    remap[:, 2 * atoms : 3 * atoms] = above[4:5, :] + float(2 * atoms)


def lend_kernel(own, below, above, wanted, rows_out, wanted_out, table, remap):
    atoms = own.shape[1]
    blocks = 3 * atoms // 128
    fill_wide(own, below, above, table, remap)
    for tile in range(wanted.shape[1] // 128):
        span = slice(tile * 128, tile * 128 + 128)
        index = jnp.broadcast_to(wanted[:, span], (8, 128))
        place = lane_pick(remap, 0, index, blocks).astype(jnp.int32)
        place = jnp.where(index < 0, -1, place)
        wanted_out[:, span] = place[0:1]
        rows_out[:, span] = lane_pick(table, None, place, blocks)


def lend_rows(own, below, above, wanted):
    atoms = own.shape[1]
    return pl.pallas_call(
        lend_kernel,
        out_shape=[
            jax.ShapeDtypeStruct(wanted.shape[:0] + (8, wanted.shape[1]), F32),
            jax.ShapeDtypeStruct(wanted.shape, jnp.int32),
        ],
        in_specs=[WHOLE] * 4,
        out_specs=[WHOLE] * 2,
        scratch_shapes=[pltpu.VMEM((8, 3 * atoms), F32), pltpu.VMEM((1, 3 * atoms), F32)],
        compiler_params=params(),
        name="lend_rows",
    )(own, below, above, wanted)


def distances(vx, vy, vz):
    dist = jnp.sqrt(vx * vx + vy * vy + vz * vz)
    inverse = 1.0 / dist
    scaled = jnp.minimum(dist * (1.0 / CUTOFF), 1.0)
    second = scaled * scaled
    fourth = second * second
    sixth = fourth * second
    cut = 1.0 - 28.0 * sixth + 48.0 * (sixth * scaled) - 21.0 * (sixth * second)
    rest = 1.0 - scaled
    slope = (-168.0 / CUTOFF) * (fourth * scaled) * (rest * rest)
    angle = scaled * math.pi
    return inverse, cut, slope, jnp.sin(angle), jnp.cos(angle)


def geometry_kernel(
    own, below, above, across, nbrs, shift, vec_out, geo_out, nbr_out, base_out, table, remap, face
):
    atoms = own.shape[1]
    slots = nbrs.shape[0]
    blocks = table.shape[1] // 128
    fill_wide(own, below, above, table, remap)
    lanes = lax.broadcasted_iota(jnp.int32, (8, atoms), 1)
    rows = lax.broadcasted_iota(jnp.int32, (8, atoms), 0)
    moved = across[...] + jnp.where(
        rows == 1, jnp.where(lanes < face, -float(SITES_Y), float(SITES_Y)), 0.0
    )
    empty = jnp.where(rows == 2, -1000.0, jnp.where(rows == 3, -1.0, 0.0))
    table[:, 3 * atoms : 4 * atoms] = jnp.where(lanes < 2 * face, moved, empty)
    remap[:, 3 * atoms : 4 * atoms] = (
        lax.broadcasted_iota(jnp.int32, (1, atoms), 1) + 3 * atoms
    ).astype(F32)
    base = jnp.zeros((1, atoms), F32)
    for kind in range(SPECIES):
        base = base + jnp.where(own[3:4, :] == float(kind), shift[kind], 0.0)
    base_out[...] = base
    for group in range(slots // 8):
        for tile in range(atoms // 128):
            up = slice(group * 8, group * 8 + 8)
            span = slice(tile * 128, tile * 128 + 128)
            index = nbrs[up, span]
            index = lane_pick(remap, 0, index, blocks).astype(jnp.int32)
            nbr_out[up, span] = index
            vx = lane_pick(table, 0, index, blocks) - own[0:1, span]
            vy = lane_pick(table, 1, index, blocks) - own[1:2, span]
            vz = lane_pick(table, 2, index, blocks) - own[2:3, span]
            kind = lane_pick(table, 3, index, blocks)
            vec_out[0, up, span] = vx
            vec_out[1, up, span] = vy
            vec_out[2, up, span] = vz
            inverse, cut, _, sine, cosine = distances(vx, vy, vz)
            ux, uy, uz = vx * inverse, vy * inverse, vz * inverse
            harm = [
                ux,
                uy,
                uz,
                ROOT3 * ux * uy,
                ROOT3 * uy * uz,
                0.5 * (3.0 * uz * uz - 1.0),
                ROOT3 * ux * uz,
                0.5 * ROOT3 * (ux * ux - uy * uy),
            ]
            geo_out[0, up, span] = cut
            for number, value in enumerate(harm):
                geo_out[1 + number, up, span] = value
            scale = math.sqrt(2.0 / CUTOFF) * inverse * cut
            before, now = jnp.zeros_like(sine), sine
            for number in range(BASIS):
                geo_out[9 + number, up, span] = now * scale
                before, now = now, 2.0 * cosine * now - before
            geo_out[17, up, span] = kind


def geometry(own, below, above, across, nbrs, shift, face):
    slots, atoms = nbrs.shape
    return pl.pallas_call(
        partial(geometry_kernel, face=face),
        out_shape=[
            jax.ShapeDtypeStruct((3, slots, atoms), F32),
            jax.ShapeDtypeStruct((18, slots, atoms), F32),
            jax.ShapeDtypeStruct((slots, atoms), jnp.int32),
            jax.ShapeDtypeStruct((1, atoms), F32),
        ],
        in_specs=[WHOLE] * 5 + [SCALARS],
        out_specs=[WHOLE] * 4,
        scratch_shapes=[pltpu.VMEM((8, 4 * atoms), F32), pltpu.VMEM((1, 4 * atoms), F32)],
        compiler_params=params(),
        name="geometry",
    )(own, below, above, across, nbrs, shift)


def silu_pair(pre):
    gate = 1.0 / (1.0 + jnp.exp(-pre))
    value = pre * gate
    return value, gate + value * (1.0 - gate)


def first_kernel(
    geo, own, two_w, mix_w, cols, x_out, slope_out, emb_out, val_out, lx_out, env_out, *, group
):
    step = pl.program_id(0)
    atoms = own.shape[1]
    norm = 1.0 / math.sqrt(geo.shape[1])
    kinds = lax.broadcasted_iota(jnp.int32, (8, atoms), 0)
    kinds_f = kinds.astype(F32)
    centre = jnp.where((own[3:4, :] == kinds_f) & (kinds < SPECIES), 1.0, 0.0)
    centre = jnp.where(kinds == SPECIES, 1.0, centre)
    parts = []
    for q in range(group):
        k = step * group + q
        other = jnp.where(geo[17, pl.ds(k, 1), :] == kinds_f, 1.0, 0.0)
        radial = [geo[9 + n, pl.ds(k, 1), :] for n in range(BASIS)]
        parts.append(jnp.concatenate([centre, other] + radial, 0))
    features = jnp.concatenate(parts, 1)
    x, slope = silu_pair(product(two_w[...], features))
    x_out[...] = x
    slope_out[...] = slope
    mixed = product(mix_w[0], x)
    emb_out[...] = mixed[:TENSORS]
    val_out[...] = mixed[TENSORS : 2 * TENSORS]
    lx_out[...] = mixed[2 * TENSORS :] + cols[:, 0:1]

    @pl.when(step == 0)
    def _():
        env_out[...] = jnp.zeros_like(env_out)

    add_env(geo, step, group, mixed, env_out, atoms, norm)


def add_env(geo, step, group, embed, env_out, atoms, norm):
    for m in range(HARM):
        total = env_out[m * TENSORS : (m + 1) * TENSORS, :]
        for q in range(group):
            k = step * group + q
            cut = geo[0, pl.ds(k, 1), :] * norm
            factor = cut if m == 0 else cut * geo[m, pl.ds(k, 1), :]
            total = total + embed[:TENSORS, q * atoms : (q + 1) * atoms] * factor
        env_out[m * TENSORS : (m + 1) * TENSORS, :] = total


def edge_spec(rows, width):
    return pl.BlockSpec((rows, width), lambda i: (0, i))


def edge_shape(rows, edges):
    return jax.ShapeDtypeStruct((rows, edges), F32)


def first_pass(geo, own, two_w, mix_w, cols, group):
    _, slots, atoms = geo.shape
    width = group * atoms
    edges = slots * atoms
    rows = (LATENT, LATENT, TENSORS, TENSORS, LATENT)
    return pl.pallas_call(
        partial(first_kernel, group=group),
        grid=(slots // group,),
        out_shape=[edge_shape(r, edges) for r in rows] + [edge_shape(HARM * TENSORS, atoms)],
        in_specs=[WHOLE] * 5,
        out_specs=[edge_spec(r, width) for r in rows] + [WHOLE],
        compiler_params=params(),
        name="first_pass",
    )(geo, own, two_w, mix_w, cols)


def lend_env_kernel(own, below, above, wanted, out):
    atoms = own.shape[1]
    total = jnp.zeros(out.shape, F32)
    for number, block in enumerate((own, below, above)):
        rows = lax.broadcasted_iota(jnp.int32, (atoms, wanted.shape[1]), 0) + number * atoms
        chosen = (rows == wanted[...]).astype(F32).astype(BF16)
        both = dot(stacked(block[...]), chosen)
        total = total + both[: out.shape[0]] + both[out.shape[0] :]
    out[...] = total


def lend_env(own, below, above, wanted):
    return pl.pallas_call(
        lend_env_kernel,
        out_shape=jax.ShapeDtypeStruct(own.shape, F32),
        in_specs=[WHOLE] * 4,
        out_specs=WHOLE,
        compiler_params=params(),
        name="lend_env",
    )(own, below, above, wanted)


def take_back_kernel(returned, wanted, below, above, own, own_out, below_out, above_out):
    atoms = own.shape[1]
    rows_total = returned.shape[0]
    value = stacked(returned[...])
    for number, (block, out) in enumerate(((own, own_out), (below, below_out), (above, above_out))):
        rows = lax.broadcasted_iota(jnp.int32, (atoms, wanted.shape[1]), 0) + number * atoms
        chosen = (rows == wanted[...]).astype(F32).astype(BF16)
        both = dot_nt(value, chosen)
        out[...] = block[...] + both[:rows_total] + both[rows_total:]


def take_back(returned, wanted, own, below, above):
    return pl.pallas_call(
        take_back_kernel,
        out_shape=[jax.ShapeDtypeStruct(own.shape, F32)] * 3,
        in_specs=[WHOLE] * 5,
        out_specs=[WHOLE] * 3,
        compiler_params=params(),
        name="take_back",
    )(returned, wanted, below, above, own)


def chosen_columns(nbrs, step, group, start, columns):
    parts = []
    for q in range(group):
        index = nbrs[pl.ds(step * group + q, 1), :] - start
        rows = lax.broadcasted_iota(jnp.int32, (columns, index.shape[1]), 0)
        parts.append((rows == index).astype(F32).astype(BF16))
    return jnp.concatenate(parts, 1)


def fill_split(blocks, split):
    rows, atoms = blocks[0].shape
    for number, block in enumerate(blocks):
        span = slice(number * atoms, (number + 1) * atoms)
        high, low = halves(block[...])
        split[:rows, span] = high
        split[rows:, span] = low


def gather_kernel(nbrs, block, before, out, split, *, group, place):
    step = pl.program_id(0)
    rows, atoms = block.shape

    @pl.when(step == 0)
    def _():
        fill_split((block,), split)

    both = dot(split[...], chosen_columns(nbrs, step, group, place * atoms, atoms))
    for q in range(group):
        span = slice(q * atoms, (q + 1) * atoms)
        added = before[...] if place == 0 else before[:, span]
        out[:, span] = both[:rows, span] + both[rows:, span] + added


def gather_block(nbrs, block, before, place, group):
    slots, atoms = nbrs.shape
    rows = block.shape[0]
    width = group * atoms
    return pl.pallas_call(
        partial(gather_kernel, group=group, place=place),
        grid=(slots // group,),
        out_shape=edge_shape(rows, slots * atoms),
        in_specs=[WHOLE, WHOLE, WHOLE if place == 0 else edge_spec(rows, width)],
        out_specs=edge_spec(rows, width),
        scratch_shapes=[pltpu.VMEM((2 * rows, atoms), BF16)],
        compiler_params=params(),
        cost_estimate=effort(4 * rows * atoms * slots * atoms),
        name="gather_block",
    )(nbrs, block, before)


def effort(flops):
    return pl.CostEstimate(flops=flops, transcendentals=0, bytes_accessed=flops // 512)


def add_rest(split, chosen, before, g):
    rows = g.shape[0]
    both = dot(split[...], chosen)
    g[...] = both[:rows] + both[rows:] + before[...]


def contracted(geo, step, group, g, value, atoms):
    columns = []
    for q in range(group):
        k = step * group + q
        span = slice(q * atoms, (q + 1) * atoms)
        sums = [g[0:TENSORS, span], None, None]
        for m in range(1, HARM):
            term = g[m * TENSORS : (m + 1) * TENSORS, span] * geo[m, pl.ds(k, 1), :]
            d = DEGREE[m]
            sums[d] = term if sums[d] is None else sums[d] + term
        columns.append(jnp.concatenate(sums, 0))
    sums = jnp.concatenate(columns, 1)
    return sums, sums * jnp.concatenate([value] * 3, 0)


def middle_kernel(
    geo, nbrs, above, across, before, x, lx, val, s_w, mix_w, cols,
    g, slope_out, x_out, emb_out, val_out, lx_out, env_out, split, *, group,
):
    step = pl.program_id(0)
    atoms = above.shape[1]
    norm = 1.0 / math.sqrt(geo.shape[1])

    @pl.when(step == 0)
    def _():
        fill_split((above, across), split)
        env_out[...] = jnp.zeros_like(env_out)

    add_rest(split, chosen_columns(nbrs, step, group, 2 * atoms, 2 * atoms), before, g)
    _, s = contracted(geo, step, group, g, val[...], atoms)
    update, slope = silu_pair(lx[...] + product(s_w[0], s))
    slope_out[...] = slope
    fresh = x[...] + update
    x_out[...] = fresh
    mixed = product(mix_w[1], fresh)
    emb_out[...] = mixed[:TENSORS]
    val_out[...] = mixed[TENSORS : 2 * TENSORS]
    lx_out[...] = mixed[2 * TENSORS :] + cols[:, 1:2]
    add_env(geo, step, group, mixed, env_out, atoms, norm)


def middle_pass(geo, nbrs, blocks, x, lx, val, s_w, mix_w, cols, group):
    _, slots, atoms = geo.shape
    width = group * atoms
    edges = slots * atoms
    rows = (HARM * TENSORS, LATENT, LATENT, TENSORS, TENSORS, LATENT)
    return pl.pallas_call(
        partial(middle_kernel, group=group),
        grid=(slots // group,),
        out_shape=[edge_shape(r, edges) for r in rows] + [edge_shape(HARM * TENSORS, atoms)],
        in_specs=[WHOLE] * 4
        + [edge_spec(r, width) for r in (HARM * TENSORS, LATENT, LATENT, TENSORS)]
        + [WHOLE] * 3,
        out_specs=[edge_spec(r, width) for r in rows] + [WHOLE],
        scratch_shapes=[pltpu.VMEM((2 * HARM * TENSORS, 2 * atoms), BF16)],
        compiler_params=params(),
        cost_estimate=effort(8 * HARM * TENSORS * atoms * edges),
        name="middle_pass",
    )(geo, nbrs, *blocks, x, lx, val, s_w, mix_w, cols)


def pull_mixed(geo, step, group, g, value, ds, dgeo, d_own, dg, atoms):
    columns = []
    for q in range(group):
        k = step * group + q
        span = slice(q * atoms, (q + 1) * atoms)
        part = value[:, span]
        pulled = [ds[d * TENSORS : (d + 1) * TENSORS, span] for d in range(3)]
        scaled = [p * part for p in pulled]
        total = None
        for m in range(HARM):
            rows = slice(m * TENSORS, (m + 1) * TENSORS)
            d = DEGREE[m]
            source = g[rows, span]
            if m == 0:
                total = source * pulled[0]
                grad = scaled[0]
            else:
                harm = geo[m, pl.ds(k, 1), :]
                total = total + source * pulled[d] * harm
                dgeo[m, pl.ds(k, 1), :] += jnp.sum(source * scaled[d], axis=0, keepdims=True)
                grad = scaled[d] * harm
            d_own[rows, :] += grad
            high, low = halves(grad)
            dg[rows, span] = high
            dg[slice(HARM * TENSORS + m * TENSORS, HARM * TENSORS + (m + 1) * TENSORS), span] = low
        columns.append(total)
    return jnp.concatenate(columns, 1)


def last_kernel(
    geo, nbrs, above, across, before, x, lx, val, s_w, back_w, cols, base,
    energy, dx_out, dval_out, dgeo, d_own, dg, split, g, *, group,
):
    step = pl.program_id(0)
    atoms = above.shape[1]
    norm = 1.0 / math.sqrt(geo.shape[1])

    @pl.when(step == 0)
    def _():
        fill_split((above, across), split)
        energy[...] = base[...]
        dgeo[...] = jnp.zeros_like(dgeo)
        d_own[...] = jnp.zeros_like(d_own)

    add_rest(split, chosen_columns(nbrs, step, group, 2 * atoms, 2 * atoms), before, g)
    value = val[...]
    _, s = contracted(geo, step, group, g, value, atoms)
    update, slope = silu_pair(lx[...] + product(s_w[1], s))
    fresh = x[...] + update
    weight = cols[:, 2:3]
    read = jnp.sum(fresh * weight, axis=0, keepdims=True) * norm
    cuts = []
    for q in range(group):
        k = step * group + q
        span = slice(q * atoms, (q + 1) * atoms)
        cut = geo[0, pl.ds(k, 1), :]
        cuts.append(cut)
        energy[...] += read[:, span] * cut
        dgeo[0, pl.ds(k, 1), :] = read[:, span]
    d_fresh = weight * (jnp.concatenate(cuts, 1) * norm)
    pulled = product(back_w[1], d_fresh * slope)
    dx_out[...] = d_fresh + pulled[:LATENT]
    dval_out[...] = pull_mixed(
        geo, step, group, g, value, pulled[LATENT:], dgeo, d_own, dg, atoms
    )


def last_pass(geo, nbrs, blocks, x, lx, val, s_w, back_w, cols, base, group):
    _, slots, atoms = geo.shape
    width = group * atoms
    edges = slots * atoms
    rows = HARM * TENSORS
    return pl.pallas_call(
        partial(last_kernel, group=group),
        grid=(slots // group,),
        out_shape=[
            jax.ShapeDtypeStruct((1, atoms), F32),
            edge_shape(LATENT, edges),
            edge_shape(TENSORS, edges),
            jax.ShapeDtypeStruct((HARM, slots, atoms), F32),
            edge_shape(rows, atoms),
            jax.ShapeDtypeStruct((2 * rows, edges), BF16),
        ],
        in_specs=[WHOLE] * 4
        + [edge_spec(r, width) for r in (rows, LATENT, LATENT, TENSORS)]
        + [WHOLE] * 4,
        out_specs=[WHOLE, edge_spec(LATENT, width), edge_spec(TENSORS, width), WHOLE, WHOLE]
        + [edge_spec(2 * rows, width)],
        scratch_shapes=[
            pltpu.VMEM((2 * rows, 2 * atoms), BF16),
            pltpu.VMEM((rows, width), F32),
        ],
        compiler_params=params(),
        cost_estimate=effort(8 * rows * atoms * edges),
        name="last_pass",
    )(geo, nbrs, *blocks, x, lx, val, s_w, back_w, cols, base)


def pull_env(geo, step, group, total, emb, dgeo, atoms, norm):
    columns = []
    for q in range(group):
        k = step * group + q
        span = slice(q * atoms, (q + 1) * atoms)
        part = emb[:, span]
        cut = geo[0, pl.ds(k, 1), :] * norm
        grad = None
        for m in range(HARM):
            source = total[m * TENSORS : (m + 1) * TENSORS, :]
            if m == 0:
                grad = source
            else:
                grad = grad + source * geo[m, pl.ds(k, 1), :]
                dgeo[m, pl.ds(k, 1), :] += cut * jnp.sum(source * part, axis=0, keepdims=True)
        dgeo[0, pl.ds(k, 1), :] += norm * jnp.sum(grad * part, axis=0, keepdims=True)
        columns.append(grad * cut)
    return jnp.concatenate(columns, 1)


def middle_back_kernel(
    geo, own, low, high, dgeo_in, dx, dval, emb, g, slope, val, ev_w, back_w,
    dx_out, dval_out, dgeo, d_own, dg, total, *, group,
):
    step = pl.program_id(0)
    atoms = own.shape[1]
    norm = 1.0 / math.sqrt(geo.shape[1])

    @pl.when(step == 0)
    def _():
        total[...] = own[...] + low[...] + high[...]
        dgeo[...] = dgeo_in[...]
        d_own[...] = jnp.zeros_like(d_own)

    demb = pull_env(geo, step, group, total, emb, dgeo, atoms, norm)
    d_fresh = dx[...] + product(ev_w[1], jnp.concatenate([demb, dval[...]], 0))
    pulled = product(back_w[0], d_fresh * slope[...])
    dx_out[...] = d_fresh + pulled[:LATENT]
    dval_out[...] = pull_mixed(
        geo, step, group, g, val[...], pulled[LATENT:], dgeo, d_own, dg, atoms
    )


def middle_back(geo, grads, dgeo, dx, dval, emb, g, slope, val, ev_w, back_w, group):
    _, slots, atoms = geo.shape
    width = group * atoms
    edges = slots * atoms
    rows = HARM * TENSORS
    return pl.pallas_call(
        partial(middle_back_kernel, group=group),
        grid=(slots // group,),
        out_shape=[
            edge_shape(LATENT, edges),
            edge_shape(TENSORS, edges),
            jax.ShapeDtypeStruct((HARM, slots, atoms), F32),
            edge_shape(rows, atoms),
            jax.ShapeDtypeStruct((2 * rows, edges), BF16),
        ],
        in_specs=[WHOLE] * 5
        + [edge_spec(r, width) for r in (LATENT, TENSORS, TENSORS, rows, LATENT, TENSORS)]
        + [WHOLE] * 2,
        out_specs=[edge_spec(LATENT, width), edge_spec(TENSORS, width), WHOLE, WHOLE]
        + [edge_spec(2 * rows, width)],
        scratch_shapes=[pltpu.VMEM((rows, atoms), F32)],
        compiler_params=params(),
        cost_estimate=effort(2 * rows * atoms * edges),
        name="middle_back",
    )(geo, *grads, dgeo, dx, dval, emb, g, slope, val, ev_w, back_w)


def first_back_kernel(
    geo, own, low, high, dgeo_in, dx, dval, emb, slope, ev_w, rad_w, dgeo, total, *, group
):
    step = pl.program_id(0)
    atoms = own.shape[1]
    norm = 1.0 / math.sqrt(geo.shape[1])

    @pl.when(step == 0)
    def _():
        total[...] = own[...] + low[...] + high[...]
        dgeo[0:HARM] = dgeo_in[...]

    demb = pull_env(geo, step, group, total, emb, dgeo, atoms, norm)
    d_fresh = dx[...] + product(ev_w[0], jnp.concatenate([demb, dval[...]], 0))
    radial = product(rad_w[...], d_fresh * slope[...])
    for q in range(group):
        k = step * group + q
        for n in range(BASIS):
            dgeo[HARM + n, pl.ds(k, 1), :] = radial[n : n + 1, q * atoms : (q + 1) * atoms]


def first_back(geo, grads, dgeo, dx, dval, emb, slope, ev_w, rad_w, group):
    _, slots, atoms = geo.shape
    width = group * atoms
    return pl.pallas_call(
        partial(first_back_kernel, group=group),
        grid=(slots // group,),
        out_shape=jax.ShapeDtypeStruct((HARM + BASIS, slots, atoms), F32),
        in_specs=[WHOLE] * 5
        + [edge_spec(r, width) for r in (LATENT, TENSORS, TENSORS, LATENT)]
        + [WHOLE] * 2,
        out_specs=WHOLE,
        scratch_shapes=[pltpu.VMEM((HARM * TENSORS, atoms), F32)],
        compiler_params=params(),
        name="first_back",
    )(geo, *grads, dgeo, dx, dval, emb, slope, ev_w, rad_w)


def geometry_back_kernel(vec, dgeo, nbrs, own_out, below_out, above_out, across_out, dvec):
    _, slots, atoms = vec.shape
    for group in range(slots // 8):
        for tile in range(atoms // 128):
            up = slice(group * 8, group * 8 + 8)
            span = slice(tile * 128, tile * 128 + 128)
            vx, vy, vz = (vec[axis, up, span] for axis in range(3))
            inverse, cut, slope, sine, cosine = distances(vx, vy, vz)
            ux, uy, uz = vx * inverse, vy * inverse, vz * inverse
            _, h1, h2, h3, h4, h5, h6, h7, h8 = (dgeo[m, up, span] for m in range(HARM))
            dux = h1 + ROOT3 * (uy * h4 + uz * h7 + ux * h8)
            duy = h2 + ROOT3 * (ux * h4 + uz * h5 - uy * h8)
            duz = h3 + ROOT3 * (uy * h5 + ux * h7) + 3.0 * uz * h6
            along = ux * dux + uy * duy + uz * duz
            scale = math.sqrt(2.0 / CUTOFF) * inverse
            by_wave = jnp.zeros_like(sine)
            by_angle = jnp.zeros_like(sine)
            before, now = jnp.zeros_like(sine), sine
            before_c, now_c = jnp.ones_like(sine), cosine
            for n in range(BASIS):
                pulled = dgeo[HARM + n, up, span]
                by_wave = by_wave + pulled * now
                by_angle = by_angle + (n + 1.0) * (pulled * now_c)
                before, now = now, 2.0 * cosine * now - before
                before_c, now_c = now_c, 2.0 * cosine * now_c - before_c
            d_dist = slope * dgeo[0, up, span] + scale * (
                (math.pi / CUTOFF) * by_angle * cut + by_wave * (slope - inverse * cut)
            )
            dvec[0, up, span] = (dux - ux * along) * inverse + ux * d_dist
            dvec[1, up, span] = (duy - uy * along) * inverse + uy * d_dist
            dvec[2, up, span] = (duz - uz * along) * inverse + uz * d_dist
    blocks = 4 * atoms // 128
    total = jnp.zeros((2 * 48, 128), F32)
    for k in range(slots):
        index = nbrs[k : k + 1, :]
        block = lax.shift_right_arithmetic(index, 7)
        rows = lax.broadcasted_iota(jnp.int32, (16, atoms), 0)
        here = rows == block
        spread = jnp.concatenate(
            [jnp.where(here, dvec[axis, k : k + 1, :], 0.0) for axis in range(3)], 0
        )
        lane = lax.broadcasted_iota(jnp.int32, (128, atoms), 0)
        chosen = (lane == (index & 127)).astype(F32).astype(BF16)
        total = total + dot_nt(stacked(spread), chosen)
    total = total[:48] + total[48:]
    outs = (own_out, below_out, above_out, across_out)
    for out in outs:
        out[...] = jnp.zeros_like(out)
    per = atoms // 128
    for axis in range(3):
        for block in range(blocks):
            row = axis * 16 + block
            span = slice(block % per * 128, block % per * 128 + 128)
            outs[block // per][axis : axis + 1, span] = total[row : row + 1]
        own_out[axis : axis + 1, :] -= jnp.sum(dvec[axis], axis=0, keepdims=True)


def geometry_back(vec, dgeo, nbrs):
    _, slots, atoms = vec.shape
    return pl.pallas_call(
        geometry_back_kernel,
        out_shape=[jax.ShapeDtypeStruct((8, atoms), F32)] * 4,
        in_specs=[WHOLE] * 3,
        out_specs=[WHOLE] * 4,
        scratch_shapes=[pltpu.VMEM((3, slots, atoms), F32)],
        compiler_params=params(),
        name="geometry_back",
    )(vec, dgeo, nbrs)


def swap_y(rows, face):
    if lax.axis_size("gy") == 2:
        return passed_along(rows, "gy", 1)
    up = passed_along(rows[:, :face], "gy", 1)
    down = passed_along(rows[:, face:], "gy", -1)
    return jnp.concatenate([up, down], 1)


def return_y(rows, face):
    if lax.axis_size("gy") == 2:
        return passed_along(rows, "gy", 1)
    up = passed_along(rows[:, :face], "gy", -1)
    down = passed_along(rows[:, face:], "gy", 1)
    return jnp.concatenate([up, down], 1)


def picked(returned, wanted, place, atoms):
    rows = lax.broadcasted_iota(jnp.int32, (atoms, wanted.shape[1]), 0) + place * atoms
    chosen = (rows == wanted[...]).astype(F32).astype(BF16)
    both = dot_nt(stacked(returned[...]), chosen)
    half = both.shape[0] // 2
    return both[:half] + both[half:]


def scatter_kernel(nbrs, dg, *rest, group, place, returning):
    out = rest[-1]
    step = pl.program_id(0)
    rows, atoms = out.shape

    @pl.when(step == 0)
    def _():
        start = picked(rest[0], rest[1], place, atoms) if returning else jnp.zeros(out.shape, F32)
        out[...] = start + rest[2][...] if place == 0 else start

    both = dot_nt(dg[...], chosen_columns(nbrs, step, group, place * atoms, atoms))
    out[...] += both[:rows] + both[rows:]


def scatter_block(nbrs, dg, place, group, *rest):
    slots, atoms = nbrs.shape
    rows = dg.shape[0] // 2
    return pl.pallas_call(
        partial(scatter_kernel, group=group, place=place, returning=len(rest) > 1),
        grid=(slots // group,),
        out_shape=edge_shape(rows, atoms),
        in_specs=[WHOLE, edge_spec(2 * rows, group * atoms)] + [WHOLE] * len(rest),
        out_specs=WHOLE,
        compiler_params=params(),
        cost_estimate=effort(4 * rows * atoms * slots * atoms),
        name="scatter_block",
    )(nbrs, dg, *rest)


def add_picked_kernel(returned, wanted, block, out, *, place):
    out[...] = block[...] + picked(returned, wanted, place, block.shape[1])


def add_picked(returned, wanted, block, place):
    return pl.pallas_call(
        partial(add_picked_kernel, place=place),
        out_shape=jax.ShapeDtypeStruct(block.shape, F32),
        in_specs=[WHOLE] * 3,
        out_specs=WHOLE,
        compiler_params=params(),
        name="add_picked",
    )(returned, wanted, block)


def spread_env(env, nbrs, wanted, face, group):
    below = passed_along(env, "gx", 1)
    part = gather_block(nbrs, env, env, 0, group)
    env_up, below, part = lax.optimization_barrier((env, below, part))
    above = passed_along(env_up, "gx", -1)
    part = gather_block(nbrs, below, part, 1, group)
    below, part = lax.optimization_barrier((below, part))
    across = swap_y(lend_env(env, below, above, wanted), face)
    return above, across, part


def env_grads(d_own, dg, nbrs, wanted, face, group, total, steps):
    total = sum_step(total, steps)
    across = scatter_block(nbrs, dg, 3, group)
    returned = return_y(across, face)
    dg, across = lax.optimization_barrier((dg, across))
    below = scatter_block(nbrs, dg, 1, group)
    returned, below, total = lax.optimization_barrier((returned, below, total))
    total = sum_step(total, steps)
    below = add_picked(returned, wanted, below, 1)
    from_above = passed_along(below, "gx", -1)
    dg, below = lax.optimization_barrier((dg, below))
    above = scatter_block(nbrs, dg, 2, group, returned, wanted)
    dg, above, from_above, total = lax.optimization_barrier((dg, above, from_above, total))
    from_below = passed_along(above, "gx", 1)
    own = scatter_block(nbrs, dg, 0, group, returned, wanted, d_own)
    return (own, from_above, from_below), total


def owned_grads(own, below, above, across, wanted, face):
    returned = return_y(across, face)
    own, below, above = take_back(returned, wanted, own, below, above)
    return own, passed_along(below, "gx", -1), passed_along(above, "gx", 1)


def sum_steps():
    count = lax.axis_size("gx")
    if count & (count - 1) or lax.axis_size("gy") != 2:
        return None
    return [("gy", 1)] + [("gx", 1 << n) for n in range(count.bit_length() - 1)]


def sum_step(total, steps):
    if steps:
        axis, by = steps.pop(0)
        total = total + passed_along(total, axis, by)
    return total


def per_device(
    positions,
    species,
    neighbours,
    send_x,
    send_y,
    two_weight,
    two_bias,
    env_weight,
    value_weight,
    latent_weight,
    latent_bias,
    out_weight,
    species_shift,
):
    group = 4
    nbrs = neighbours[0, 0]
    atoms = nbrs.shape[1]
    face = send_y.shape[3]
    rows = jnp.concatenate(
        [
            positions[0, 0],
            species[0, 0][None].astype(F32),
            send_x[0, 0].astype(F32),
            jnp.zeros((2, atoms), F32),
        ],
        0,
    )
    wanted = jnp.concatenate(
        [
            send_y[0, 0, 1],
            send_y[0, 0, 0],
            jnp.full((atoms - 2 * face,), -1, jnp.int32),
        ]
    )[None]
    below = passed_along(rows, "gx", 1)
    above = passed_along(rows, "gx", -1)
    two_w, mix_w, s_w, back_w, ev_w, rad_w, cols = prepare_weights(
        two_weight, two_bias, env_weight, value_weight, latent_weight, latent_bias, out_weight
    )
    lent, wanted = lend_rows(rows, below, above, wanted)
    across = swap_y(lent, face)
    vec, geo, nbrs, base = geometry(rows, below, above, across, nbrs, species_shift, face)
    x0, slope_a, emb0, val0, lx0, env0 = first_pass(geo, rows, two_w, mix_w, cols, group)
    blocks = spread_env(env0, nbrs, wanted, face, group)
    g0, slope0, x1, emb1, val1, lx1, env1 = middle_pass(
        geo, nbrs, blocks, x0, lx0, val0, s_w, mix_w, cols, group
    )
    blocks = spread_env(env1, nbrs, wanted, face, group)
    energy, dx, dval, dgeo, d_own, dg = last_pass(
        geo, nbrs, blocks, x1, lx1, val1, s_w, back_w, cols, base, group
    )
    total = jnp.sum(energy)
    steps = sum_steps()
    if steps is None:
        total = lax.psum(total, ("gx", "gy"))
    total = jnp.full((8, 128), total, F32)
    grads, total = env_grads(d_own, dg, nbrs, wanted, face, group, total, steps)
    dx, dval, dgeo, d_own, dg = middle_back(
        geo, grads, dgeo, dx, dval, emb1, g0, slope0, val0, ev_w, back_w, group
    )
    grads, total = env_grads(d_own, dg, nbrs, wanted, face, group, total, steps)
    dgeo = first_back(geo, grads, dgeo, dx, dval, emb0, slope_a, ev_w, rad_w, group)
    while steps:
        total = sum_step(total, steps)
    mean_energy = total[0, 0] / (atoms * lax.axis_size("gx") * lax.axis_size("gy"))
    grads = owned_grads(*geometry_back(vec, dgeo, nbrs), wanted, face)
    forces = -(grads[0] + grads[1] + grads[2])[:3]
    return (energy[None], forces[None, None], mean_energy.reshape(1))


def solution(mesh):
    placed = (
        P(("groups", "gx"), "gy", None, None),
        P(("groups", "gx"), "gy", None),
        P(("groups", "gx"), "gy", None, None),
        P(("groups", "gx"), "gy", None, None),
        P(("groups", "gx"), "gy", None, None),
        P(),
        P(),
        P(),
        P(),
        P(),
        P(),
        P(),
        P(),
    )
    return jax.shard_map(
        per_device,
        mesh=mesh,
        in_specs=placed,
        out_specs=(
            P(("groups", "gx"), "gy", None),
            P(("groups", "gx"), "gy", None, None),
            P("groups"),
        ),
        check_vma=False,
    )
```

```python
from functools import partial
import math

import jax
import jax.numpy as jnp
from jax import lax
from jax.experimental import pallas as pl
from jax.experimental.pallas import tpu as pltpu
from jax.sharding import PartitionSpec as P

BASIS = 8
SPECIES = 5
SITES_X = 2
SITES_Y = 16
CUTOFF = 2.5
LATENT = 128
TENSORS = 32
HARM = 9
UNIT = 128
ROOT3 = math.sqrt(3.0)
DEGREE = (0, 1, 1, 1, 2, 2, 2, 2, 2)
F32 = jnp.float32
BF16 = jnp.bfloat16
WHOLE = pl.BlockSpec(memory_space=pltpu.VMEM)
SCALARS = pl.BlockSpec(memory_space=pltpu.SMEM)


def params():
    return pltpu.CompilerParams(vmem_limit_bytes=60 << 20)


def passed_along(value, axis, by):
    count = lax.axis_size(axis)
    return lax.ppermute(value, axis, [(i, (i + by) % count) for i in range(count)])


def dot(a, b):
    return jnp.dot(a, b, preferred_element_type=F32)


def dot_nt(a, b):
    return lax.dot_general(a, b, (((1,), (1,)), ((), ())), preferred_element_type=F32)


def halves(value):
    high = value.astype(BF16)
    return high, (value - high.astype(F32)).astype(BF16)


def stacked(value):
    return jnp.concatenate(halves(value), 0)


def product(weights, value):
    rows = weights.shape[0] // 2
    both = dot(weights, stacked(value))
    return both[:rows] + both[rows:]


def rounded(value):
    high = value.astype(BF16).astype(F32)
    return high, value - high


def weights_kernel(two, bias, env, val, lat, lat_bias, out_w, *outs):
    two_out, mix_out, s_out, back_out, ev_out, rad_out, cols = outs

    def depth_stack(piece):
        high, low = rounded(piece)
        top = jnp.concatenate([high, high], 0)
        bottom = jnp.concatenate([low, jnp.zeros_like(low)], 0)
        return top.T, bottom.T

    def join(pieces):
        tops, bottoms = zip(*[depth_stack(p) for p in pieces])
        return jnp.concatenate(list(tops) + list(bottoms), 0).astype(BF16)

    def wide_stack(piece):
        high, low = rounded(piece)
        top = jnp.concatenate([high, high], 1)
        bottom = jnp.concatenate([low, jnp.zeros_like(low)], 1)
        return jnp.concatenate([top, bottom], 0).astype(BF16)

    width = two.shape[1]
    first = jnp.concatenate(
        [
            two[0:SPECIES, :],
            bias[...],
            jnp.zeros((2, width), F32),
            two[SPECIES : 2 * SPECIES, :],
            jnp.zeros((3, width), F32),
            two[2 * SPECIES :, :],
        ],
        0,
    )
    two_out[...] = join([first])
    rad_out[...] = wide_stack(two[2 * SPECIES :, :])
    for layer in range(env.shape[0]):
        latent = lat[layer]
        mix_out[layer] = join([env[layer], val[layer], latent[:width]])
        s_out[layer] = join([latent[width:]])
        back_out[layer] = wide_stack(latent)
        high = [rounded(env[layer].T), rounded(val[layer].T)]
        top = jnp.concatenate([high[0][0], high[1][0]] * 2, 0).T
        bottom = jnp.concatenate([high[0][1], high[1][1]] + [jnp.zeros_like(high[0][1])] * 2, 0).T
        ev_out[layer] = jnp.concatenate([top, bottom], 0).astype(BF16)
    columns = jnp.concatenate(
        [lat_bias[...], out_w[...], jnp.zeros((8 - lat_bias.shape[0] - 1, width), F32)], 0
    )
    cols[...] = columns.T


def prepare_weights(two, bias, env, val, lat, lat_bias, out_w):
    layers = env.shape[0]
    shapes = [
        (2 * LATENT, 48),
        (layers, 2 * (LATENT + 2 * TENSORS), 2 * LATENT),
        (layers, 2 * LATENT, 6 * TENSORS),
        (layers, 2 * (LATENT + 3 * TENSORS), 2 * LATENT),
        (layers, 2 * LATENT, 4 * TENSORS),
        (2 * BASIS, 2 * LATENT),
    ]
    out_shape = [jax.ShapeDtypeStruct(s, BF16) for s in shapes]
    out_shape.append(jax.ShapeDtypeStruct((LATENT, 8), F32))
    return pl.pallas_call(
        weights_kernel,
        out_shape=out_shape,
        in_specs=[WHOLE] * 7,
        out_specs=[WHOLE] * 7,
        compiler_params=params(),
        name="prepare_weights",
    )(two, bias[None], env, val, lat, lat_bias, out_w[None])


def shifted(rows, by_x, by_y):
    lane_row = lax.broadcasted_iota(jnp.int32, rows.shape, 0)
    return rows + jnp.where(lane_row == 0, by_x, jnp.where(lane_row == 1, by_y, 0.0))


def lane_pick(table, row, index, blocks):
    low = index & 127
    high = lax.shift_right_arithmetic(index, 7)
    found = jnp.zeros(index.shape, F32)
    for block in range(blocks):
        span = slice(block * 128, block * 128 + 128)
        source = table[...][:, span] if row is None else table[row : row + 1, span]
        source = jnp.broadcast_to(source, index.shape)
        taken = jnp.take_along_axis(source, low, axis=1)
        found = jnp.where(high == block, taken, found)
    return found


def fill_wide(own, below, above, table, remap):
    atoms = own.shape[1]
    table[:, 0:atoms] = own[...]
    table[:, atoms : 2 * atoms] = shifted(below[...], -float(SITES_X), 0.0)
    table[:, 2 * atoms : 3 * atoms] = shifted(above[...], float(SITES_X), 0.0)
    lanes = lax.broadcasted_iota(jnp.int32, (1, atoms), 1).astype(F32)
    remap[:, 0:atoms] = lanes
    remap[:, atoms : 2 * atoms] = below[5:6, :] + float(atoms)
    remap[:, 2 * atoms : 3 * atoms] = above[4:5, :] + float(2 * atoms)


def lend_kernel(own, below, above, wanted, rows_out, wanted_out, table, remap):
    atoms = own.shape[1]
    blocks = 3 * atoms // 128
    fill_wide(own, below, above, table, remap)
    for tile in range(wanted.shape[1] // 128):
        span = slice(tile * 128, tile * 128 + 128)
        index = jnp.broadcast_to(wanted[:, span], (8, 128))
        place = lane_pick(remap, 0, index, blocks).astype(jnp.int32)
        place = jnp.where(index < 0, -1, place)
        wanted_out[:, span] = place[0:1]
        rows_out[:, span] = lane_pick(table, None, place, blocks)


def lend_rows(own, below, above, wanted):
    atoms = own.shape[1]
    return pl.pallas_call(
        lend_kernel,
        out_shape=[
            jax.ShapeDtypeStruct(wanted.shape[:0] + (8, wanted.shape[1]), F32),
            jax.ShapeDtypeStruct(wanted.shape, jnp.int32),
        ],
        in_specs=[WHOLE] * 4,
        out_specs=[WHOLE] * 2,
        scratch_shapes=[pltpu.VMEM((8, 3 * atoms), F32), pltpu.VMEM((1, 3 * atoms), F32)],
        compiler_params=params(),
        name="lend_rows",
    )(own, below, above, wanted)


def distances(vx, vy, vz):
    dist = jnp.sqrt(vx * vx + vy * vy + vz * vz)
    inverse = 1.0 / dist
    scaled = jnp.minimum(dist * (1.0 / CUTOFF), 1.0)
    second = scaled * scaled
    fourth = second * second
    sixth = fourth * second
    cut = 1.0 - 28.0 * sixth + 48.0 * (sixth * scaled) - 21.0 * (sixth * second)
    rest = 1.0 - scaled
    slope = (-168.0 / CUTOFF) * (fourth * scaled) * (rest * rest)
    angle = scaled * math.pi
    return inverse, cut, slope, jnp.sin(angle), jnp.cos(angle)


def geometry_kernel(
    own, below, above, across, nbrs, shift, vec_out, geo_out, nbr_out, base_out, table, remap, face
):
    atoms = own.shape[1]
    slots = nbrs.shape[0]
    blocks = table.shape[1] // 128
    fill_wide(own, below, above, table, remap)
    lanes = lax.broadcasted_iota(jnp.int32, (8, atoms), 1)
    rows = lax.broadcasted_iota(jnp.int32, (8, atoms), 0)
    moved = across[...] + jnp.where(
        rows == 1, jnp.where(lanes < face, -float(SITES_Y), float(SITES_Y)), 0.0
    )
    empty = jnp.where(rows == 2, -1000.0, jnp.where(rows == 3, -1.0, 0.0))
    table[:, 3 * atoms : 4 * atoms] = jnp.where(lanes < 2 * face, moved, empty)
    remap[:, 3 * atoms : 4 * atoms] = (
        lax.broadcasted_iota(jnp.int32, (1, atoms), 1) + 3 * atoms
    ).astype(F32)
    base = jnp.zeros((1, atoms), F32)
    for kind in range(SPECIES):
        base = base + jnp.where(own[3:4, :] == float(kind), shift[kind], 0.0)
    base_out[...] = base
    for group in range(slots // 8):
        for tile in range(atoms // UNIT):
            span = slice(tile * UNIT, tile * UNIT + UNIT)
            index = nbrs[group * 8 : group * 8 + 8, span]
            up = slice(tile * slots + group * 8, tile * slots + group * 8 + 8)
            index = lane_pick(remap, 0, index, blocks).astype(jnp.int32)
            nbr_out[up, :] = index
            vx = lane_pick(table, 0, index, blocks) - own[0:1, span]
            vy = lane_pick(table, 1, index, blocks) - own[1:2, span]
            vz = lane_pick(table, 2, index, blocks) - own[2:3, span]
            kind = lane_pick(table, 3, index, blocks)
            vec_out[0, up, :] = vx
            vec_out[1, up, :] = vy
            vec_out[2, up, :] = vz
            inverse, cut, _, sine, cosine = distances(vx, vy, vz)
            ux, uy, uz = vx * inverse, vy * inverse, vz * inverse
            harm = [
                ux,
                uy,
                uz,
                ROOT3 * ux * uy,
                ROOT3 * uy * uz,
                0.5 * (3.0 * uz * uz - 1.0),
                ROOT3 * ux * uz,
                0.5 * ROOT3 * (ux * ux - uy * uy),
            ]
            geo_out[0, up, :] = cut
            for number, value in enumerate(harm):
                geo_out[1 + number, up, :] = value
            scale = math.sqrt(2.0 / CUTOFF) * inverse * cut
            before, now = jnp.zeros_like(sine), sine
            for number in range(BASIS):
                geo_out[9 + number, up, :] = now * scale
                before, now = now, 2.0 * cosine * now - before
            geo_out[17, up, :] = kind


def geometry(own, below, above, across, nbrs, shift, face):
    slots, atoms = nbrs.shape
    return pl.pallas_call(
        partial(geometry_kernel, face=face),
        out_shape=[
            jax.ShapeDtypeStruct((3, slots * atoms // UNIT, UNIT), F32),
            jax.ShapeDtypeStruct((18, slots * atoms // UNIT, UNIT), F32),
            jax.ShapeDtypeStruct((slots * atoms // UNIT, UNIT), jnp.int32),
            jax.ShapeDtypeStruct((1, atoms), F32),
        ],
        in_specs=[WHOLE] * 5 + [SCALARS],
        out_specs=[WHOLE] * 4,
        scratch_shapes=[pltpu.VMEM((8, 4 * atoms), F32), pltpu.VMEM((1, 4 * atoms), F32)],
        compiler_params=params(),
        name="geometry",
    )(own, below, above, across, nbrs, shift)


def silu_pair(pre):
    gate = 1.0 / (1.0 + jnp.exp(-pre))
    value = pre * gate
    return value, gate + value * (1.0 - gate)


def row_spec(count, group, first):
    return pl.BlockSpec((count, group, UNIT), lambda i: (0, first + i, 0))


def index_spec(group, first):
    return pl.BlockSpec((group, UNIT), lambda i: (first + i, 0))


def edge_spec(rows, group, first):
    return pl.BlockSpec((rows, group * UNIT), lambda i: (0, first + i))


def unit_spec(rows, per):
    return pl.BlockSpec((rows, UNIT), lambda i: (0, i // per))


def edge_shape(rows, edges):
    return jax.ShapeDtypeStruct((rows, edges), F32)


def lanes_of(q):
    return slice(q * UNIT, (q + 1) * UNIT)


def rows_of(m):
    return slice(m * TENSORS, (m + 1) * TENSORS)


def add_env(geo, step, per, group, embed, env_out, norm):
    @pl.when(step % per == 0)
    def _():
        env_out[...] = jnp.zeros_like(env_out)

    cuts = [geo[0, q : q + 1, :] * norm for q in range(group)]
    for m in range(HARM):
        total = env_out[rows_of(m), :]
        for q in range(group):
            factor = cuts[q] if m == 0 else cuts[q] * geo[m, q : q + 1, :]
            total = total + embed[:TENSORS, lanes_of(q)] * factor
        env_out[rows_of(m), :] = total


def first_kernel(
    geo, own, two_w, mix_w, cols, x_out, slope_out, emb_out, val_out, lx_out, env_out,
    *, group, per, norm,
):
    step = pl.program_id(0)
    kinds = lax.broadcasted_iota(jnp.int32, (8, UNIT), 0)
    kinds_f = kinds.astype(F32)
    centre = jnp.where((own[3:4, :] == kinds_f) & (kinds < SPECIES), 1.0, 0.0)
    centre = jnp.where(kinds == SPECIES, 1.0, centre)
    parts = []
    for q in range(group):
        other = jnp.where(geo[17, q : q + 1, :] == kinds_f, 1.0, 0.0)
        radial = [geo[9 + n, q : q + 1, :] for n in range(BASIS)]
        parts.append(jnp.concatenate([centre, other] + radial, 0))
    features = jnp.concatenate(parts, 1)
    x, slope = silu_pair(product(two_w[...], features))
    x_out[...] = x
    slope_out[...] = slope
    mixed = product(mix_w[0], x)
    emb_out[...] = mixed[:TENSORS]
    val_out[...] = mixed[TENSORS : 2 * TENSORS]
    lx_out[...] = mixed[2 * TENSORS :] + cols[:, 0:1]
    add_env(geo, step, per, group, mixed, env_out, norm)


def first_pass(geo, own, two_w, mix_w, cols, slots, group):
    edges = geo.shape[1] * UNIT
    per = slots // group
    rows = (LATENT, LATENT, TENSORS, TENSORS, LATENT)
    return pl.pallas_call(
        partial(first_kernel, group=group, per=per, norm=1.0 / math.sqrt(slots)),
        grid=(geo.shape[1] // group,),
        out_shape=[edge_shape(r, edges) for r in rows]
        + [edge_shape(HARM * TENSORS, own.shape[1])],
        in_specs=[row_spec(18, group, 0), unit_spec(8, per)] + [WHOLE] * 3,
        out_specs=[edge_spec(r, group, 0) for r in rows] + [unit_spec(HARM * TENSORS, per)],
        compiler_params=params(),
        name="first_pass",
    )(geo, own, two_w, mix_w, cols)


def chosen_rows(index, columns, start):
    rows = lax.broadcasted_iota(jnp.int32, (columns, index.shape[1]), 0) + start
    return (rows == index).astype(F32).astype(BF16)


def chosen_columns(nbrs, group, columns):
    return jnp.concatenate(
        [chosen_rows(nbrs[q : q + 1, :], columns, 0) for q in range(group)], 1
    )


def lend_env_kernel(wanted, *refs):
    out = refs[-1]
    rows = out.shape[0]
    total = jnp.zeros((2 * rows, out.shape[1]), F32)
    start = 0
    for block in refs[:-1]:
        chosen = chosen_rows(wanted[...], block.shape[1], start)
        total = total + dot(stacked(block[...]), chosen)
        start += block.shape[1]
    out[...] = total[:rows] + total[rows:]


def lend_env(wanted, pieces):
    return pl.pallas_call(
        lend_env_kernel,
        out_shape=jax.ShapeDtypeStruct((HARM * TENSORS, wanted.shape[1]), F32),
        in_specs=[WHOLE] * (1 + len(pieces)),
        out_specs=WHOLE,
        compiler_params=params(),
        name="lend_env",
    )(wanted, *pieces)


def take_back_kernel(returned, wanted, centre, wide, *outs, widths):
    atoms = centre.shape[1]
    rows = returned.shape[0]
    value = stacked(returned[...])
    for place in range(3):
        chosen = chosen_rows(wanted[...], atoms, place * atoms)
        both = dot_nt(value, chosen)
        total = wide[:, place * atoms : (place + 1) * atoms] + both[:rows] + both[rows:]
        if place == 0:
            total = total + centre[...]
        start = 0
        for number, width in enumerate(widths):
            outs[place * len(widths) + number][...] = total[:, start : start + width]
            start += width


def take_back(returned, wanted, centre, wide, widths):
    outs = pl.pallas_call(
        partial(take_back_kernel, widths=widths),
        out_shape=[edge_shape(centre.shape[0], w) for w in widths] * 3,
        in_specs=[WHOLE] * 4,
        out_specs=[WHOLE] * (3 * len(widths)),
        compiler_params=params(),
        name="take_back",
    )(returned, wanted, centre, wide)
    count = len(widths)
    return [outs[place * count : (place + 1) * count] for place in range(3)]


def fill_split(pieces, split):
    rows = pieces[0].shape[0]
    start = 0
    for block in pieces:
        span = slice(start, start + block.shape[1])
        high, low = halves(block[...])
        split[:rows, span] = high
        split[rows:, span] = low
        start += block.shape[1]


def gathered(split, chosen, own, g, group):
    rows = HARM * TENSORS
    both = dot(split[...], chosen)
    for q in range(group):
        g[:, lanes_of(q)] = both[:rows, lanes_of(q)] + both[rows:, lanes_of(q)] + own[...]


def contracted(geo, group, g, value):
    columns = []
    for q in range(group):
        span = lanes_of(q)
        sums = [g[0:TENSORS, span], None, None]
        for m in range(1, HARM):
            term = g[rows_of(m), span] * geo[m, q : q + 1, :]
            d = DEGREE[m]
            sums[d] = term if sums[d] is None else sums[d] + term
        columns.append(jnp.concatenate([part * value[:, span] for part in sums], 0))
    return jnp.concatenate(columns, 1)


def middle_kernel(*refs, group, per, norm, count, aliased):
    geo, nbrs, own, x, lx, val, s_w, mix_w, cols = refs[:9]
    pieces = refs[9 : 9 + count]
    g, slope_out, x_out, emb_out, val_out, lx_out, env_out, split = refs[9 + count + aliased :]
    step = pl.program_id(0)

    @pl.when(step == 0)
    def _():
        fill_split(pieces, split)

    chosen = chosen_columns(nbrs, group, split.shape[1])
    gathered(split, chosen, own, g, group)
    s = contracted(geo, group, g, val[...])
    update, slope = silu_pair(lx[...] + product(s_w[0], s))
    slope_out[...] = slope
    fresh = x[...] + update
    x_out[...] = fresh
    mixed = product(mix_w[1], fresh)
    emb_out[...] = mixed[:TENSORS]
    val_out[...] = mixed[TENSORS : 2 * TENSORS]
    lx_out[...] = mixed[2 * TENSORS :] + cols[:, 1:2]
    add_env(geo, step, per, group, mixed, env_out, norm)


def middle_pass(geo, nbrs, own, pieces, x, lx, val, s_w, mix_w, cols, slots, group, span, before):
    edges = x.shape[1]
    per = slots // group
    first = span[0] * per
    rows = (HARM * TENSORS, LATENT, LATENT, TENSORS, TENSORS, LATENT)
    ins = 9 + len(pieces)
    return pl.pallas_call(
        partial(
            middle_kernel, group=group, per=per, norm=1.0 / math.sqrt(slots),
            count=len(pieces), aliased=len(before),
        ),
        grid=((span[1] - span[0]) * per,),
        out_shape=[edge_shape(r, edges) for r in rows]
        + [edge_shape(HARM * TENSORS, (span[1] - span[0]) * UNIT)],
        in_specs=[
            row_spec(18, group, first),
            index_spec(group, first),
            pl.BlockSpec((HARM * TENSORS, UNIT), lambda i: (0, span[0] + i // per)),
        ]
        + [edge_spec(r, group, first) for r in (LATENT, LATENT, TENSORS)]
        + [WHOLE] * (3 + len(pieces))
        + [pl.BlockSpec(memory_space=pl.ANY)] * len(before),
        out_specs=[edge_spec(r, group, first) for r in rows] + [unit_spec(HARM * TENSORS, per)],
        scratch_shapes=[
            pltpu.VMEM((2 * HARM * TENSORS, sum(p.shape[1] for p in pieces)), BF16)
        ],
        input_output_aliases={ins + n: n for n in range(len(before))},
        compiler_params=params(),
        cost_estimate=effort(8 * HARM * TENSORS * edges * edges // slots),
        name="middle_pass",
    )(geo, nbrs, own, x, lx, val, s_w, mix_w, cols, *pieces, *before)


def effort(flops):
    return pl.CostEstimate(flops=flops, transcendentals=0, bytes_accessed=flops // 512)


def pull_mixed(geo, group, g, value, ds, chosen, dgeo, centre, wide, dg):
    columns = []
    for q in range(group):
        span = lanes_of(q)
        part = value[:, span]
        pulled = [ds[rows_of(d), span] for d in range(3)]
        scaled = [p * part for p in pulled]
        total = None
        for m in range(HARM):
            d = DEGREE[m]
            source = g[rows_of(m), span]
            if m == 0:
                total = source * pulled[0]
                grad = scaled[0]
            else:
                harm = geo[m, q : q + 1, :]
                total = total + source * pulled[d] * harm
                dgeo[m, q : q + 1, :] += jnp.sum(source * scaled[d], axis=0, keepdims=True)
                grad = scaled[d] * harm
            centre[rows_of(m), :] += grad
            high, low = halves(grad)
            dg[rows_of(m), span] = high
            dg[rows_of(HARM + m), span] = low
        columns.append(total)
    both = dot_nt(dg[...], chosen)
    rows = HARM * TENSORS
    wide[...] += both[:rows] + both[rows:]
    return jnp.concatenate(columns, 1)


def last_kernel(*refs, group, per, norm, count):
    geo, nbrs, own, x, lx, val, s_w, back_w, cols, base = refs[:10]
    pieces = refs[10 : 10 + count]
    energy, dx_out, dval_out, dgeo, centre, wide, split, g, dg = refs[10 + count :]
    step = pl.program_id(0)

    @pl.when(step == 0)
    def _():
        fill_split(pieces, split)
        wide[...] = jnp.zeros_like(wide)

    @pl.when(step % per == 0)
    def _():
        energy[...] = base[...]
        centre[...] = jnp.zeros_like(centre)

    chosen = chosen_columns(nbrs, group, split.shape[1])
    gathered(split, chosen, own, g, group)
    value = val[...]
    s = contracted(geo, group, g, value)
    update, slope = silu_pair(lx[...] + product(s_w[1], s))
    fresh = x[...] + update
    weight = cols[:, 2:3]
    read = jnp.sum(fresh * weight, axis=0, keepdims=True) * norm
    cuts = []
    dgeo[...] = jnp.zeros_like(dgeo)
    for q in range(group):
        cut = geo[0, q : q + 1, :]
        cuts.append(cut)
        energy[...] += read[:, lanes_of(q)] * cut
        dgeo[0, q : q + 1, :] = read[:, lanes_of(q)]
    d_fresh = weight * (jnp.concatenate(cuts, 1) * norm)
    pulled = product(back_w[1], d_fresh * slope)
    dx_out[...] = d_fresh + pulled[:LATENT]
    dval_out[...] = pull_mixed(
        geo, group, g, value, pulled[LATENT:], chosen, dgeo, centre, wide, dg
    )


def last_pass(geo, nbrs, own, pieces, x, lx, val, s_w, back_w, cols, base, slots, group):
    edges = x.shape[1]
    per = slots // group
    rows = HARM * TENSORS
    columns = sum(p.shape[1] for p in pieces)
    return pl.pallas_call(
        partial(
            last_kernel, group=group, per=per, norm=1.0 / math.sqrt(slots), count=len(pieces)
        ),
        grid=(geo.shape[1] // group,),
        out_shape=[
            jax.ShapeDtypeStruct(base.shape, F32),
            edge_shape(LATENT, edges),
            edge_shape(TENSORS, edges),
            jax.ShapeDtypeStruct((HARM,) + geo.shape[1:], F32),
            edge_shape(rows, base.shape[1]),
            edge_shape(rows, columns),
        ],
        in_specs=[row_spec(18, group, 0), index_spec(group, 0), unit_spec(rows, per)]
        + [edge_spec(r, group, 0) for r in (LATENT, LATENT, TENSORS)]
        + [WHOLE] * 3
        + [unit_spec(1, per)]
        + [WHOLE] * len(pieces),
        out_specs=[
            unit_spec(1, per),
            edge_spec(LATENT, group, 0),
            edge_spec(TENSORS, group, 0),
            row_spec(HARM, group, 0),
            unit_spec(rows, per),
            WHOLE,
        ],
        scratch_shapes=[
            pltpu.VMEM((2 * rows, columns), BF16),
            pltpu.VMEM((rows, group * UNIT), F32),
            pltpu.VMEM((2 * rows, group * UNIT), BF16),
        ],
        compiler_params=params(),
        cost_estimate=effort(16 * rows * edges * edges // slots),
        name="last_pass",
    )(geo, nbrs, own, x, lx, val, s_w, back_w, cols, base, *pieces)


def pull_env(geo, group, total, emb, dgeo, norm):
    columns = []
    for q in range(group):
        part = emb[:, lanes_of(q)]
        cut = geo[0, q : q + 1, :] * norm
        grad = None
        for m in range(HARM):
            source = total[rows_of(m), :]
            if m == 0:
                grad = source
            else:
                grad = grad + source * geo[m, q : q + 1, :]
                dgeo[m, q : q + 1, :] += cut * jnp.sum(source * part, axis=0, keepdims=True)
        dgeo[0, q : q + 1, :] += norm * jnp.sum(grad * part, axis=0, keepdims=True)
        columns.append(grad * cut)
    return jnp.concatenate(columns, 1)


def middle_back_kernel(*refs, group, per, norm, aliased):
    geo, nbrs, own, low, high, dgeo_in, dx, dval, emb, g, slope, val, ev_w, back_w = refs[:14]
    wide_in = refs[14] if aliased else None
    dx_out, dval_out, dgeo, centre, wide, total, dg = refs[14 + aliased :]
    step = pl.program_id(0)

    @pl.when(step == 0)
    def _():
        wide[...] = wide_in[...] if aliased else jnp.zeros_like(wide)

    @pl.when(step % per == 0)
    def _():
        total[...] = own[...] + low[...] + high[...]
        centre[...] = jnp.zeros_like(centre)

    chosen = chosen_columns(nbrs, group, wide.shape[1])
    dgeo[...] = dgeo_in[...]
    demb = pull_env(geo, group, total, emb, dgeo, norm)
    d_fresh = dx[...] + product(ev_w[1], jnp.concatenate([demb, dval[...]], 0))
    pulled = product(back_w[0], d_fresh * slope[...])
    dx_out[...] = d_fresh + pulled[:LATENT]
    dval_out[...] = pull_mixed(
        geo, group, g, val[...], pulled[LATENT:], chosen, dgeo, centre, wide, dg
    )


def middle_back(
    geo, nbrs, grads, dgeo, dx, dval, emb, g, slope, val, ev_w, back_w, slots, group, span, before
):
    edges = dx.shape[1]
    per = slots // group
    first = span[0] * per
    rows = HARM * TENSORS
    atoms = geo.shape[1] // slots * UNIT
    columns = 4 * atoms
    aliased = len(before)
    shapes = [
        edge_shape(LATENT, edges),
        edge_shape(TENSORS, edges),
        jax.ShapeDtypeStruct((HARM,) + geo.shape[1:], F32),
        edge_shape(rows, atoms),
        edge_shape(rows, columns),
    ]
    extra = [before[4], *before[:4]] if before else []
    return pl.pallas_call(
        partial(
            middle_back_kernel, group=group, per=per, norm=1.0 / math.sqrt(slots), aliased=aliased
        ),
        grid=((span[1] - span[0]) * per,),
        out_shape=shapes,
        in_specs=[row_spec(18, group, first), index_spec(group, first)]
        + [unit_spec(rows, per)] * 3
        + [row_spec(HARM, group, first)]
        + [
            edge_spec(r, group, first)
            for r in (LATENT, TENSORS, TENSORS, rows, LATENT, TENSORS)
        ]
        + [WHOLE] * 2
        + ([WHOLE] + [pl.BlockSpec(memory_space=pl.ANY)] * 4 if before else []),
        out_specs=[
            edge_spec(LATENT, group, first),
            edge_spec(TENSORS, group, first),
            row_spec(HARM, group, first),
            pl.BlockSpec((rows, UNIT), lambda i: (0, span[0] + i // per)),
            WHOLE,
        ],
        scratch_shapes=[
            pltpu.VMEM((rows, UNIT), F32),
            pltpu.VMEM((2 * rows, group * UNIT), BF16),
        ],
        input_output_aliases={15 + n: n for n in range(4)} if before else {},
        compiler_params=params(),
        cost_estimate=effort(8 * rows * edges * edges // slots),
        name="middle_back",
    )(geo, nbrs, *grads, dgeo, dx, dval, emb, g, slope, val, ev_w, back_w, *extra)


def first_back_kernel(
    geo, own, low, high, dgeo_in, dx, dval, emb, slope, ev_w, rad_w, dgeo, total,
    *, group, per, norm,
):
    step = pl.program_id(0)

    @pl.when(step % per == 0)
    def _():
        total[...] = own[...] + low[...] + high[...]

    dgeo[0:HARM] = dgeo_in[...]
    demb = pull_env(geo, group, total, emb, dgeo, norm)
    d_fresh = dx[...] + product(ev_w[0], jnp.concatenate([demb, dval[...]], 0))
    radial = product(rad_w[...], d_fresh * slope[...])
    for q in range(group):
        for n in range(BASIS):
            dgeo[HARM + n, q : q + 1, :] = radial[n : n + 1, lanes_of(q)]


def first_back(geo, grads, dgeo, dx, dval, emb, slope, ev_w, rad_w, slots, group):
    per = slots // group
    rows = HARM * TENSORS
    return pl.pallas_call(
        partial(first_back_kernel, group=group, per=per, norm=1.0 / math.sqrt(slots)),
        grid=(geo.shape[1] // group,),
        out_shape=jax.ShapeDtypeStruct((HARM + BASIS,) + geo.shape[1:], F32),
        in_specs=[row_spec(18, group, 0)]
        + [unit_spec(rows, per)] * 3
        + [row_spec(HARM, group, 0)]
        + [edge_spec(r, group, 0) for r in (LATENT, TENSORS, TENSORS, LATENT)]
        + [WHOLE] * 2,
        out_specs=row_spec(HARM + BASIS, group, 0),
        scratch_shapes=[pltpu.VMEM((rows, UNIT), F32)],
        compiler_params=params(),
        name="first_back",
    )(geo, *grads, dgeo, dx, dval, emb, slope, ev_w, rad_w)


def geometry_back_kernel(vec, dgeo, nbrs, centre_out, wide_out, dvec, *, slots):
    rows_total = vec.shape[1]
    units = rows_total // slots
    for group in range(rows_total // 8):
        up = slice(group * 8, group * 8 + 8)
        vx, vy, vz = (vec[axis, up, :] for axis in range(3))
        inverse, cut, slope, sine, cosine = distances(vx, vy, vz)
        ux, uy, uz = vx * inverse, vy * inverse, vz * inverse
        _, h1, h2, h3, h4, h5, h6, h7, h8 = (dgeo[m, up, :] for m in range(HARM))
        dux = h1 + ROOT3 * (uy * h4 + uz * h7 + ux * h8)
        duy = h2 + ROOT3 * (ux * h4 + uz * h5 - uy * h8)
        duz = h3 + ROOT3 * (uy * h5 + ux * h7) + 3.0 * uz * h6
        along = ux * dux + uy * duy + uz * duz
        scale = math.sqrt(2.0 / CUTOFF) * inverse
        by_wave = jnp.zeros_like(sine)
        by_angle = jnp.zeros_like(sine)
        before, now = jnp.zeros_like(sine), sine
        before_c, now_c = jnp.ones_like(sine), cosine
        for n in range(BASIS):
            pulled = dgeo[HARM + n, up, :]
            by_wave = by_wave + pulled * now
            by_angle = by_angle + (n + 1.0) * (pulled * now_c)
            before, now = now, 2.0 * cosine * now - before
            before_c, now_c = now_c, 2.0 * cosine * now_c - before_c
        d_dist = slope * dgeo[0, up, :] + scale * (
            (math.pi / CUTOFF) * by_angle * cut + by_wave * (slope - inverse * cut)
        )
        dvec[0, up, :] = (dux - ux * along) * inverse + ux * d_dist
        dvec[1, up, :] = (duy - uy * along) * inverse + uy * d_dist
        dvec[2, up, :] = (duz - uz * along) * inverse + uz * d_dist
    total = jnp.zeros((2 * 48, UNIT), F32)
    rows = lax.broadcasted_iota(jnp.int32, (16, UNIT), 0)
    lane = lax.broadcasted_iota(jnp.int32, (UNIT, UNIT), 0)
    for group in range(rows_total // 4):
        spreads, picks = [], []
        for k in range(group * 4, group * 4 + 4):
            index = nbrs[k : k + 1, :]
            here = rows == lax.shift_right_arithmetic(index, 7)
            spreads.append(
                jnp.concatenate(
                    [jnp.where(here, dvec[axis, k : k + 1, :], 0.0) for axis in range(3)], 0
                )
            )
            picks.append((lane == (index & 127)).astype(F32).astype(BF16))
        spread = jnp.concatenate(spreads, 1)
        total = total + dot_nt(stacked(spread), jnp.concatenate(picks, 1))
    total = total[:48] + total[48:]
    wide_out[...] = jnp.zeros_like(wide_out)
    centre_out[...] = jnp.zeros_like(centre_out)
    for axis in range(3):
        for block in range(wide_out.shape[1] // UNIT):
            row = axis * 16 + block
            wide_out[axis : axis + 1, lanes_of(block)] = total[row : row + 1]
        for unit in range(units):
            part = dvec[axis, unit * slots : (unit + 1) * slots, :]
            centre_out[axis : axis + 1, lanes_of(unit)] = -jnp.sum(part, axis=0, keepdims=True)


def geometry_back(vec, dgeo, nbrs, slots):
    atoms = vec.shape[1] // slots * UNIT
    return pl.pallas_call(
        partial(geometry_back_kernel, slots=slots),
        out_shape=[edge_shape(8, atoms), edge_shape(8, 4 * atoms)],
        in_specs=[WHOLE] * 3,
        out_specs=[WHOLE] * 2,
        scratch_shapes=[pltpu.VMEM(vec.shape, F32)],
        compiler_params=params(),
        name="geometry_back",
    )(vec, dgeo, nbrs)


def swap_y(rows, face):
    if lax.axis_size("gy") == 2:
        return passed_along(rows, "gy", 1)
    up = passed_along(rows[:, :face], "gy", 1)
    down = passed_along(rows[:, face:], "gy", -1)
    return jnp.concatenate([up, down], 1)


def return_y(rows, face):
    if lax.axis_size("gy") == 2:
        return passed_along(rows, "gy", 1)
    up = passed_along(rows[:, :face], "gy", -1)
    down = passed_along(rows[:, face:], "gy", 1)
    return jnp.concatenate([up, down], 1)


def across_part(wide):
    return wide[:, wide.shape[1] // 4 * 3 :]


def ghost_rows(parts, wanted, face):
    below = [passed_along(part, "gx", 1) for part in parts]
    above = [passed_along(part, "gx", -1) for part in parts]
    pieces = [*parts, *below, *above]
    return pieces + [swap_y(lend_env(wanted, pieces), face)]


def owned_grads(centre, wide, wanted, face, widths):
    returned = return_y(across_part(wide), face)
    own, below, above = take_back(returned, wanted, centre, wide, widths)
    found = []
    for number in range(len(widths)):
        send = below[number], above[number]
        if found:
            send, found[-1] = lax.optimization_barrier((send, found[-1]))
        found.append(
            [own[number], passed_along(send[0], "gx", -1), passed_along(send[1], "gx", 1)]
        )
    return found


def sum_steps():
    count = lax.axis_size("gx")
    if count & (count - 1) or lax.axis_size("gy") != 2:
        return None
    return [("gy", 1)] + [("gx", 1 << n) for n in range(count.bit_length() - 1)]


def sum_step(total, steps):
    if steps:
        axis, by = steps.pop(0)
        total = total + passed_along(total, axis, by)
    return total


def per_device(
    positions,
    species,
    neighbours,
    send_x,
    send_y,
    two_weight,
    two_bias,
    env_weight,
    value_weight,
    latent_weight,
    latent_bias,
    out_weight,
    species_shift,
):
    group = 8
    nbrs = neighbours[0, 0]
    atoms = nbrs.shape[1]
    face = send_y.shape[3]
    rows = jnp.concatenate(
        [
            positions[0, 0],
            species[0, 0][None].astype(F32),
            send_x[0, 0].astype(F32),
            jnp.zeros((2, atoms), F32),
        ],
        0,
    )
    wanted = jnp.concatenate(
        [
            send_y[0, 0, 1],
            send_y[0, 0, 0],
            jnp.full((atoms - 2 * face,), -1, jnp.int32),
        ]
    )[None]
    below = passed_along(rows, "gx", 1)
    above = passed_along(rows, "gx", -1)
    two_w, mix_w, s_w, back_w, ev_w, rad_w, cols = prepare_weights(
        two_weight, two_bias, env_weight, value_weight, latent_weight, latent_bias, out_weight
    )
    lent, wanted = lend_rows(rows, below, above, wanted)
    across = swap_y(lent, face)
    slots = nbrs.shape[0]
    units = atoms // UNIT
    vec, geo, nbrs, base = geometry(rows, below, above, across, nbrs, species_shift, face)
    x0, slope_a, emb0, val0, lx0, env0 = first_pass(
        geo, rows, two_w, mix_w, cols, slots, group
    )
    pieces = ghost_rows([env0], wanted, face)
    parts, before = [], []
    for span in ((0, units - 1), (units - 1, units)):
        *before, part = middle_pass(
            geo, nbrs, env0, pieces, x0, lx0, val0, s_w, mix_w, cols, slots, group, span, before
        )
        parts.append(part)
    g0, slope0, x1, emb1, val1, lx1 = before
    pieces = ghost_rows(parts, wanted, face)
    env1 = jnp.concatenate(parts, 1)
    energy, dx, dval, dgeo, centre, wide = last_pass(
        geo, nbrs, env1, pieces, x1, lx1, val1, s_w, back_w, cols, base, slots, group
    )
    total = jnp.sum(energy)
    steps = sum_steps()
    if steps is None:
        total = lax.psum(total, ("gx", "gy"))
    total = sum_step(jnp.full((8, 128), total, F32), steps)
    widths = (UNIT, atoms - UNIT)
    grads = owned_grads(centre, wide, wanted, face, widths)
    before = []
    for number, span in enumerate(((0, 1), (1, units))):
        grads[number][0], total = lax.optimization_barrier((grads[number][0], total))
        total = sum_step(total, steps)
        before = middle_back(
            geo, nbrs, grads[number], dgeo, dx, dval, emb1, g0, slope0, val0, ev_w, back_w,
            slots, group, span, before,
        )
    dx, dval, dgeo, centre, wide = before
    (grads,) = owned_grads(centre, wide, wanted, face, (atoms,))
    grads[0], total = lax.optimization_barrier((grads[0], total))
    total = sum_step(total, steps)
    dgeo = first_back(geo, grads, dgeo, dx, dval, emb0, slope_a, ev_w, rad_w, slots, group)
    while steps:
        total = sum_step(total, steps)
    mean_energy = total[0, 0] / (atoms * lax.axis_size("gx") * lax.axis_size("gy"))
    (grads,) = owned_grads(*geometry_back(vec, dgeo, nbrs, slots), wanted, face, (atoms,))
    forces = -(grads[0] + grads[1] + grads[2])[:3]
    return (energy[None], forces[None, None], mean_energy.reshape(1))


def solution(mesh):
    placed = (
        P(("groups", "gx"), "gy", None, None),
        P(("groups", "gx"), "gy", None),
        P(("groups", "gx"), "gy", None, None),
        P(("groups", "gx"), "gy", None, None),
        P(("groups", "gx"), "gy", None, None),
        P(),
        P(),
        P(),
        P(),
        P(),
        P(),
        P(),
        P(),
    )
    return jax.shard_map(
        per_device,
        mesh=mesh,
        in_specs=placed,
        out_specs=(
            P(("groups", "gx"), "gy", None),
            P(("groups", "gx"), "gy", None, None),
            P("groups"),
        ),
        check_vma=False,
    )
```

```python
from functools import partial
import math

import jax
import jax.numpy as jnp
from jax import lax
from jax.experimental import pallas as pl
from jax.experimental.pallas import tpu as pltpu
from jax.sharding import PartitionSpec as P

BASIS = 8
SPECIES = 5
SITES_X = 2
SITES_Y = 16
CUTOFF = 2.5
LATENT = 128
TENSORS = 32
HARM = 9
UNIT = 128
ROOT3 = math.sqrt(3.0)
DEGREE = (0, 1, 1, 1, 2, 2, 2, 2, 2)
F32 = jnp.float32
BF16 = jnp.bfloat16
WHOLE = pl.BlockSpec(memory_space=pltpu.VMEM)
SCALARS = pl.BlockSpec(memory_space=pltpu.SMEM)


def params():
    return pltpu.CompilerParams(vmem_limit_bytes=60 << 20)


def passed_along(value, axis, by):
    count = lax.axis_size(axis)
    return lax.ppermute(value, axis, [(i, (i + by) % count) for i in range(count)])


def dot(a, b):
    return jnp.dot(a, b, preferred_element_type=F32)


def dot_nt(a, b):
    return lax.dot_general(a, b, (((1,), (1,)), ((), ())), preferred_element_type=F32)


def halves(value):
    high = value.astype(BF16)
    return high, (value - high.astype(F32)).astype(BF16)


def stacked(value):
    return jnp.concatenate(halves(value), 0)


def product(weights, value):
    rows = weights.shape[0] // 2
    both = dot(weights, stacked(value))
    return both[:rows] + both[rows:]


def rounded(value):
    high = value.astype(BF16).astype(F32)
    return high, value - high


def weights_kernel(two, bias, env, val, lat, lat_bias, out_w, *outs):
    two_out, mix_out, s_out, back_out, ev_out, rad_out, cols = outs

    def depth_stack(piece):
        high, low = rounded(piece)
        top = jnp.concatenate([high, high], 0)
        bottom = jnp.concatenate([low, jnp.zeros_like(low)], 0)
        return top.T, bottom.T

    def lane_stack(piece):
        high, low = rounded(piece)
        top = jnp.concatenate([high, high], 1)
        return top, jnp.concatenate([low, jnp.zeros_like(low)], 1)

    def join(pieces):
        tops, bottoms = zip(*pieces)
        return jnp.concatenate(list(tops) + list(bottoms), 0).astype(BF16)

    def wide_stack(piece):
        return jnp.concatenate(lane_stack(piece), 0).astype(BF16)

    width = two.shape[1]
    first = jnp.concatenate(
        [
            two[0:SPECIES, :],
            bias[...],
            jnp.zeros((2, width), F32),
            two[SPECIES : 2 * SPECIES, :],
            jnp.zeros((3, width), F32),
            two[2 * SPECIES :, :],
        ],
        0,
    )
    two_out[...] = join([depth_stack(first)])
    rad_out[...] = wide_stack(two[2 * SPECIES :, :])
    for layer in range(env.shape[0]):
        latent = lat[layer]
        mix_out[layer] = join(
            [lane_stack(env[layer]), lane_stack(val[layer]), depth_stack(latent[:width])]
        )
        s_out[layer] = join([depth_stack(latent[width:])])
        back_out[layer] = wide_stack(latent)
        high = [rounded(env[layer]), rounded(val[layer])]
        top = jnp.concatenate([high[0][0], high[1][0]] * 2, 0).T
        bottom = jnp.concatenate([high[0][1], high[1][1]] + [jnp.zeros_like(high[0][1])] * 2, 0).T
        ev_out[layer] = jnp.concatenate([top, bottom], 0).astype(BF16)
    columns = jnp.concatenate(
        [lat_bias[...], out_w[...], jnp.zeros((8 - lat_bias.shape[0] - 1, width), F32)], 0
    )
    cols[...] = columns.T


def prepare_weights(two, bias, env, val, lat, lat_bias, out_w):
    layers = env.shape[0]
    shapes = [
        (2 * LATENT, 48),
        (layers, 2 * (LATENT + 2 * TENSORS), 2 * LATENT),
        (layers, 2 * LATENT, 6 * TENSORS),
        (layers, 2 * (LATENT + 3 * TENSORS), 2 * LATENT),
        (layers, 2 * LATENT, 4 * TENSORS),
        (2 * BASIS, 2 * LATENT),
    ]
    out_shape = [jax.ShapeDtypeStruct(s, BF16) for s in shapes]
    out_shape.append(jax.ShapeDtypeStruct((LATENT, 8), F32))
    return pl.pallas_call(
        weights_kernel,
        out_shape=out_shape,
        in_specs=[WHOLE] * 7,
        out_specs=[WHOLE] * 7,
        compiler_params=params(),
        name="prepare_weights",
    )(two, bias[None], env.swapaxes(1, 2), val.swapaxes(1, 2), lat, lat_bias, out_w[None])


def shifted(rows, by_x, by_y):
    lane_row = lax.broadcasted_iota(jnp.int32, rows.shape, 0)
    return rows + jnp.where(lane_row == 0, by_x, jnp.where(lane_row == 1, by_y, 0.0))


def lane_pick(table, row, index, blocks):
    low = index & 127
    high = lax.shift_right_arithmetic(index, 7)
    found = jnp.zeros(index.shape, F32)
    for block in range(blocks):
        span = slice(block * 128, block * 128 + 128)
        source = table[...][:, span] if row is None else table[row : row + 1, span]
        source = jnp.broadcast_to(source, index.shape)
        taken = jnp.take_along_axis(source, low, axis=1)
        found = jnp.where(high == block, taken, found)
    return found


def fill_wide(own, below, above, table, remap):
    atoms = own.shape[1]
    table[:, 0:atoms] = own[...]
    table[:, atoms : 2 * atoms] = shifted(below[...], -float(SITES_X), 0.0)
    table[:, 2 * atoms : 3 * atoms] = shifted(above[...], float(SITES_X), 0.0)
    lanes = lax.broadcasted_iota(jnp.int32, (1, atoms), 1).astype(F32)
    remap[:, 0:atoms] = lanes
    remap[:, atoms : 2 * atoms] = below[5:6, :] + float(atoms)
    remap[:, 2 * atoms : 3 * atoms] = above[4:5, :] + float(2 * atoms)


def lend_kernel(own, below, above, wanted, rows_out, wanted_out, table, remap):
    atoms = own.shape[1]
    blocks = 3 * atoms // 128
    fill_wide(own, below, above, table, remap)
    for tile in range(wanted.shape[1] // 128):
        span = slice(tile * 128, tile * 128 + 128)
        index = jnp.broadcast_to(wanted[:, span], (8, 128))
        place = lane_pick(remap, 0, index, blocks).astype(jnp.int32)
        place = jnp.where(index < 0, -1, place)
        wanted_out[:, span] = place[0:1]
        rows_out[:, span] = lane_pick(table, None, place, blocks)


def lend_rows(own, below, above, wanted):
    atoms = own.shape[1]
    return pl.pallas_call(
        lend_kernel,
        out_shape=[
            jax.ShapeDtypeStruct(wanted.shape[:0] + (8, wanted.shape[1]), F32),
            jax.ShapeDtypeStruct(wanted.shape, jnp.int32),
        ],
        in_specs=[WHOLE] * 4,
        out_specs=[WHOLE] * 2,
        scratch_shapes=[pltpu.VMEM((8, 3 * atoms), F32), pltpu.VMEM((1, 3 * atoms), F32)],
        compiler_params=params(),
        name="lend_rows",
    )(own, below, above, wanted)


def distances(vx, vy, vz):
    dist = jnp.sqrt(vx * vx + vy * vy + vz * vz)
    inverse = 1.0 / dist
    scaled = jnp.minimum(dist * (1.0 / CUTOFF), 1.0)
    second = scaled * scaled
    fourth = second * second
    sixth = fourth * second
    cut = 1.0 - 28.0 * sixth + 48.0 * (sixth * scaled) - 21.0 * (sixth * second)
    rest = 1.0 - scaled
    slope = (-168.0 / CUTOFF) * (fourth * scaled) * (rest * rest)
    angle = scaled * math.pi
    return inverse, cut, slope, jnp.sin(angle), jnp.cos(angle)


def geometry_kernel(
    own, below, above, across, nbrs, shift, vec_out, geo_out, nbr_out, base_out, table, remap, face
):
    atoms = own.shape[1]
    slots = nbrs.shape[0]
    blocks = table.shape[1] // 128
    fill_wide(own, below, above, table, remap)
    lanes = lax.broadcasted_iota(jnp.int32, (8, atoms), 1)
    rows = lax.broadcasted_iota(jnp.int32, (8, atoms), 0)
    moved = across[...] + jnp.where(
        rows == 1, jnp.where(lanes < face, -float(SITES_Y), float(SITES_Y)), 0.0
    )
    empty = jnp.where(rows == 2, -1000.0, jnp.where(rows == 3, -1.0, 0.0))
    table[:, 3 * atoms : 4 * atoms] = jnp.where(lanes < 2 * face, moved, empty)
    remap[:, 3 * atoms : 4 * atoms] = (
        lax.broadcasted_iota(jnp.int32, (1, atoms), 1) + 3 * atoms
    ).astype(F32)
    base = jnp.zeros((1, atoms), F32)
    for kind in range(SPECIES):
        base = base + jnp.where(own[3:4, :] == float(kind), shift[kind], 0.0)
    base_out[...] = base
    for group in range(slots // 8):
        for tile in range(atoms // UNIT):
            span = slice(tile * UNIT, tile * UNIT + UNIT)
            index = nbrs[group * 8 : group * 8 + 8, span]
            up = slice(tile * slots + group * 8, tile * slots + group * 8 + 8)
            index = lane_pick(remap, 0, index, blocks).astype(jnp.int32)
            nbr_out[up, :] = index
            vx = lane_pick(table, 0, index, blocks) - own[0:1, span]
            vy = lane_pick(table, 1, index, blocks) - own[1:2, span]
            vz = lane_pick(table, 2, index, blocks) - own[2:3, span]
            kind = lane_pick(table, 3, index, blocks)
            vec_out[0, up, :] = vx
            vec_out[1, up, :] = vy
            vec_out[2, up, :] = vz
            inverse, cut, _, sine, cosine = distances(vx, vy, vz)
            ux, uy, uz = vx * inverse, vy * inverse, vz * inverse
            harm = [
                ux,
                uy,
                uz,
                ROOT3 * ux * uy,
                ROOT3 * uy * uz,
                0.5 * (3.0 * uz * uz - 1.0),
                ROOT3 * ux * uz,
                0.5 * ROOT3 * (ux * ux - uy * uy),
            ]
            geo_out[0, up, :] = cut
            for number, value in enumerate(harm):
                geo_out[1 + number, up, :] = value
            scale = math.sqrt(2.0 / CUTOFF) * inverse * cut
            before, now = jnp.zeros_like(sine), sine
            for number in range(BASIS):
                geo_out[9 + number, up, :] = now * scale
                before, now = now, 2.0 * cosine * now - before
            geo_out[17, up, :] = kind


def geometry(own, below, above, across, nbrs, shift, face):
    slots, atoms = nbrs.shape
    return pl.pallas_call(
        partial(geometry_kernel, face=face),
        out_shape=[
            jax.ShapeDtypeStruct((3, slots * atoms // UNIT, UNIT), F32),
            jax.ShapeDtypeStruct((18, slots * atoms // UNIT, UNIT), F32),
            jax.ShapeDtypeStruct((slots * atoms // UNIT, UNIT), jnp.int32),
            jax.ShapeDtypeStruct((1, atoms), F32),
        ],
        in_specs=[WHOLE] * 5 + [SCALARS],
        out_specs=[WHOLE] * 4,
        scratch_shapes=[pltpu.VMEM((8, 4 * atoms), F32), pltpu.VMEM((1, 4 * atoms), F32)],
        compiler_params=params(),
        name="geometry",
    )(own, below, above, across, nbrs, shift)


def silu_pair(pre):
    gate = 1.0 / (1.0 + jnp.exp(-pre))
    value = pre * gate
    return value, gate + value * (1.0 - gate)


def row_spec(count, group, first):
    return pl.BlockSpec((count, group, UNIT), lambda i: (0, first + i, 0))


def index_spec(group, first):
    return pl.BlockSpec((group, UNIT), lambda i: (first + i, 0))


def edge_spec(rows, group, first):
    return pl.BlockSpec((rows, group * UNIT), lambda i: (0, first + i))


def unit_spec(rows, per):
    return pl.BlockSpec((rows, UNIT), lambda i: (0, i // per))


def edge_shape(rows, edges):
    return jax.ShapeDtypeStruct((rows, edges), F32)


def lanes_of(q):
    return slice(q * UNIT, (q + 1) * UNIT)


def rows_of(m):
    return slice(m * TENSORS, (m + 1) * TENSORS)


def add_env(geo, step, per, group, embed, env_out, norm):
    @pl.when(step % per == 0)
    def _():
        env_out[...] = jnp.zeros_like(env_out)

    cuts = [geo[0, q : q + 1, :] * norm for q in range(group)]
    for m in range(HARM):
        total = env_out[rows_of(m), :]
        for q in range(group):
            factor = cuts[q] if m == 0 else cuts[q] * geo[m, q : q + 1, :]
            total = total + embed[:TENSORS, lanes_of(q)] * factor
        env_out[rows_of(m), :] = total


def first_kernel(
    geo, own, two_w, mix_w, cols, *outs, group, per, norm
):
    x_out, slope_out, emb_out, val_out, lx_out, env_all, env_out = outs[-7:]
    step = pl.program_id(0)
    kinds = lax.broadcasted_iota(jnp.int32, (8, UNIT), 0)
    kinds_f = kinds.astype(F32)
    centre = jnp.where((own[3:4, :] == kinds_f) & (kinds < SPECIES), 1.0, 0.0)
    centre = jnp.where(kinds == SPECIES, 1.0, centre)
    parts = []
    for q in range(group):
        other = jnp.where(geo[17, q : q + 1, :] == kinds_f, 1.0, 0.0)
        radial = [geo[9 + n, q : q + 1, :] for n in range(BASIS)]
        parts.append(jnp.concatenate([centre, other] + radial, 0))
    features = jnp.concatenate(parts, 1)
    x, slope = silu_pair(product(two_w[...], features))
    x_out[...] = x
    slope_out[...] = slope
    mixed = product(mix_w[0], x)
    emb_out[...] = mixed[:TENSORS]
    val_out[...] = mixed[TENSORS : 2 * TENSORS]
    lx_out[...] = mixed[2 * TENSORS :] + cols[:, 0:1]
    add_env(geo, step, per, group, mixed, env_out, norm)
    env_all[...] = env_out[...]


def wide_unit_spec(rows, per, first):
    return pl.BlockSpec((rows, UNIT), lambda i: (0, first + i // per))


def first_pass(geo, own, two_w, mix_w, cols, slots, group, span, before):
    edges = geo.shape[1] * UNIT
    per = slots // group
    first = span[0] * per
    rows = (LATENT, LATENT, TENSORS, TENSORS, LATENT)
    return pl.pallas_call(
        partial(first_kernel, group=group, per=per, norm=1.0 / math.sqrt(slots)),
        grid=((span[1] - span[0]) * per,),
        out_shape=[edge_shape(r, edges) for r in rows]
        + [edge_shape(HARM * TENSORS, w) for w in (own.shape[1], (span[1] - span[0]) * UNIT)],
        in_specs=[row_spec(18, group, first), wide_unit_spec(8, per, span[0])]
        + [WHOLE] * 3
        + [pl.BlockSpec(memory_space=pl.ANY)] * len(before),
        out_specs=[edge_spec(r, group, first) for r in rows]
        + [wide_unit_spec(HARM * TENSORS, per, span[0]), unit_spec(HARM * TENSORS, per)],
        input_output_aliases={5 + n: n for n in range(len(before))},
        compiler_params=params(),
        cost_estimate=effort(64 * LATENT * LATENT * edges),
        name="first_pass",
    )(geo, own, two_w, mix_w, cols, *before)


def chosen_rows(index, columns, start):
    rows = lax.broadcasted_iota(jnp.int32, (columns, index.shape[1]), 0) + start
    return (rows == index).astype(F32).astype(BF16)


def chosen_columns(nbrs, group, columns):
    return jnp.concatenate(
        [chosen_rows(nbrs[q : q + 1, :], columns, 0) for q in range(group)], 1
    )


def lend_env_kernel(wanted, *refs):
    out = refs[-1]
    rows = out.shape[0]
    total = jnp.zeros((2 * rows, out.shape[1]), F32)
    start = 0
    for block in refs[:-1]:
        chosen = chosen_rows(wanted[...], block.shape[1], start)
        total = total + dot(stacked(block[...]), chosen)
        start += block.shape[1]
    out[...] = total[:rows] + total[rows:]


def lend_env(wanted, pieces):
    return pl.pallas_call(
        lend_env_kernel,
        out_shape=jax.ShapeDtypeStruct((HARM * TENSORS, wanted.shape[1]), F32),
        in_specs=[WHOLE] * (1 + len(pieces)),
        out_specs=WHOLE,
        compiler_params=params(),
        name="lend_env",
    )(wanted, *pieces)


def take_back_kernel(returned, wanted, centre, wide, *outs, widths):
    atoms = centre.shape[1]
    rows = returned.shape[0]
    value = stacked(returned[...])
    for place in range(3):
        chosen = chosen_rows(wanted[...], atoms, place * atoms)
        both = dot_nt(value, chosen)
        total = wide[:, place * atoms : (place + 1) * atoms] + both[:rows] + both[rows:]
        if place == 0:
            total = total + centre[...]
        start = 0
        for number, width in enumerate(widths):
            outs[place * len(widths) + number][...] = total[:, start : start + width]
            start += width


def take_back(returned, wanted, centre, wide, widths):
    outs = pl.pallas_call(
        partial(take_back_kernel, widths=widths),
        out_shape=[edge_shape(centre.shape[0], w) for w in widths] * 3,
        in_specs=[WHOLE] * 4,
        out_specs=[WHOLE] * (3 * len(widths)),
        compiler_params=params(),
        name="take_back",
    )(returned, wanted, centre, wide)
    count = len(widths)
    return [outs[place * count : (place + 1) * count] for place in range(3)]


def fill_split(pieces, split):
    rows = pieces[0].shape[0]
    start = 0
    for block in pieces:
        span = slice(start, start + block.shape[1])
        high, low = halves(block[...])
        split[:rows, span] = high
        split[rows:, span] = low
        start += block.shape[1]


def gathered(split, chosen, own, g, group):
    rows = HARM * TENSORS
    both = dot(split[...], chosen)
    for q in range(group):
        g[:, lanes_of(q)] = both[:rows, lanes_of(q)] + both[rows:, lanes_of(q)] + own[...]


def contracted(geo, group, g, value):
    columns = []
    for q in range(group):
        span = lanes_of(q)
        sums = [g[0:TENSORS, span], None, None]
        for m in range(1, HARM):
            term = g[rows_of(m), span] * geo[m, q : q + 1, :]
            d = DEGREE[m]
            sums[d] = term if sums[d] is None else sums[d] + term
        columns.append(jnp.concatenate([part * value[:, span] for part in sums], 0))
    return jnp.concatenate(columns, 1)


def middle_kernel(*refs, group, per, norm, count, aliased):
    geo, nbrs, own, x, lx, val, s_w, mix_w, cols = refs[:9]
    pieces = refs[9 : 9 + count]
    g, slope_out, x_out, emb_out, val_out, lx_out, env_all, env_out, split = refs[
        9 + count + aliased :
    ]
    step = pl.program_id(0)

    @pl.when(step == 0)
    def _():
        fill_split(pieces, split)

    chosen = chosen_columns(nbrs, group, split.shape[1])
    gathered(split, chosen, own, g, group)
    s = contracted(geo, group, g, val[...])
    update, slope = silu_pair(lx[...] + product(s_w[0], s))
    slope_out[...] = slope
    fresh = x[...] + update
    x_out[...] = fresh
    mixed = product(mix_w[1], fresh)
    emb_out[...] = mixed[:TENSORS]
    val_out[...] = mixed[TENSORS : 2 * TENSORS]
    lx_out[...] = mixed[2 * TENSORS :] + cols[:, 1:2]
    add_env(geo, step, per, group, mixed, env_out, norm)
    env_all[...] = env_out[...]


def middle_pass(geo, nbrs, own, pieces, x, lx, val, s_w, mix_w, cols, slots, group, span, before):
    edges = x.shape[1]
    per = slots // group
    first = span[0] * per
    rows = (HARM * TENSORS, LATENT, LATENT, TENSORS, TENSORS, LATENT)
    ins = 9 + len(pieces)
    return pl.pallas_call(
        partial(
            middle_kernel, group=group, per=per, norm=1.0 / math.sqrt(slots),
            count=len(pieces), aliased=len(before),
        ),
        grid=((span[1] - span[0]) * per,),
        out_shape=[edge_shape(r, edges) for r in rows]
        + [edge_shape(HARM * TENSORS, w) for w in (own.shape[1], (span[1] - span[0]) * UNIT)],
        in_specs=[
            row_spec(18, group, first),
            index_spec(group, first),
            wide_unit_spec(HARM * TENSORS, per, span[0]),
        ]
        + [edge_spec(r, group, first) for r in (LATENT, LATENT, TENSORS)]
        + [WHOLE] * (3 + len(pieces))
        + [pl.BlockSpec(memory_space=pl.ANY)] * len(before),
        out_specs=[edge_spec(r, group, first) for r in rows]
        + [wide_unit_spec(HARM * TENSORS, per, span[0]), unit_spec(HARM * TENSORS, per)],
        scratch_shapes=[
            pltpu.VMEM((2 * HARM * TENSORS, sum(p.shape[1] for p in pieces)), BF16)
        ],
        input_output_aliases={ins + n: n for n in range(len(before))},
        compiler_params=params(),
        cost_estimate=effort(8 * HARM * TENSORS * edges * edges // slots),
        name="middle_pass",
    )(geo, nbrs, own, x, lx, val, s_w, mix_w, cols, *pieces, *before)


def effort(flops):
    return pl.CostEstimate(flops=flops, transcendentals=0, bytes_accessed=flops // 512)


def pull_mixed(geo, group, g, value, ds, chosen, dgeo, centre, wide, across, dg):
    columns = []
    for q in range(group):
        span = lanes_of(q)
        part = value[:, span]
        pulled = [ds[rows_of(d), span] for d in range(3)]
        scaled = [p * part for p in pulled]
        total = None
        for m in range(HARM):
            d = DEGREE[m]
            source = g[rows_of(m), span]
            if m == 0:
                total = source * pulled[0]
                grad = scaled[0]
            else:
                harm = geo[m, q : q + 1, :]
                total = total + source * pulled[d] * harm
                dgeo[m, q : q + 1, :] += jnp.sum(source * scaled[d], axis=0, keepdims=True)
                grad = scaled[d] * harm
            centre[rows_of(m), :] += grad
            high, low = halves(grad)
            dg[rows_of(m), span] = high
            dg[rows_of(HARM + m), span] = low
        columns.append(total)
    both = dot_nt(dg[...], chosen)
    rows = HARM * TENSORS
    total = both[:rows] + both[rows:]
    wide[...] += total[:, : wide.shape[1]]
    across[...] += total[:, wide.shape[1] :]
    return jnp.concatenate(columns, 1)


def last_kernel(*refs, group, per, norm, count):
    geo, nbrs, own, x, lx, val, s_w, back_w, cols, base = refs[:10]
    pieces = refs[10 : 10 + count]
    energy, esum, dx_out, dval_out, dgeo, centre, wide, across, split, g, dg = refs[10 + count :]
    step = pl.program_id(0)

    @pl.when(step == 0)
    def _():
        fill_split(pieces, split)
        wide[...] = jnp.zeros_like(wide)
        across[...] = jnp.zeros_like(across)
        esum[...] = jnp.zeros_like(esum)

    @pl.when(step % per == 0)
    def _():
        energy[...] = base[...]
        centre[...] = jnp.zeros_like(centre)

    chosen = chosen_columns(nbrs, group, split.shape[1])
    gathered(split, chosen, own, g, group)
    value = val[...]
    s = contracted(geo, group, g, value)
    update, slope = silu_pair(lx[...] + product(s_w[1], s))
    fresh = x[...] + update
    weight = cols[:, 2:3]
    read = jnp.sum(fresh * weight, axis=0, keepdims=True) * norm
    cuts = []
    dgeo[...] = jnp.zeros_like(dgeo)
    for q in range(group):
        cut = geo[0, q : q + 1, :]
        cuts.append(cut)
        energy[...] += read[:, lanes_of(q)] * cut
        dgeo[0, q : q + 1, :] = read[:, lanes_of(q)]

    @pl.when(step % per == per - 1)
    def _():
        esum[0:1, :] += energy[...]

    d_fresh = weight * (jnp.concatenate(cuts, 1) * norm)
    pulled = product(back_w[1], d_fresh * slope)
    dx_out[...] = d_fresh + pulled[:LATENT]
    dval_out[...] = pull_mixed(
        geo, group, g, value, pulled[LATENT:], chosen, dgeo, centre, wide, across, dg
    )


def last_pass(geo, nbrs, own, pieces, x, lx, val, s_w, back_w, cols, base, slots, group):
    edges = x.shape[1]
    per = slots // group
    rows = HARM * TENSORS
    columns = sum(p.shape[1] for p in pieces)
    return pl.pallas_call(
        partial(
            last_kernel, group=group, per=per, norm=1.0 / math.sqrt(slots), count=len(pieces)
        ),
        grid=(geo.shape[1] // group,),
        out_shape=[
            jax.ShapeDtypeStruct(base.shape, F32),
            edge_shape(8, UNIT),
            edge_shape(LATENT, edges),
            edge_shape(TENSORS, edges),
            jax.ShapeDtypeStruct((HARM,) + geo.shape[1:], F32),
            edge_shape(rows, base.shape[1]),
            edge_shape(rows, columns - base.shape[1]),
            edge_shape(rows, base.shape[1]),
        ],
        in_specs=[row_spec(18, group, 0), index_spec(group, 0), unit_spec(rows, per)]
        + [edge_spec(r, group, 0) for r in (LATENT, LATENT, TENSORS)]
        + [WHOLE] * 3
        + [unit_spec(1, per)]
        + [WHOLE] * len(pieces),
        out_specs=[
            unit_spec(1, per),
            WHOLE,
            edge_spec(LATENT, group, 0),
            edge_spec(TENSORS, group, 0),
            row_spec(HARM, group, 0),
            unit_spec(rows, per),
            WHOLE,
            WHOLE,
        ],
        scratch_shapes=[
            pltpu.VMEM((2 * rows, columns), BF16),
            pltpu.VMEM((rows, group * UNIT), F32),
            pltpu.VMEM((2 * rows, group * UNIT), BF16),
        ],
        compiler_params=params(),
        cost_estimate=effort(16 * rows * edges * edges // slots),
        name="last_pass",
    )(geo, nbrs, own, x, lx, val, s_w, back_w, cols, base, *pieces)


def pull_env(geo, group, total, emb, dgeo, norm):
    columns = []
    for q in range(group):
        part = emb[:, lanes_of(q)]
        cut = geo[0, q : q + 1, :] * norm
        grad = None
        for m in range(HARM):
            source = total[rows_of(m), :]
            if m == 0:
                grad = source
            else:
                grad = grad + source * geo[m, q : q + 1, :]
                dgeo[m, q : q + 1, :] += cut * jnp.sum(source * part, axis=0, keepdims=True)
        dgeo[0, q : q + 1, :] += norm * jnp.sum(grad * part, axis=0, keepdims=True)
        columns.append(grad * cut)
    return jnp.concatenate(columns, 1)


def middle_back_kernel(*refs, group, per, norm, aliased):
    geo, nbrs, own, low, high, dgeo_in, dx, dval, emb, g, slope, val, ev_w, back_w = refs[:14]
    wide_in, across_in = refs[14:16] if aliased else (None, None)
    dx_out, dval_out, dgeo, centre, wide, across, total, dg = refs[14 + aliased :]
    step = pl.program_id(0)

    @pl.when(step == 0)
    def _():
        wide[...] = wide_in[...] if aliased else jnp.zeros_like(wide)
        across[...] = across_in[...] if aliased else jnp.zeros_like(across)

    @pl.when(step % per == 0)
    def _():
        total[...] = own[...] + low[...] + high[...]
        centre[...] = jnp.zeros_like(centre)

    chosen = chosen_columns(nbrs, group, wide.shape[1] + across.shape[1])
    dgeo[...] = dgeo_in[...]
    demb = pull_env(geo, group, total, emb, dgeo, norm)
    d_fresh = dx[...] + product(ev_w[1], jnp.concatenate([demb, dval[...]], 0))
    pulled = product(back_w[0], d_fresh * slope[...])
    dx_out[...] = d_fresh + pulled[:LATENT]
    dval_out[...] = pull_mixed(
        geo, group, g, val[...], pulled[LATENT:], chosen, dgeo, centre, wide, across, dg
    )


def middle_back(
    geo, nbrs, grads, dgeo, dx, dval, emb, g, slope, val, ev_w, back_w, slots, group, span, before
):
    edges = dx.shape[1]
    per = slots // group
    first = span[0] * per
    rows = HARM * TENSORS
    atoms = geo.shape[1] // slots * UNIT
    aliased = len(before)
    shapes = [
        edge_shape(LATENT, edges),
        edge_shape(TENSORS, edges),
        jax.ShapeDtypeStruct((HARM,) + geo.shape[1:], F32),
        edge_shape(rows, atoms),
        edge_shape(rows, 3 * atoms),
        edge_shape(rows, atoms),
    ]
    extra = [*before[4:], *before[:4]]
    return pl.pallas_call(
        partial(
            middle_back_kernel, group=group, per=per, norm=1.0 / math.sqrt(slots), aliased=aliased
        ),
        grid=((span[1] - span[0]) * per,),
        out_shape=shapes,
        in_specs=[row_spec(18, group, first), index_spec(group, first)]
        + [unit_spec(rows, per)] * 3
        + [row_spec(HARM, group, first)]
        + [
            edge_spec(r, group, first)
            for r in (LATENT, TENSORS, TENSORS, rows, LATENT, TENSORS)
        ]
        + [WHOLE] * 2
        + ([WHOLE] * 2 + [pl.BlockSpec(memory_space=pl.ANY)] * 4 if before else []),
        out_specs=[
            edge_spec(LATENT, group, first),
            edge_spec(TENSORS, group, first),
            row_spec(HARM, group, first),
            wide_unit_spec(rows, per, span[0]),
            WHOLE,
            WHOLE,
        ],
        scratch_shapes=[
            pltpu.VMEM((rows, UNIT), F32),
            pltpu.VMEM((2 * rows, group * UNIT), BF16),
        ],
        input_output_aliases={16 + n: n for n in range(4)} if before else {},
        compiler_params=params(),
        cost_estimate=effort(8 * rows * edges * edges // slots),
        name="middle_back",
    )(geo, nbrs, *grads, dgeo, dx, dval, emb, g, slope, val, ev_w, back_w, *extra)


def first_back_kernel(
    geo, own, low, high, dgeo_in, dx, dval, emb, slope, ev_w, rad_w, *rest, group, per, norm
):
    dgeo, total = rest[-2:]
    step = pl.program_id(0)

    @pl.when(step % per == 0)
    def _():
        total[...] = own[...] + low[...] + high[...]

    dgeo[0:HARM] = dgeo_in[...]
    demb = pull_env(geo, group, total, emb, dgeo, norm)
    d_fresh = dx[...] + product(ev_w[0], jnp.concatenate([demb, dval[...]], 0))
    radial = product(rad_w[...], d_fresh * slope[...])
    for q in range(group):
        for n in range(BASIS):
            dgeo[HARM + n, q : q + 1, :] = radial[n : n + 1, lanes_of(q)]


def first_back(
    geo, grads, dgeo, dx, dval, emb, slope, ev_w, rad_w, slots, group, span, before
):
    per = slots // group
    first = span[0] * per
    rows = HARM * TENSORS
    return pl.pallas_call(
        partial(first_back_kernel, group=group, per=per, norm=1.0 / math.sqrt(slots)),
        grid=((span[1] - span[0]) * per,),
        out_shape=jax.ShapeDtypeStruct((HARM + BASIS,) + geo.shape[1:], F32),
        in_specs=[row_spec(18, group, first)]
        + [unit_spec(rows, per)] * 3
        + [row_spec(HARM, group, first)]
        + [edge_spec(r, group, first) for r in (LATENT, TENSORS, TENSORS, LATENT)]
        + [WHOLE] * 2
        + [pl.BlockSpec(memory_space=pl.ANY)] * len(before),
        out_specs=row_spec(HARM + BASIS, group, first),
        scratch_shapes=[pltpu.VMEM((rows, UNIT), F32)],
        input_output_aliases={11 + n: n for n in range(len(before))},
        compiler_params=params(),
        cost_estimate=effort(64 * LATENT * LATENT * dx.shape[1]),
        name="first_back",
    )(geo, *grads, dgeo, dx, dval, emb, slope, ev_w, rad_w, *before)


def geometry_back_kernel(vec, dgeo, nbrs, centre_out, wide_out, across_out, dvec, *, slots):
    rows_total = vec.shape[1]
    units = rows_total // slots
    for group in range(rows_total // 8):
        up = slice(group * 8, group * 8 + 8)
        vx, vy, vz = (vec[axis, up, :] for axis in range(3))
        inverse, cut, slope, sine, cosine = distances(vx, vy, vz)
        ux, uy, uz = vx * inverse, vy * inverse, vz * inverse
        _, h1, h2, h3, h4, h5, h6, h7, h8 = (dgeo[m, up, :] for m in range(HARM))
        dux = h1 + ROOT3 * (uy * h4 + uz * h7 + ux * h8)
        duy = h2 + ROOT3 * (ux * h4 + uz * h5 - uy * h8)
        duz = h3 + ROOT3 * (uy * h5 + ux * h7) + 3.0 * uz * h6
        along = ux * dux + uy * duy + uz * duz
        scale = math.sqrt(2.0 / CUTOFF) * inverse
        by_wave = jnp.zeros_like(sine)
        by_angle = jnp.zeros_like(sine)
        before, now = jnp.zeros_like(sine), sine
        before_c, now_c = jnp.ones_like(sine), cosine
        for n in range(BASIS):
            pulled = dgeo[HARM + n, up, :]
            by_wave = by_wave + pulled * now
            by_angle = by_angle + (n + 1.0) * (pulled * now_c)
            before, now = now, 2.0 * cosine * now - before
            before_c, now_c = now_c, 2.0 * cosine * now_c - before_c
        d_dist = slope * dgeo[0, up, :] + scale * (
            (math.pi / CUTOFF) * by_angle * cut + by_wave * (slope - inverse * cut)
        )
        dvec[0, up, :] = (dux - ux * along) * inverse + ux * d_dist
        dvec[1, up, :] = (duy - uy * along) * inverse + uy * d_dist
        dvec[2, up, :] = (duz - uz * along) * inverse + uz * d_dist
    total = jnp.zeros((2 * 48, UNIT), F32)
    rows = lax.broadcasted_iota(jnp.int32, (16, UNIT), 0)
    lane = lax.broadcasted_iota(jnp.int32, (UNIT, UNIT), 0)
    for group in range(rows_total // 4):
        spreads, picks = [], []
        for k in range(group * 4, group * 4 + 4):
            index = nbrs[k : k + 1, :]
            here = rows == lax.shift_right_arithmetic(index, 7)
            spreads.append(
                jnp.concatenate(
                    [jnp.where(here, dvec[axis, k : k + 1, :], 0.0) for axis in range(3)], 0
                )
            )
            picks.append((lane == (index & 127)).astype(F32).astype(BF16))
        spread = jnp.concatenate(spreads, 1)
        total = total + dot_nt(stacked(spread), jnp.concatenate(picks, 1))
    total = total[:48] + total[48:]
    wide_out[...] = jnp.zeros_like(wide_out)
    across_out[...] = jnp.zeros_like(across_out)
    centre_out[...] = jnp.zeros_like(centre_out)
    for axis in range(3):
        for block in range(4 * units):
            row = axis * 16 + block
            out, place = (wide_out, block) if block < 3 * units else (across_out, block - 3 * units)
            out[axis : axis + 1, lanes_of(place)] = total[row : row + 1]
        for unit in range(units):
            part = dvec[axis, unit * slots : (unit + 1) * slots, :]
            centre_out[axis : axis + 1, lanes_of(unit)] = -jnp.sum(part, axis=0, keepdims=True)


def geometry_back(vec, dgeo, nbrs, slots):
    atoms = vec.shape[1] // slots * UNIT
    return pl.pallas_call(
        partial(geometry_back_kernel, slots=slots),
        out_shape=[edge_shape(8, atoms), edge_shape(8, 3 * atoms), edge_shape(8, atoms)],
        in_specs=[WHOLE] * 3,
        out_specs=[WHOLE] * 3,
        scratch_shapes=[pltpu.VMEM(vec.shape, F32)],
        compiler_params=params(),
        name="geometry_back",
    )(vec, dgeo, nbrs)


def swap_y(rows, face):
    if lax.axis_size("gy") == 2:
        return passed_along(rows, "gy", 1)
    up = passed_along(rows[:, :face], "gy", 1)
    down = passed_along(rows[:, face:], "gy", -1)
    return jnp.concatenate([up, down], 1)


def return_y(rows, face):
    if lax.axis_size("gy") == 2:
        return passed_along(rows, "gy", 1)
    up = passed_along(rows[:, :face], "gy", -1)
    down = passed_along(rows[:, face:], "gy", 1)
    return jnp.concatenate([up, down], 1)


def ghost_rows(parts, wanted, face):
    below, above = [], []
    for part in parts:
        if below:
            part, below[-1], above[-1] = lax.optimization_barrier((part, below[-1], above[-1]))
        below.append(passed_along(part, "gx", 1))
        above.append(passed_along(part, "gx", -1))
    pieces = [*parts, *below, *above]
    return pieces + [swap_y(lend_env(wanted, pieces), face)]


def owned_grads(centre, wide, across, wanted, face, widths):
    returned = return_y(across, face)
    own, below, above = take_back(returned, wanted, centre, wide, widths)
    found = []
    for number in range(len(widths)):
        send = below[number], above[number]
        if found:
            send, found[-1] = lax.optimization_barrier((send, found[-1]))
        found.append(
            [own[number], passed_along(send[0], "gx", -1), passed_along(send[1], "gx", 1)]
        )
    return found


def sum_steps():
    count = lax.axis_size("gx")
    if count & (count - 1) or lax.axis_size("gy") != 2:
        return None
    return [("gy", 1)] + [("gx", 1 << n) for n in range(count.bit_length() - 1)]


def sum_step(total, steps):
    if steps:
        axis, by = steps.pop(0)
        total = total + passed_along(total, axis, by)
    return total


def per_device(
    positions,
    species,
    neighbours,
    send_x,
    send_y,
    two_weight,
    two_bias,
    env_weight,
    value_weight,
    latent_weight,
    latent_bias,
    out_weight,
    species_shift,
):
    group = 16
    nbrs = neighbours[0, 0]
    atoms = nbrs.shape[1]
    face = send_y.shape[3]
    rows = jnp.concatenate(
        [
            positions[0, 0],
            species[0, 0][None].astype(F32),
            send_x[0, 0].astype(F32),
            jnp.zeros((2, atoms), F32),
        ],
        0,
    )
    wanted = jnp.concatenate(
        [
            send_y[0, 0, 1],
            send_y[0, 0, 0],
            jnp.full((atoms - 2 * face,), -1, jnp.int32),
        ]
    )[None]
    below = passed_along(rows, "gx", 1)
    above = passed_along(rows, "gx", -1)
    two_w, mix_w, s_w, back_w, ev_w, rad_w, cols = prepare_weights(
        two_weight, two_bias, env_weight, value_weight, latent_weight, latent_bias, out_weight
    )
    lent, wanted = lend_rows(rows, below, above, wanted)
    across = swap_y(lent, face)
    slots = nbrs.shape[0]
    units = atoms // UNIT
    vec, geo, nbrs, base = geometry(rows, below, above, across, nbrs, species_shift, face)
    parts, before = [], []
    for span in ((0, 1), (1, units)):
        *before, part = first_pass(
            geo, rows, two_w, mix_w, cols, slots, group, span, before
        )
        parts.append(part)
    x0, slope_a, emb0, val0, lx0, env0 = before
    pieces = ghost_rows(parts, wanted, face)
    parts, before = [], []
    for span in ((0, units - 1), (units - 1, units)):
        *before, part = middle_pass(
            geo, nbrs, env0, pieces, x0, lx0, val0, s_w, mix_w, cols, slots, group, span, before
        )
        parts.append(part)
    g0, slope0, x1, emb1, val1, lx1, env1 = before
    pieces = ghost_rows(parts, wanted, face)
    energy, total, dx, dval, dgeo, centre, wide, across = last_pass(
        geo, nbrs, env1, pieces, x1, lx1, val1, s_w, back_w, cols, base, slots, group
    )
    steps = sum_steps()
    if steps is None:
        total = lax.psum(total, ("gx", "gy"))
    total = sum_step(total, steps)
    grads = owned_grads(centre, wide, across, wanted, face, (UNIT, atoms - UNIT))
    before = []
    for number, span in enumerate(((0, 1), (1, units))):
        grads[number][0], total = lax.optimization_barrier((grads[number][0], total))
        total = sum_step(total, steps)
        before = middle_back(
            geo, nbrs, grads[number], dgeo, dx, dval, emb1, g0, slope0, val0, ev_w, back_w,
            slots, group, span, before,
        )
    dx, dval, dgeo, centre, wide, across = before
    grads = owned_grads(centre, wide, across, wanted, face, (atoms - UNIT, UNIT))
    before = []
    for number, span in enumerate(((0, units - 1), (units - 1, units))):
        grads[number][0], total = lax.optimization_barrier((grads[number][0], total))
        total = sum_step(total, steps)
        before = [
            first_back(
                geo, grads[number], dgeo, dx, dval, emb0, slope_a, ev_w, rad_w, slots, group,
                span, before,
            )
        ]
    (dgeo,) = before
    while steps:
        total = sum_step(total, steps)
    mean_energy = jnp.sum(total) / (atoms * lax.axis_size("gx") * lax.axis_size("gy"))
    (grads,) = owned_grads(*geometry_back(vec, dgeo, nbrs, slots), wanted, face, (atoms,))
    forces = -(grads[0] + grads[1] + grads[2])[:3]
    return (energy[None], forces[None, None], mean_energy.reshape(1))


def solution(mesh):
    placed = (
        P(("groups", "gx"), "gy", None, None),
        P(("groups", "gx"), "gy", None),
        P(("groups", "gx"), "gy", None, None),
        P(("groups", "gx"), "gy", None, None),
        P(("groups", "gx"), "gy", None, None),
        P(),
        P(),
        P(),
        P(),
        P(),
        P(),
        P(),
        P(),
    )
    return jax.shard_map(
        per_device,
        mesh=mesh,
        in_specs=placed,
        out_specs=(
            P(("groups", "gx"), "gy", None),
            P(("groups", "gx"), "gy", None, None),
            P("groups"),
        ),
        check_vma=False,
    )
```

```python
from functools import partial
import math

import jax
import jax.numpy as jnp
from jax import lax
from jax.experimental import pallas as pl
from jax.experimental.pallas import tpu as pltpu
from jax.sharding import PartitionSpec as P

BASIS = 8
SPECIES = 5
SITES_X = 2
SITES_Y = 16
CUTOFF = 2.5
LATENT = 128
TENSORS = 32
HARM = 9
UNIT = 128
ROOT3 = math.sqrt(3.0)
DEGREE = (0, 1, 1, 1, 2, 2, 2, 2, 2)
F32 = jnp.float32
BF16 = jnp.bfloat16
WHOLE = pl.BlockSpec(memory_space=pltpu.VMEM)
SCALARS = pl.BlockSpec(memory_space=pltpu.SMEM)


def params():
    return pltpu.CompilerParams(vmem_limit_bytes=60 << 20)


def passed_along(value, axis, by):
    count = lax.axis_size(axis)
    return lax.ppermute(value, axis, [(i, (i + by) % count) for i in range(count)])


def dot(a, b):
    return jnp.dot(a, b, preferred_element_type=F32)


def dot_nt(a, b):
    return lax.dot_general(a, b, (((1,), (1,)), ((), ())), preferred_element_type=F32)


def halves(value):
    high = value.astype(BF16)
    return high, (value - high.astype(F32)).astype(BF16)


def stacked(value):
    return jnp.concatenate(halves(value), 0)


def product(weights, value):
    rows = weights.shape[0] // 2
    both = dot(weights, stacked(value))
    return both[:rows] + both[rows:]


def rounded(value):
    high = value.astype(BF16).astype(F32)
    return high, value - high


def weights_kernel(two, bias, env, val, lat, lat_bias, out_w, *outs):
    two_out, mix_out, s_out, back_out, ev_out, rad_out, cols = outs

    def depth_stack(piece):
        high, low = rounded(piece)
        top = jnp.concatenate([high, high], 0)
        bottom = jnp.concatenate([low, jnp.zeros_like(low)], 0)
        return top.T, bottom.T

    def lane_stack(piece):
        high, low = rounded(piece)
        top = jnp.concatenate([high, high], 1)
        return top, jnp.concatenate([low, jnp.zeros_like(low)], 1)

    def join(pieces):
        tops, bottoms = zip(*pieces)
        return jnp.concatenate(list(tops) + list(bottoms), 0).astype(BF16)

    def wide_stack(piece):
        return jnp.concatenate(lane_stack(piece), 0).astype(BF16)

    width = two.shape[1]
    first = jnp.concatenate(
        [
            two[0:SPECIES, :],
            bias[...],
            jnp.zeros((2, width), F32),
            two[SPECIES : 2 * SPECIES, :],
            jnp.zeros((3, width), F32),
            two[2 * SPECIES :, :],
        ],
        0,
    )
    two_out[...] = join([depth_stack(first)])
    rad_out[...] = wide_stack(two[2 * SPECIES :, :])
    for layer in range(env.shape[0]):
        latent = lat[layer]
        mix_out[layer] = join(
            [lane_stack(env[layer]), lane_stack(val[layer]), depth_stack(latent[:width])]
        )
        s_out[layer] = join([depth_stack(latent[width:])])
        back_out[layer] = wide_stack(latent)
        high = [rounded(env[layer]), rounded(val[layer])]
        top = jnp.concatenate([high[0][0], high[1][0]] * 2, 0).T
        bottom = jnp.concatenate([high[0][1], high[1][1]] + [jnp.zeros_like(high[0][1])] * 2, 0).T
        ev_out[layer] = jnp.concatenate([top, bottom], 0).astype(BF16)
    columns = jnp.concatenate(
        [lat_bias[...], out_w[...], jnp.zeros((8 - lat_bias.shape[0] - 1, width), F32)], 0
    )
    cols[...] = columns.T


def prepare_weights(two, bias, env, val, lat, lat_bias, out_w):
    layers = env.shape[0]
    shapes = [
        (2 * LATENT, 48),
        (layers, 2 * (LATENT + 2 * TENSORS), 2 * LATENT),
        (layers, 2 * LATENT, 6 * TENSORS),
        (layers, 2 * (LATENT + 3 * TENSORS), 2 * LATENT),
        (layers, 2 * LATENT, 4 * TENSORS),
        (2 * BASIS, 2 * LATENT),
    ]
    out_shape = [jax.ShapeDtypeStruct(s, BF16) for s in shapes]
    out_shape.append(jax.ShapeDtypeStruct((LATENT, 8), F32))
    return pl.pallas_call(
        weights_kernel,
        out_shape=out_shape,
        in_specs=[WHOLE] * 7,
        out_specs=[WHOLE] * 7,
        compiler_params=params(),
        name="prepare_weights",
    )(two, bias[None], env.swapaxes(1, 2), val.swapaxes(1, 2), lat, lat_bias, out_w[None])


def shifted(rows, by_x, by_y):
    lane_row = lax.broadcasted_iota(jnp.int32, rows.shape, 0)
    return rows + jnp.where(lane_row == 0, by_x, jnp.where(lane_row == 1, by_y, 0.0))


def lane_pick(table, row, index, blocks):
    low = index & 127
    high = lax.shift_right_arithmetic(index, 7)
    found = jnp.zeros(index.shape, F32)
    for block in range(blocks):
        span = slice(block * 128, block * 128 + 128)
        source = table[...][:, span] if row is None else table[row : row + 1, span]
        source = jnp.broadcast_to(source, index.shape)
        taken = jnp.take_along_axis(source, low, axis=1)
        found = jnp.where(high == block, taken, found)
    return found


def fill_wide(own, below, above, table, remap):
    atoms = own.shape[1]
    table[:, 0:atoms] = own[...]
    table[:, atoms : 2 * atoms] = shifted(below[...], -float(SITES_X), 0.0)
    table[:, 2 * atoms : 3 * atoms] = shifted(above[...], float(SITES_X), 0.0)
    lanes = lax.broadcasted_iota(jnp.int32, (1, atoms), 1).astype(F32)
    remap[:, 0:atoms] = lanes
    remap[:, atoms : 2 * atoms] = below[5:6, :] + float(atoms)
    remap[:, 2 * atoms : 3 * atoms] = above[4:5, :] + float(2 * atoms)


def lend_kernel(own, below, above, wanted, rows_out, wanted_out, table, remap):
    atoms = own.shape[1]
    blocks = 3 * atoms // 128
    fill_wide(own, below, above, table, remap)
    for tile in range(wanted.shape[1] // 128):
        span = slice(tile * 128, tile * 128 + 128)
        index = jnp.broadcast_to(wanted[:, span], (8, 128))
        place = lane_pick(remap, 0, index, blocks).astype(jnp.int32)
        place = jnp.where(index < 0, -1, place)
        wanted_out[:, span] = place[0:1]
        rows_out[:, span] = lane_pick(table, None, place, blocks)


def lend_rows(own, below, above, wanted):
    atoms = own.shape[1]
    return pl.pallas_call(
        lend_kernel,
        out_shape=[
            jax.ShapeDtypeStruct(wanted.shape[:0] + (8, wanted.shape[1]), F32),
            jax.ShapeDtypeStruct(wanted.shape, jnp.int32),
        ],
        in_specs=[WHOLE] * 4,
        out_specs=[WHOLE] * 2,
        scratch_shapes=[pltpu.VMEM((8, 3 * atoms), F32), pltpu.VMEM((1, 3 * atoms), F32)],
        compiler_params=params(),
        name="lend_rows",
    )(own, below, above, wanted)


def distances(vx, vy, vz):
    dist = jnp.sqrt(vx * vx + vy * vy + vz * vz)
    inverse = 1.0 / dist
    scaled = jnp.minimum(dist * (1.0 / CUTOFF), 1.0)
    second = scaled * scaled
    fourth = second * second
    sixth = fourth * second
    cut = 1.0 - 28.0 * sixth + 48.0 * (sixth * scaled) - 21.0 * (sixth * second)
    rest = 1.0 - scaled
    slope = (-168.0 / CUTOFF) * (fourth * scaled) * (rest * rest)
    angle = scaled * math.pi
    return inverse, cut, slope, jnp.sin(angle), jnp.cos(angle)


def geometry_kernel(
    own, below, above, across, nbrs, shift, vec_out, geo_out, nbr_out, base_out, table, remap, face
):
    atoms = own.shape[1]
    slots = nbrs.shape[0]
    blocks = table.shape[1] // 128
    fill_wide(own, below, above, table, remap)
    lanes = lax.broadcasted_iota(jnp.int32, (8, atoms), 1)
    rows = lax.broadcasted_iota(jnp.int32, (8, atoms), 0)
    moved = across[...] + jnp.where(
        rows == 1, jnp.where(lanes < face, -float(SITES_Y), float(SITES_Y)), 0.0
    )
    empty = jnp.where(rows == 2, -1000.0, jnp.where(rows == 3, -1.0, 0.0))
    table[:, 3 * atoms : 4 * atoms] = jnp.where(lanes < 2 * face, moved, empty)
    remap[:, 3 * atoms : 4 * atoms] = (
        lax.broadcasted_iota(jnp.int32, (1, atoms), 1) + 3 * atoms
    ).astype(F32)
    base = jnp.zeros((1, atoms), F32)
    for kind in range(SPECIES):
        base = base + jnp.where(own[3:4, :] == float(kind), shift[kind], 0.0)
    base_out[...] = base
    for group in range(slots // 8):
        for tile in range(atoms // UNIT):
            span = slice(tile * UNIT, tile * UNIT + UNIT)
            index = nbrs[group * 8 : group * 8 + 8, span]
            up = slice(tile * slots + group * 8, tile * slots + group * 8 + 8)
            index = lane_pick(remap, 0, index, blocks).astype(jnp.int32)
            nbr_out[up, :] = index
            vx = lane_pick(table, 0, index, blocks) - own[0:1, span]
            vy = lane_pick(table, 1, index, blocks) - own[1:2, span]
            vz = lane_pick(table, 2, index, blocks) - own[2:3, span]
            kind = lane_pick(table, 3, index, blocks)
            vec_out[0, up, :] = vx
            vec_out[1, up, :] = vy
            vec_out[2, up, :] = vz
            inverse, cut, _, sine, cosine = distances(vx, vy, vz)
            ux, uy, uz = vx * inverse, vy * inverse, vz * inverse
            harm = [
                ux,
                uy,
                uz,
                ROOT3 * ux * uy,
                ROOT3 * uy * uz,
                0.5 * (3.0 * uz * uz - 1.0),
                ROOT3 * ux * uz,
                0.5 * ROOT3 * (ux * ux - uy * uy),
            ]
            geo_out[0, up, :] = cut
            for number, value in enumerate(harm):
                geo_out[1 + number, up, :] = value
            scale = math.sqrt(2.0 / CUTOFF) * inverse * cut
            before, now = jnp.zeros_like(sine), sine
            for number in range(BASIS):
                geo_out[9 + number, up, :] = now * scale
                before, now = now, 2.0 * cosine * now - before
            geo_out[17, up, :] = kind


def geometry(own, below, above, across, nbrs, shift, face):
    slots, atoms = nbrs.shape
    return pl.pallas_call(
        partial(geometry_kernel, face=face),
        out_shape=[
            jax.ShapeDtypeStruct((3, slots * atoms // UNIT, UNIT), F32),
            jax.ShapeDtypeStruct((18, slots * atoms // UNIT, UNIT), F32),
            jax.ShapeDtypeStruct((slots * atoms // UNIT, UNIT), jnp.int32),
            jax.ShapeDtypeStruct((1, atoms), F32),
        ],
        in_specs=[WHOLE] * 5 + [SCALARS],
        out_specs=[WHOLE] * 4,
        scratch_shapes=[pltpu.VMEM((8, 4 * atoms), F32), pltpu.VMEM((1, 4 * atoms), F32)],
        compiler_params=params(),
        name="geometry",
    )(own, below, above, across, nbrs, shift)


def silu_pair(pre):
    gate = 1.0 / (1.0 + jnp.exp(-pre))
    value = pre * gate
    return value, gate + value * (1.0 - gate)


def row_spec(count, group, first):
    return pl.BlockSpec((count, group, UNIT), lambda i: (0, first + i, 0))


def index_spec(group, first):
    return pl.BlockSpec((group, UNIT), lambda i: (first + i, 0))


def edge_spec(rows, group, first):
    return pl.BlockSpec((rows, group * UNIT), lambda i: (0, first + i))


def unit_spec(rows, per):
    return pl.BlockSpec((rows, UNIT), lambda i: (0, i // per))


def edge_shape(rows, edges):
    return jax.ShapeDtypeStruct((rows, edges), F32)


def lanes_of(q):
    return slice(q * UNIT, (q + 1) * UNIT)


def rows_of(m):
    return slice(m * TENSORS, (m + 1) * TENSORS)


def add_env(geo, step, per, group, embed, env_out, norm):
    @pl.when(step % per == 0)
    def _():
        env_out[...] = jnp.zeros_like(env_out)

    cuts = [geo[0, q : q + 1, :] * norm for q in range(group)]
    for m in range(HARM):
        total = env_out[rows_of(m), :]
        for q in range(group):
            factor = cuts[q] if m == 0 else cuts[q] * geo[m, q : q + 1, :]
            total = total + embed[:TENSORS, lanes_of(q)] * factor
        env_out[rows_of(m), :] = total


def first_kernel(
    geo, own, two_w, mix_w, cols, *outs, group, per, norm
):
    x_out, slope_out, emb_out, val_out, lx_out, env_out = outs[-6:]
    step = pl.program_id(0)
    kinds = lax.broadcasted_iota(jnp.int32, (8, UNIT), 0)
    kinds_f = kinds.astype(F32)
    centre = jnp.where((own[3:4, :] == kinds_f) & (kinds < SPECIES), 1.0, 0.0)
    centre = jnp.where(kinds == SPECIES, 1.0, centre)
    parts = []
    for q in range(group):
        other = jnp.where(geo[17, q : q + 1, :] == kinds_f, 1.0, 0.0)
        radial = [geo[9 + n, q : q + 1, :] for n in range(BASIS)]
        parts.append(jnp.concatenate([centre, other] + radial, 0))
    features = jnp.concatenate(parts, 1)
    x, slope = silu_pair(product(two_w[...], features))
    x_out[...] = x
    slope_out[...] = slope
    mixed = product(mix_w[0], x)
    emb_out[...] = mixed[:TENSORS]
    val_out[...] = mixed[TENSORS : 2 * TENSORS]
    lx_out[...] = mixed[2 * TENSORS :] + cols[:, 0:1]
    add_env(geo, step, per, group, mixed, env_out, norm)


def wide_unit_spec(rows, per, first):
    return pl.BlockSpec((rows, UNIT), lambda i: (0, first + i // per))


def first_pass(geo, own, two_w, mix_w, cols, slots, group, span, before):
    edges = geo.shape[1] * UNIT
    per = slots // group
    first = span[0] * per
    rows = (LATENT, LATENT, TENSORS, TENSORS, LATENT)
    return pl.pallas_call(
        partial(first_kernel, group=group, per=per, norm=1.0 / math.sqrt(slots)),
        grid=((span[1] - span[0]) * per,),
        out_shape=[edge_shape(r, edges) for r in rows]
        + [edge_shape(HARM * TENSORS, (span[1] - span[0]) * UNIT)],
        in_specs=[row_spec(18, group, first), wide_unit_spec(8, per, span[0])]
        + [WHOLE] * 3
        + [pl.BlockSpec(memory_space=pl.ANY)] * len(before),
        out_specs=[edge_spec(r, group, first) for r in rows]
        + [unit_spec(HARM * TENSORS, per)],
        input_output_aliases={5 + n: n for n in range(len(before))},
        compiler_params=params(),
        cost_estimate=effort(64 * LATENT * LATENT * edges),
        name="first_pass",
    )(geo, own, two_w, mix_w, cols, *before)


def chosen_rows(index, columns, start):
    rows = lax.broadcasted_iota(jnp.int32, (columns, index.shape[1]), 0) + start
    return (rows == index).astype(F32).astype(BF16)


def mark_atoms(nbrs, unit, chosen):
    start = pl.multiple_of(unit * UNIT, UNIT)
    rows = lax.broadcasted_iota(jnp.int32, (UNIT, UNIT), 0)
    centre = (rows == lax.broadcasted_iota(jnp.int32, (UNIT, UNIT), 1)).astype(F32)
    for q in range(nbrs.shape[0]):
        index = nbrs[q : q + 1, :]
        chosen[:, lanes_of(q)] = chosen_rows(index, chosen.shape[0], 0)
        both = (rows + start == index).astype(F32) + centre
        chosen[pl.ds(start, UNIT), lanes_of(q)] = both.astype(BF16)


def lend_env_kernel(wanted, *refs):
    out = refs[-1]
    rows = out.shape[0]
    total = jnp.zeros((2 * rows, out.shape[1]), F32)
    start = 0
    for block in refs[:-1]:
        chosen = chosen_rows(wanted[...], block.shape[1], start)
        total = total + dot(stacked(block[...]), chosen)
        start += block.shape[1]
    out[...] = total[:rows] + total[rows:]


def lend_env(wanted, pieces):
    return pl.pallas_call(
        lend_env_kernel,
        out_shape=jax.ShapeDtypeStruct((HARM * TENSORS, wanted.shape[1]), F32),
        in_specs=[WHOLE] * (1 + len(pieces)),
        out_specs=WHOLE,
        compiler_params=params(),
        name="lend_env",
    )(wanted, *pieces)


def take_back_kernel(returned, wanted, wide, *outs, widths):
    atoms = wide.shape[1] // 3
    rows = returned.shape[0]
    value = stacked(returned[...])
    for place in range(3):
        chosen = chosen_rows(wanted[...], atoms, place * atoms)
        both = dot_nt(value, chosen)
        total = wide[:, place * atoms : (place + 1) * atoms] + both[:rows] + both[rows:]
        start = 0
        for number, width in enumerate(widths):
            outs[place * len(widths) + number][...] = total[:, start : start + width]
            start += width


def take_back(returned, wanted, wide, widths):
    outs = pl.pallas_call(
        partial(take_back_kernel, widths=widths),
        out_shape=[edge_shape(wide.shape[0], w) for w in widths] * 3,
        in_specs=[WHOLE] * 3,
        out_specs=[WHOLE] * (3 * len(widths)),
        compiler_params=params(),
        name="take_back",
    )(returned, wanted, wide)
    count = len(widths)
    return [list(outs[place * count : (place + 1) * count]) for place in range(3)]


def fill_split(pieces, split):
    rows = pieces[0].shape[0]
    start = 0
    for block in pieces:
        span = slice(start, start + block.shape[1])
        high, low = halves(block[...])
        split[:rows, span] = high
        split[rows:, span] = low
        start += block.shape[1]


def gathered(split, chosen, g):
    rows = HARM * TENSORS
    both = dot(split[...], chosen[...])
    g[...] = both[:rows] + both[rows:]


def contracted(geo, group, g, value):
    columns = []
    for q in range(group):
        span = lanes_of(q)
        sums = [g[0:TENSORS, span], None, None]
        for m in range(1, HARM):
            term = g[rows_of(m), span] * geo[m, q : q + 1, :]
            d = DEGREE[m]
            sums[d] = term if sums[d] is None else sums[d] + term
        columns.append(jnp.concatenate([part * value[:, span] for part in sums], 0))
    return jnp.concatenate(columns, 1)


def middle_kernel(*refs, group, per, norm, count, aliased, first):
    geo, nbrs, x, lx, val, s_w, mix_w, cols = refs[:8]
    pieces = refs[8 : 8 + count]
    g, slope_out, x_out, emb_out, val_out, lx_out, env_out, split, chosen = refs[
        8 + count + aliased :
    ]
    step = pl.program_id(0)

    @pl.when(step == 0)
    def _():
        fill_split(pieces, split)

    mark_atoms(nbrs, first + step // per, chosen)
    gathered(split, chosen, g)
    s = contracted(geo, group, g, val[...])
    update, slope = silu_pair(lx[...] + product(s_w[0], s))
    slope_out[...] = slope
    fresh = x[...] + update
    x_out[...] = fresh
    mixed = product(mix_w[1], fresh)
    emb_out[...] = mixed[:TENSORS]
    val_out[...] = mixed[TENSORS : 2 * TENSORS]
    lx_out[...] = mixed[2 * TENSORS :] + cols[:, 1:2]
    add_env(geo, step, per, group, mixed, env_out, norm)


def middle_pass(geo, nbrs, pieces, x, lx, val, s_w, mix_w, cols, slots, group, span, before):
    edges = x.shape[1]
    per = slots // group
    first = span[0] * per
    rows = (HARM * TENSORS, LATENT, LATENT, TENSORS, TENSORS, LATENT)
    ins = 8 + len(pieces)
    columns = sum(p.shape[1] for p in pieces)
    return pl.pallas_call(
        partial(
            middle_kernel, group=group, per=per, norm=1.0 / math.sqrt(slots),
            count=len(pieces), aliased=len(before), first=span[0],
        ),
        grid=((span[1] - span[0]) * per,),
        out_shape=[edge_shape(r, edges) for r in rows]
        + [edge_shape(HARM * TENSORS, (span[1] - span[0]) * UNIT)],
        in_specs=[row_spec(18, group, first), index_spec(group, first)]
        + [edge_spec(r, group, first) for r in (LATENT, LATENT, TENSORS)]
        + [WHOLE] * (3 + len(pieces))
        + [pl.BlockSpec(memory_space=pl.ANY)] * len(before),
        out_specs=[edge_spec(r, group, first) for r in rows]
        + [unit_spec(HARM * TENSORS, per)],
        scratch_shapes=[
            pltpu.VMEM((2 * HARM * TENSORS, columns), BF16),
            pltpu.VMEM((columns, group * UNIT), BF16),
        ],
        input_output_aliases={ins + n: n for n in range(len(before))},
        compiler_params=params(),
        cost_estimate=effort(8 * HARM * TENSORS * edges * edges // slots),
        name="middle_pass",
    )(geo, nbrs, x, lx, val, s_w, mix_w, cols, *pieces, *before)


def effort(flops):
    return pl.CostEstimate(flops=flops, transcendentals=0, bytes_accessed=flops // 512)


def pull_mixed(geo, group, g, value, ds, chosen, dgeo, wide, across, dg):
    columns = []
    for q in range(group):
        span = lanes_of(q)
        part = value[:, span]
        pulled = [ds[rows_of(d), span] for d in range(3)]
        scaled = [p * part for p in pulled]
        total = None
        for m in range(HARM):
            d = DEGREE[m]
            source = g[rows_of(m), span]
            if m == 0:
                total = source * pulled[0]
                grad = scaled[0]
            else:
                harm = geo[m, q : q + 1, :]
                total = total + source * pulled[d] * harm
                dgeo[m, q : q + 1, :] += jnp.sum(source * scaled[d], axis=0, keepdims=True)
                grad = scaled[d] * harm
            high, low = halves(grad)
            dg[rows_of(m), span] = high
            dg[rows_of(HARM + m), span] = low
        columns.append(total)
    both = dot_nt(dg[...], chosen[...])
    rows = HARM * TENSORS
    total = both[:rows] + both[rows:]
    wide[...] += total[:, : wide.shape[1]]
    across[...] += total[:, wide.shape[1] :]
    return jnp.concatenate(columns, 1)


def last_kernel(*refs, group, per, norm, count):
    geo, nbrs, x, lx, val, s_w, back_w, cols, base = refs[:9]
    pieces = refs[9 : 9 + count]
    energy, esum, dx_out, dval_out, dgeo, wide, across, split, chosen, g, dg = refs[9 + count :]
    step = pl.program_id(0)

    @pl.when(step == 0)
    def _():
        fill_split(pieces, split)
        wide[...] = jnp.zeros_like(wide)
        across[...] = jnp.zeros_like(across)
        esum[...] = jnp.zeros_like(esum)

    @pl.when(step % per == 0)
    def _():
        energy[...] = base[...]

    mark_atoms(nbrs, step // per, chosen)
    gathered(split, chosen, g)
    value = val[...]
    s = contracted(geo, group, g, value)
    update, slope = silu_pair(lx[...] + product(s_w[1], s))
    fresh = x[...] + update
    weight = cols[:, 2:3]
    read = jnp.sum(fresh * weight, axis=0, keepdims=True) * norm
    cuts = []
    dgeo[...] = jnp.zeros_like(dgeo)
    for q in range(group):
        cut = geo[0, q : q + 1, :]
        cuts.append(cut)
        energy[...] += read[:, lanes_of(q)] * cut
        dgeo[0, q : q + 1, :] = read[:, lanes_of(q)]

    @pl.when(step % per == per - 1)
    def _():
        esum[0:1, :] += energy[...]

    d_fresh = weight * (jnp.concatenate(cuts, 1) * norm)
    pulled = product(back_w[1], d_fresh * slope)
    dx_out[...] = d_fresh + pulled[:LATENT]
    dval_out[...] = pull_mixed(
        geo, group, g, value, pulled[LATENT:], chosen, dgeo, wide, across, dg
    )


def last_pass(geo, nbrs, pieces, x, lx, val, s_w, back_w, cols, base, slots, group):
    edges = x.shape[1]
    per = slots // group
    rows = HARM * TENSORS
    columns = sum(p.shape[1] for p in pieces)
    return pl.pallas_call(
        partial(
            last_kernel, group=group, per=per, norm=1.0 / math.sqrt(slots), count=len(pieces)
        ),
        grid=(geo.shape[1] // group,),
        out_shape=[
            jax.ShapeDtypeStruct(base.shape, F32),
            edge_shape(8, UNIT),
            edge_shape(LATENT, edges),
            edge_shape(TENSORS, edges),
            jax.ShapeDtypeStruct((HARM,) + geo.shape[1:], F32),
            edge_shape(rows, columns - base.shape[1]),
            edge_shape(rows, base.shape[1]),
        ],
        in_specs=[row_spec(18, group, 0), index_spec(group, 0)]
        + [edge_spec(r, group, 0) for r in (LATENT, LATENT, TENSORS)]
        + [WHOLE] * 3
        + [unit_spec(1, per)]
        + [WHOLE] * len(pieces),
        out_specs=[
            unit_spec(1, per),
            WHOLE,
            edge_spec(LATENT, group, 0),
            edge_spec(TENSORS, group, 0),
            row_spec(HARM, group, 0),
            WHOLE,
            WHOLE,
        ],
        scratch_shapes=[
            pltpu.VMEM((2 * rows, columns), BF16),
            pltpu.VMEM((columns, group * UNIT), BF16),
            pltpu.VMEM((rows, group * UNIT), F32),
            pltpu.VMEM((2 * rows, group * UNIT), BF16),
        ],
        compiler_params=params(),
        cost_estimate=effort(16 * rows * edges * edges // slots),
        name="last_pass",
    )(geo, nbrs, x, lx, val, s_w, back_w, cols, base, *pieces)


def pull_env(geo, group, total, emb, dgeo, norm):
    columns = []
    for q in range(group):
        part = emb[:, lanes_of(q)]
        cut = geo[0, q : q + 1, :] * norm
        grad = None
        for m in range(HARM):
            source = total[rows_of(m), :]
            if m == 0:
                grad = source
            else:
                grad = grad + source * geo[m, q : q + 1, :]
                dgeo[m, q : q + 1, :] += cut * jnp.sum(source * part, axis=0, keepdims=True)
        dgeo[0, q : q + 1, :] += norm * jnp.sum(grad * part, axis=0, keepdims=True)
        columns.append(grad * cut)
    return jnp.concatenate(columns, 1)


def middle_back_kernel(*refs, group, per, norm, aliased, first):
    geo, nbrs, own, low, high, dgeo_in, dx, dval, emb, g, slope, val, ev_w, back_w = refs[:14]
    wide_in, across_in = refs[14:16] if aliased else (None, None)
    dx_out, dval_out, dgeo, wide, across, total, chosen, dg = refs[14 + aliased :]
    step = pl.program_id(0)

    @pl.when(step == 0)
    def _():
        wide[...] = wide_in[...] if aliased else jnp.zeros_like(wide)
        across[...] = across_in[...] if aliased else jnp.zeros_like(across)

    @pl.when(step % per == 0)
    def _():
        total[...] = own[...] + low[...] + high[...]

    mark_atoms(nbrs, first + step // per, chosen)
    dgeo[...] = dgeo_in[...]
    demb = pull_env(geo, group, total, emb, dgeo, norm)
    d_fresh = dx[...] + product(ev_w[1], jnp.concatenate([demb, dval[...]], 0))
    pulled = product(back_w[0], d_fresh * slope[...])
    dx_out[...] = d_fresh + pulled[:LATENT]
    dval_out[...] = pull_mixed(
        geo, group, g, val[...], pulled[LATENT:], chosen, dgeo, wide, across, dg
    )


def middle_back(
    geo, nbrs, grads, dgeo, dx, dval, emb, g, slope, val, ev_w, back_w, slots, group, span, before
):
    edges = dx.shape[1]
    per = slots // group
    first = span[0] * per
    rows = HARM * TENSORS
    atoms = geo.shape[1] // slots * UNIT
    aliased = len(before)
    shapes = [
        edge_shape(LATENT, edges),
        edge_shape(TENSORS, edges),
        jax.ShapeDtypeStruct((HARM,) + geo.shape[1:], F32),
        edge_shape(rows, 3 * atoms),
        edge_shape(rows, atoms),
    ]
    extra = [*before[3:], *before[:3]]
    return pl.pallas_call(
        partial(
            middle_back_kernel, group=group, per=per, norm=1.0 / math.sqrt(slots), aliased=aliased,
            first=span[0],
        ),
        grid=((span[1] - span[0]) * per,),
        out_shape=shapes,
        in_specs=[row_spec(18, group, first), index_spec(group, first)]
        + [unit_spec(rows, per)] * 3
        + [row_spec(HARM, group, first)]
        + [
            edge_spec(r, group, first)
            for r in (LATENT, TENSORS, TENSORS, rows, LATENT, TENSORS)
        ]
        + [WHOLE] * 2
        + ([WHOLE] * 2 + [pl.BlockSpec(memory_space=pl.ANY)] * 3 if before else []),
        out_specs=[
            edge_spec(LATENT, group, first),
            edge_spec(TENSORS, group, first),
            row_spec(HARM, group, first),
            WHOLE,
            WHOLE,
        ],
        scratch_shapes=[
            pltpu.VMEM((rows, UNIT), F32),
            pltpu.VMEM((4 * atoms, group * UNIT), BF16),
            pltpu.VMEM((2 * rows, group * UNIT), BF16),
        ],
        input_output_aliases={16 + n: n for n in range(3)} if before else {},
        compiler_params=params(),
        cost_estimate=effort(8 * rows * edges * edges // slots),
        name="middle_back",
    )(geo, nbrs, *grads, dgeo, dx, dval, emb, g, slope, val, ev_w, back_w, *extra)


def first_back_kernel(
    geo, own, low, high, dgeo_in, dx, dval, emb, slope, ev_w, rad_w, *rest, group, per, norm
):
    dgeo, total = rest[-2:]
    step = pl.program_id(0)

    @pl.when(step % per == 0)
    def _():
        total[...] = own[...] + low[...] + high[...]

    dgeo[0:HARM] = dgeo_in[...]
    demb = pull_env(geo, group, total, emb, dgeo, norm)
    d_fresh = dx[...] + product(ev_w[0], jnp.concatenate([demb, dval[...]], 0))
    radial = product(rad_w[...], d_fresh * slope[...])
    for q in range(group):
        for n in range(BASIS):
            dgeo[HARM + n, q : q + 1, :] = radial[n : n + 1, lanes_of(q)]


def first_back(
    geo, grads, dgeo, dx, dval, emb, slope, ev_w, rad_w, slots, group, span, before
):
    per = slots // group
    first = span[0] * per
    rows = HARM * TENSORS
    return pl.pallas_call(
        partial(first_back_kernel, group=group, per=per, norm=1.0 / math.sqrt(slots)),
        grid=((span[1] - span[0]) * per,),
        out_shape=jax.ShapeDtypeStruct((HARM + BASIS,) + geo.shape[1:], F32),
        in_specs=[row_spec(18, group, first)]
        + [unit_spec(rows, per)] * 3
        + [row_spec(HARM, group, first)]
        + [edge_spec(r, group, first) for r in (LATENT, TENSORS, TENSORS, LATENT)]
        + [WHOLE] * 2
        + [pl.BlockSpec(memory_space=pl.ANY)] * len(before),
        out_specs=row_spec(HARM + BASIS, group, first),
        scratch_shapes=[pltpu.VMEM((rows, UNIT), F32)],
        input_output_aliases={11 + n: n for n in range(len(before))},
        compiler_params=params(),
        cost_estimate=effort(64 * LATENT * LATENT * dx.shape[1]),
        name="first_back",
    )(geo, *grads, dgeo, dx, dval, emb, slope, ev_w, rad_w, *before)


def geometry_back_kernel(vec, dgeo, nbrs, wide_out, across_out, dvec, *, slots):
    rows_total = vec.shape[1]
    units = rows_total // slots
    for group in range(rows_total // 8):
        up = slice(group * 8, group * 8 + 8)
        vx, vy, vz = (vec[axis, up, :] for axis in range(3))
        inverse, cut, slope, sine, cosine = distances(vx, vy, vz)
        ux, uy, uz = vx * inverse, vy * inverse, vz * inverse
        _, h1, h2, h3, h4, h5, h6, h7, h8 = (dgeo[m, up, :] for m in range(HARM))
        dux = h1 + ROOT3 * (uy * h4 + uz * h7 + ux * h8)
        duy = h2 + ROOT3 * (ux * h4 + uz * h5 - uy * h8)
        duz = h3 + ROOT3 * (uy * h5 + ux * h7) + 3.0 * uz * h6
        along = ux * dux + uy * duy + uz * duz
        scale = math.sqrt(2.0 / CUTOFF) * inverse
        by_wave = jnp.zeros_like(sine)
        by_angle = jnp.zeros_like(sine)
        before, now = jnp.zeros_like(sine), sine
        before_c, now_c = jnp.ones_like(sine), cosine
        for n in range(BASIS):
            pulled = dgeo[HARM + n, up, :]
            by_wave = by_wave + pulled * now
            by_angle = by_angle + (n + 1.0) * (pulled * now_c)
            before, now = now, 2.0 * cosine * now - before
            before_c, now_c = now_c, 2.0 * cosine * now_c - before_c
        d_dist = slope * dgeo[0, up, :] + scale * (
            (math.pi / CUTOFF) * by_angle * cut + by_wave * (slope - inverse * cut)
        )
        dvec[0, up, :] = (dux - ux * along) * inverse + ux * d_dist
        dvec[1, up, :] = (duy - uy * along) * inverse + uy * d_dist
        dvec[2, up, :] = (duz - uz * along) * inverse + uz * d_dist
    total = jnp.zeros((2 * 48, UNIT), F32)
    rows = lax.broadcasted_iota(jnp.int32, (16, UNIT), 0)
    lane = lax.broadcasted_iota(jnp.int32, (UNIT, UNIT), 0)
    for group in range(rows_total // 4):
        spreads, picks = [], []
        for k in range(group * 4, group * 4 + 4):
            index = nbrs[k : k + 1, :]
            here = rows == lax.shift_right_arithmetic(index, 7)
            spreads.append(
                jnp.concatenate(
                    [jnp.where(here, dvec[axis, k : k + 1, :], 0.0) for axis in range(3)], 0
                )
            )
            picks.append((lane == (index & 127)).astype(F32).astype(BF16))
        spread = jnp.concatenate(spreads, 1)
        total = total + dot_nt(stacked(spread), jnp.concatenate(picks, 1))
    total = total[:48] + total[48:]
    wide_out[...] = jnp.zeros_like(wide_out)
    across_out[...] = jnp.zeros_like(across_out)
    for axis in range(3):
        for block in range(4 * units):
            row = axis * 16 + block
            out, place = (wide_out, block) if block < 3 * units else (across_out, block - 3 * units)
            out[axis : axis + 1, lanes_of(place)] = total[row : row + 1]
        for unit in range(units):
            part = dvec[axis, unit * slots : (unit + 1) * slots, :]
            wide_out[axis : axis + 1, lanes_of(unit)] -= jnp.sum(part, axis=0, keepdims=True)


def geometry_back(vec, dgeo, nbrs, slots):
    atoms = vec.shape[1] // slots * UNIT
    return pl.pallas_call(
        partial(geometry_back_kernel, slots=slots),
        out_shape=[edge_shape(8, 3 * atoms), edge_shape(8, atoms)],
        in_specs=[WHOLE] * 3,
        out_specs=[WHOLE] * 2,
        scratch_shapes=[pltpu.VMEM(vec.shape, F32)],
        compiler_params=params(),
        name="geometry_back",
    )(vec, dgeo, nbrs)


def swap_y(rows, face):
    if lax.axis_size("gy") == 2:
        return passed_along(rows, "gy", 1)
    up = passed_along(rows[:, :face], "gy", 1)
    down = passed_along(rows[:, face:], "gy", -1)
    return jnp.concatenate([up, down], 1)


def return_y(rows, face):
    if lax.axis_size("gy") == 2:
        return passed_along(rows, "gy", 1)
    up = passed_along(rows[:, :face], "gy", -1)
    down = passed_along(rows[:, face:], "gy", 1)
    return jnp.concatenate([up, down], 1)


def ghost_rows(parts, wanted, face):
    below, above = [], []
    for part in parts:
        if below:
            part, below[-1], above[-1] = lax.optimization_barrier((part, below[-1], above[-1]))
        below.append(passed_along(part, "gx", 1))
        above.append(passed_along(part, "gx", -1))
    pieces = [*parts, *below, *above]
    return pieces + [swap_y(lend_env(wanted, pieces), face)]


def owned_grads(wide, across, wanted, face, widths, total, steps):
    across, total = lax.optimization_barrier((across, total))
    returned = return_y(across, face)
    total = sum_step(total, steps)
    own, below, above = take_back(returned, wanted, wide, widths)
    below[0], above[0], total = lax.optimization_barrier((below[0], above[0], total))
    found = []
    for number in range(len(widths)):
        send = below[number], above[number]
        if found:
            send, found[-1] = lax.optimization_barrier((send, found[-1]))
        found.append(
            [own[number], passed_along(send[0], "gx", -1), passed_along(send[1], "gx", 1)]
        )
    return found, total


def sum_steps():
    count = lax.axis_size("gx")
    if count & (count - 1) or lax.axis_size("gy") != 2:
        return None
    return [("gx", 1 << n) for n in range(count.bit_length() - 1)] + [("gy", 1)]


def sum_step(total, steps):
    if steps:
        axis, by = steps.pop(0)
        total = total + passed_along(total, axis, by)
    return total


def per_device(
    positions,
    species,
    neighbours,
    send_x,
    send_y,
    two_weight,
    two_bias,
    env_weight,
    value_weight,
    latent_weight,
    latent_bias,
    out_weight,
    species_shift,
):
    group = 16
    nbrs = neighbours[0, 0]
    atoms = nbrs.shape[1]
    face = send_y.shape[3]
    rows = jnp.concatenate(
        [
            positions[0, 0],
            species[0, 0][None].astype(F32),
            send_x[0, 0].astype(F32),
            jnp.zeros((2, atoms), F32),
        ],
        0,
    )
    wanted = jnp.concatenate(
        [
            send_y[0, 0, 1],
            send_y[0, 0, 0],
            jnp.full((atoms - 2 * face,), -1, jnp.int32),
        ]
    )[None]
    below = passed_along(rows, "gx", 1)
    above = passed_along(rows, "gx", -1)
    two_w, mix_w, s_w, back_w, ev_w, rad_w, cols = prepare_weights(
        two_weight, two_bias, env_weight, value_weight, latent_weight, latent_bias, out_weight
    )
    lent, wanted = lend_rows(rows, below, above, wanted)
    across = swap_y(lent, face)
    slots = nbrs.shape[0]
    units = atoms // UNIT
    vec, geo, nbrs, base = geometry(rows, below, above, across, nbrs, species_shift, face)
    parts, before = [], []
    for span in ((0, 1), (1, units)):
        *before, part = first_pass(
            geo, rows, two_w, mix_w, cols, slots, group, span, before
        )
        parts.append(part)
    x0, slope_a, emb0, val0, lx0 = before
    pieces = ghost_rows(parts, wanted, face)
    parts, before = [], []
    for span in ((0, units - 1), (units - 1, units)):
        *before, part = middle_pass(
            geo, nbrs, pieces, x0, lx0, val0, s_w, mix_w, cols, slots, group, span, before
        )
        parts.append(part)
    g0, slope0, x1, emb1, val1, lx1 = before
    pieces = ghost_rows(parts, wanted, face)
    energy, total, dx, dval, dgeo, wide, across = last_pass(
        geo, nbrs, pieces, x1, lx1, val1, s_w, back_w, cols, base, slots, group
    )
    steps = sum_steps()
    if steps is None:
        total = lax.psum(total, ("gx", "gy"))
    grads, total = owned_grads(wide, across, wanted, face, (UNIT, atoms - UNIT), total, steps)
    before = []
    for number, span in enumerate(((0, 1), (1, units))):
        before = middle_back(
            geo, nbrs, grads[number], dgeo, dx, dval, emb1, g0, slope0, val0, ev_w, back_w,
            slots, group, span, before,
        )
    dx, dval, dgeo, wide, across = before
    grads, total = owned_grads(wide, across, wanted, face, (atoms - UNIT, UNIT), total, steps)
    before = []
    for number, span in enumerate(((0, units - 1), (units - 1, units))):
        before = [
            first_back(
                geo, grads[number], dgeo, dx, dval, emb0, slope_a, ev_w, rad_w, slots, group,
                span, before,
            )
        ]
    wide, across = geometry_back(vec, before[0], nbrs, slots)
    grads, total = owned_grads(wide, across, wanted, face, (atoms,), total, steps)
    while steps:
        total = sum_step(total, steps)
    mean_energy = jnp.sum(total) / (atoms * lax.axis_size("gx") * lax.axis_size("gy"))
    forces = -(grads[0][0] + grads[0][1] + grads[0][2])[:3]
    return (energy[None], forces[None, None], mean_energy.reshape(1))


def solution(mesh):
    placed = (
        P(("groups", "gx"), "gy", None, None),
        P(("groups", "gx"), "gy", None),
        P(("groups", "gx"), "gy", None, None),
        P(("groups", "gx"), "gy", None, None),
        P(("groups", "gx"), "gy", None, None),
        P(),
        P(),
        P(),
        P(),
        P(),
        P(),
        P(),
        P(),
    )
    return jax.shard_map(
        per_device,
        mesh=mesh,
        in_specs=placed,
        out_specs=(
            P(("groups", "gx"), "gy", None),
            P(("groups", "gx"), "gy", None, None),
            P("groups"),
        ),
        check_vma=False,
    )
```

```python
from functools import partial
import math

import jax
import jax.numpy as jnp
from jax import lax
from jax.experimental import pallas as pl
from jax.experimental.pallas import tpu as pltpu
from jax.sharding import PartitionSpec as P

BASIS = 8
SPECIES = 5
SITES_X = 2
SITES_Y = 16
CUTOFF = 2.5
LATENT = 128
TENSORS = 32
HARM = 9
UNIT = 128
ROOT3 = math.sqrt(3.0)
DEGREE = (0, 1, 1, 1, 2, 2, 2, 2, 2)
F32 = jnp.float32
BF16 = jnp.bfloat16
WHOLE = pl.BlockSpec(memory_space=pltpu.VMEM)
SCALARS = pl.BlockSpec(memory_space=pltpu.SMEM)


def params():
    return pltpu.CompilerParams(vmem_limit_bytes=60 << 20)


def passed_along(value, axis, by):
    count = lax.axis_size(axis)
    return lax.ppermute(value, axis, [(i, (i + by) % count) for i in range(count)])


def dot(a, b):
    return jnp.dot(a, b, preferred_element_type=F32)


def dot_nt(a, b):
    return lax.dot_general(a, b, (((1,), (1,)), ((), ())), preferred_element_type=F32)


def halves(value):
    high = value.astype(BF16)
    return high, (value - high.astype(F32)).astype(BF16)


def stacked(value):
    return jnp.concatenate(halves(value), 0)


def product(weights, value):
    rows = weights.shape[0] // 2
    both = dot(weights, stacked(value))
    return both[:rows] + both[rows:]


def rounded(value):
    high = value.astype(BF16).astype(F32)
    return high, value - high


def weights_kernel(two, bias, env, val, lat, lat_bias, out_w, *outs):
    two_out, mix_out, s_out, back_out, ev_out, rad_out, cols = outs

    def depth_stack(piece):
        high, low = rounded(piece)
        top = jnp.concatenate([high, high], 0)
        bottom = jnp.concatenate([low, jnp.zeros_like(low)], 0)
        return top.T, bottom.T

    def lane_stack(piece):
        high, low = rounded(piece)
        top = jnp.concatenate([high, high], 1)
        return top, jnp.concatenate([low, jnp.zeros_like(low)], 1)

    def join(pieces):
        tops, bottoms = zip(*pieces)
        return jnp.concatenate(list(tops) + list(bottoms), 0).astype(BF16)

    def wide_stack(piece):
        return jnp.concatenate(lane_stack(piece), 0).astype(BF16)

    width = two.shape[1]
    first = jnp.concatenate(
        [
            two[0:SPECIES, :],
            bias[...],
            jnp.zeros((2, width), F32),
            two[SPECIES : 2 * SPECIES, :],
            jnp.zeros((3, width), F32),
            two[2 * SPECIES :, :],
        ],
        0,
    )
    two_out[...] = join([depth_stack(first)])
    rad_out[...] = wide_stack(two[2 * SPECIES :, :])
    for layer in range(env.shape[0]):
        latent = lat[layer]
        mix_out[layer] = join(
            [lane_stack(env[layer]), lane_stack(val[layer]), depth_stack(latent[:width])]
        )
        s_out[layer] = join([depth_stack(latent[width:])])
        back_out[layer] = wide_stack(latent)
        high = [rounded(env[layer]), rounded(val[layer])]
        top = jnp.concatenate([high[0][0], high[1][0]] * 2, 0).T
        bottom = jnp.concatenate([high[0][1], high[1][1]] + [jnp.zeros_like(high[0][1])] * 2, 0).T
        ev_out[layer] = jnp.concatenate([top, bottom], 0).astype(BF16)
    columns = jnp.concatenate(
        [lat_bias[...], out_w[...], jnp.zeros((8 - lat_bias.shape[0] - 1, width), F32)], 0
    )
    cols[...] = columns.T


def prepare_weights(two, bias, env, val, lat, lat_bias, out_w):
    layers = env.shape[0]
    shapes = [
        (2 * LATENT, 48),
        (layers, 2 * (LATENT + 2 * TENSORS), 2 * LATENT),
        (layers, 2 * LATENT, 6 * TENSORS),
        (layers, 2 * (LATENT + 3 * TENSORS), 2 * LATENT),
        (layers, 2 * LATENT, 4 * TENSORS),
        (2 * BASIS, 2 * LATENT),
    ]
    out_shape = [jax.ShapeDtypeStruct(s, BF16) for s in shapes]
    out_shape.append(jax.ShapeDtypeStruct((LATENT, 8), F32))
    return pl.pallas_call(
        weights_kernel,
        out_shape=out_shape,
        in_specs=[WHOLE] * 7,
        out_specs=[WHOLE] * 7,
        compiler_params=params(),
        name="prepare_weights",
    )(two, bias[None], env.swapaxes(1, 2), val.swapaxes(1, 2), lat, lat_bias, out_w[None])


def shifted(rows, by_x, by_y):
    lane_row = lax.broadcasted_iota(jnp.int32, rows.shape, 0)
    return rows + jnp.where(lane_row == 0, by_x, jnp.where(lane_row == 1, by_y, 0.0))


def lane_pick(table, row, index, blocks):
    low = index & 127
    high = lax.shift_right_arithmetic(index, 7)
    found = jnp.zeros(index.shape, F32)
    for block in range(blocks):
        span = slice(block * 128, block * 128 + 128)
        source = table[...][:, span] if row is None else table[row : row + 1, span]
        source = jnp.broadcast_to(source, index.shape)
        taken = jnp.take_along_axis(source, low, axis=1)
        found = jnp.where(high == block, taken, found)
    return found


def fill_wide(own, below, above, table, remap):
    atoms = own.shape[1]
    table[:, 0:atoms] = own[...]
    table[:, atoms : 2 * atoms] = shifted(below[...], -float(SITES_X), 0.0)
    table[:, 2 * atoms : 3 * atoms] = shifted(above[...], float(SITES_X), 0.0)
    lanes = lax.broadcasted_iota(jnp.int32, (1, atoms), 1).astype(F32)
    remap[:, 0:atoms] = lanes
    remap[:, atoms : 2 * atoms] = below[5:6, :] + float(atoms)
    remap[:, 2 * atoms : 3 * atoms] = above[4:5, :] + float(2 * atoms)


def lend_kernel(own, below, above, wanted, rows_out, wanted_out, table, remap):
    atoms = own.shape[1]
    blocks = 3 * atoms // 128
    fill_wide(own, below, above, table, remap)
    for tile in range(wanted.shape[1] // 128):
        span = slice(tile * 128, tile * 128 + 128)
        index = jnp.broadcast_to(wanted[:, span], (8, 128))
        place = lane_pick(remap, 0, index, blocks).astype(jnp.int32)
        place = jnp.where(index < 0, -1, place)
        wanted_out[:, span] = place[0:1]
        rows_out[:, span] = lane_pick(table, None, place, blocks)


def pack_kernel(coords, species, lend_x, lend_y, rows, wanted):
    face = lend_y.shape[1]
    rows[...] = jnp.zeros_like(rows)
    rows[0:3, :] = coords[...]
    rows[3:4, :] = species[...].astype(F32)
    rows[4:6, :] = lend_x[...].astype(F32)
    wanted[...] = jnp.full(wanted.shape, -1, jnp.int32)
    wanted[:, 0:face] = lend_y[1:2, :]
    wanted[:, face : 2 * face] = lend_y[0:1, :]


def pack_rows(coords, species, lend_x, lend_y):
    atoms = coords.shape[1]
    return pl.pallas_call(
        pack_kernel,
        out_shape=[edge_shape(8, atoms), jax.ShapeDtypeStruct((1, atoms), jnp.int32)],
        in_specs=[WHOLE] * 4,
        out_specs=[WHOLE] * 2,
        compiler_params=params(),
        name="pack_rows",
    )(coords, species, lend_x, lend_y)


def lend_rows(own, below, above, wanted):
    atoms = own.shape[1]
    return pl.pallas_call(
        lend_kernel,
        out_shape=[
            jax.ShapeDtypeStruct(wanted.shape[:0] + (8, wanted.shape[1]), F32),
            jax.ShapeDtypeStruct(wanted.shape, jnp.int32),
        ],
        in_specs=[WHOLE] * 4,
        out_specs=[WHOLE] * 2,
        scratch_shapes=[pltpu.VMEM((8, 3 * atoms), F32), pltpu.VMEM((1, 3 * atoms), F32)],
        compiler_params=params(),
        name="lend_rows",
    )(own, below, above, wanted)


def distances(vx, vy, vz):
    dist = jnp.sqrt(vx * vx + vy * vy + vz * vz)
    inverse = 1.0 / dist
    scaled = jnp.minimum(dist * (1.0 / CUTOFF), 1.0)
    second = scaled * scaled
    fourth = second * second
    sixth = fourth * second
    cut = 1.0 - 28.0 * sixth + 48.0 * (sixth * scaled) - 21.0 * (sixth * second)
    rest = 1.0 - scaled
    slope = (-168.0 / CUTOFF) * (fourth * scaled) * (rest * rest)
    angle = scaled * math.pi
    return inverse, cut, slope, jnp.sin(angle), jnp.cos(angle)


def geometry_kernel(
    own, below, above, across, nbrs, shift, vec_out, geo_out, nbr_out, base_out, table, remap, face
):
    atoms = own.shape[1]
    slots = nbrs.shape[0]
    blocks = table.shape[1] // 128
    fill_wide(own, below, above, table, remap)
    lanes = lax.broadcasted_iota(jnp.int32, (8, atoms), 1)
    rows = lax.broadcasted_iota(jnp.int32, (8, atoms), 0)
    moved = across[...] + jnp.where(
        rows == 1, jnp.where(lanes < face, -float(SITES_Y), float(SITES_Y)), 0.0
    )
    empty = jnp.where(rows == 2, -1000.0, jnp.where(rows == 3, -1.0, 0.0))
    table[:, 3 * atoms : 4 * atoms] = jnp.where(lanes < 2 * face, moved, empty)
    remap[:, 3 * atoms : 4 * atoms] = (
        lax.broadcasted_iota(jnp.int32, (1, atoms), 1) + 3 * atoms
    ).astype(F32)
    base = jnp.zeros((1, atoms), F32)
    for kind in range(SPECIES):
        base = base + jnp.where(own[3:4, :] == float(kind), shift[kind], 0.0)
    base_out[...] = base
    for group in range(slots // 8):
        for tile in range(atoms // UNIT):
            span = slice(tile * UNIT, tile * UNIT + UNIT)
            index = nbrs[group * 8 : group * 8 + 8, span]
            up = slice(tile * slots + group * 8, tile * slots + group * 8 + 8)
            index = lane_pick(remap, 0, index, blocks).astype(jnp.int32)
            nbr_out[up, :] = index
            vx = lane_pick(table, 0, index, blocks) - own[0:1, span]
            vy = lane_pick(table, 1, index, blocks) - own[1:2, span]
            vz = lane_pick(table, 2, index, blocks) - own[2:3, span]
            kind = lane_pick(table, 3, index, blocks)
            vec_out[0, up, :] = vx
            vec_out[1, up, :] = vy
            vec_out[2, up, :] = vz
            inverse, cut, _, sine, cosine = distances(vx, vy, vz)
            ux, uy, uz = vx * inverse, vy * inverse, vz * inverse
            harm = [
                ux,
                uy,
                uz,
                ROOT3 * ux * uy,
                ROOT3 * uy * uz,
                0.5 * (3.0 * uz * uz - 1.0),
                ROOT3 * ux * uz,
                0.5 * ROOT3 * (ux * ux - uy * uy),
            ]
            geo_out[0, up, :] = cut
            for number, value in enumerate(harm):
                geo_out[1 + number, up, :] = value
            scale = math.sqrt(2.0 / CUTOFF) * inverse * cut
            before, now = jnp.zeros_like(sine), sine
            for number in range(BASIS):
                geo_out[9 + number, up, :] = now * scale
                before, now = now, 2.0 * cosine * now - before
            geo_out[17, up, :] = kind


def geometry(own, below, above, across, nbrs, shift, face):
    slots, atoms = nbrs.shape
    return pl.pallas_call(
        partial(geometry_kernel, face=face),
        out_shape=[
            jax.ShapeDtypeStruct((3, slots * atoms // UNIT, UNIT), F32),
            jax.ShapeDtypeStruct((18, slots * atoms // UNIT, UNIT), F32),
            jax.ShapeDtypeStruct((slots * atoms // UNIT, UNIT), jnp.int32),
            jax.ShapeDtypeStruct((1, atoms), F32),
        ],
        in_specs=[WHOLE] * 5 + [SCALARS],
        out_specs=[WHOLE] * 4,
        scratch_shapes=[pltpu.VMEM((8, 4 * atoms), F32), pltpu.VMEM((1, 4 * atoms), F32)],
        compiler_params=params(),
        name="geometry",
    )(own, below, above, across, nbrs, shift)


def silu_pair(pre):
    gate = 1.0 / (1.0 + jnp.exp(-pre))
    value = pre * gate
    return value, gate + value * (1.0 - gate)


def row_spec(count, group, first):
    return pl.BlockSpec((count, group, UNIT), lambda i: (0, first + i, 0))


def index_spec(group, first):
    return pl.BlockSpec((group, UNIT), lambda i: (first + i, 0))


def edge_spec(rows, group, first):
    return pl.BlockSpec((rows, group * UNIT), lambda i: (0, first + i))


def unit_spec(rows, per):
    return pl.BlockSpec((rows, UNIT), lambda i: (0, i // per))


def edge_shape(rows, edges):
    return jax.ShapeDtypeStruct((rows, edges), F32)


def lanes_of(q):
    return slice(q * UNIT, (q + 1) * UNIT)


def rows_of(m):
    return slice(m * TENSORS, (m + 1) * TENSORS)


def add_env(geo, step, per, group, embed, env_out, norm):
    @pl.when(step % per == 0)
    def _():
        env_out[...] = jnp.zeros_like(env_out)

    cuts = [geo[0, q : q + 1, :] * norm for q in range(group)]
    for m in range(HARM):
        total = env_out[rows_of(m), :]
        for q in range(group):
            factor = cuts[q] if m == 0 else cuts[q] * geo[m, q : q + 1, :]
            total = total + embed[:TENSORS, lanes_of(q)] * factor
        env_out[rows_of(m), :] = total


def first_kernel(
    geo, own, two_w, mix_w, cols, *outs, group, per, norm
):
    x_out, slope_out, emb_out, val_out, lx_out, env_out = outs[-6:]
    step = pl.program_id(0)
    kinds = lax.broadcasted_iota(jnp.int32, (8, UNIT), 0)
    kinds_f = kinds.astype(F32)
    centre = jnp.where((own[3:4, :] == kinds_f) & (kinds < SPECIES), 1.0, 0.0)
    centre = jnp.where(kinds == SPECIES, 1.0, centre)
    parts = []
    for q in range(group):
        other = jnp.where(geo[17, q : q + 1, :] == kinds_f, 1.0, 0.0)
        radial = [geo[9 + n, q : q + 1, :] for n in range(BASIS)]
        parts.append(jnp.concatenate([centre, other] + radial, 0))
    features = jnp.concatenate(parts, 1)
    x, slope = silu_pair(product(two_w[...], features))
    x_out[...] = x
    slope_out[...] = slope
    mixed = product(mix_w[0], x)
    emb_out[...] = mixed[:TENSORS]
    val_out[...] = mixed[TENSORS : 2 * TENSORS]
    lx_out[...] = mixed[2 * TENSORS :] + cols[:, 0:1]
    add_env(geo, step, per, group, mixed, env_out, norm)


def wide_unit_spec(rows, per, first):
    return pl.BlockSpec((rows, UNIT), lambda i: (0, first + i // per))


def first_pass(geo, own, two_w, mix_w, cols, slots, group, span, before):
    edges = geo.shape[1] * UNIT
    per = slots // group
    first = span[0] * per
    rows = (LATENT, LATENT, TENSORS, TENSORS, LATENT)
    return pl.pallas_call(
        partial(first_kernel, group=group, per=per, norm=1.0 / math.sqrt(slots)),
        grid=((span[1] - span[0]) * per,),
        out_shape=[edge_shape(r, edges) for r in rows]
        + [edge_shape(HARM * TENSORS, (span[1] - span[0]) * UNIT)],
        in_specs=[row_spec(18, group, first), wide_unit_spec(8, per, span[0])]
        + [WHOLE] * 3
        + [pl.BlockSpec(memory_space=pl.ANY)] * len(before),
        out_specs=[edge_spec(r, group, first) for r in rows]
        + [unit_spec(HARM * TENSORS, per)],
        input_output_aliases={5 + n: n for n in range(len(before))},
        compiler_params=params(),
        cost_estimate=effort(64 * LATENT * LATENT * edges),
        name="first_pass",
    )(geo, own, two_w, mix_w, cols, *before)


def chosen_rows(index, columns, start):
    rows = lax.broadcasted_iota(jnp.int32, (columns, index.shape[1]), 0) + start
    return (rows == index).astype(F32).astype(BF16)


def mark_atoms(nbrs, unit, columns):
    own = columns // 4
    centre = lax.broadcasted_iota(jnp.int32, (1, UNIT), 1) + unit * UNIT
    here = lax.broadcasted_iota(jnp.int32, (own, UNIT), 0)
    away = lax.broadcasted_iota(jnp.int32, (columns - own, UNIT), 0) + own
    parts = []
    for q in range(nbrs.shape[0]):
        index = nbrs[q : q + 1, :]
        top = (here == index).astype(F32) + (here == centre).astype(F32)
        rest = (away == index).astype(F32)
        parts.append(jnp.concatenate([top, rest], 0).astype(BF16))
    return jnp.concatenate(parts, 1)


def lend_env_kernel(wanted, *refs):
    out = refs[-1]
    rows = out.shape[0]
    total = jnp.zeros((2 * rows, out.shape[1]), F32)
    start = 0
    for block in refs[:-1]:
        chosen = chosen_rows(wanted[...], block.shape[1], start)
        total = total + dot(stacked(block[...]), chosen)
        start += block.shape[1]
    out[...] = total[:rows] + total[rows:]


def lend_env(wanted, pieces):
    return pl.pallas_call(
        lend_env_kernel,
        out_shape=jax.ShapeDtypeStruct((HARM * TENSORS, wanted.shape[1]), F32),
        in_specs=[WHOLE] * (1 + len(pieces)),
        out_specs=WHOLE,
        compiler_params=params(),
        name="lend_env",
    )(wanted, *pieces)


def take_back_kernel(returned, wanted, wide, *outs, widths):
    atoms = wide.shape[1] // 3
    rows = returned.shape[0]
    value = stacked(returned[...])
    for place in range(3):
        chosen = chosen_rows(wanted[...], atoms, place * atoms)
        both = dot_nt(value, chosen)
        total = wide[:, place * atoms : (place + 1) * atoms] + both[:rows] + both[rows:]
        start = 0
        for number, width in enumerate(widths):
            outs[place * len(widths) + number][...] = total[:, start : start + width]
            start += width


def take_back(returned, wanted, wide, widths):
    outs = pl.pallas_call(
        partial(take_back_kernel, widths=widths),
        out_shape=[edge_shape(wide.shape[0], w) for w in widths] * 3,
        in_specs=[WHOLE] * 3,
        out_specs=[WHOLE] * (3 * len(widths)),
        compiler_params=params(),
        name="take_back",
    )(returned, wanted, wide)
    count = len(widths)
    return [list(outs[place * count : (place + 1) * count]) for place in range(3)]


def fill_split(pieces, split):
    rows = pieces[0].shape[0]
    start = 0
    for block in pieces:
        span = slice(start, start + block.shape[1])
        high, low = halves(block[...])
        split[:rows, span] = high
        split[rows:, span] = low
        start += block.shape[1]


def gathered(split, chosen, g):
    rows = HARM * TENSORS
    both = dot(split[...], chosen)
    g[...] = both[:rows] + both[rows:]


def contracted(geo, group, g, value):
    columns = []
    for q in range(group):
        span = lanes_of(q)
        sums = [g[0:TENSORS, span], None, None]
        for m in range(1, HARM):
            term = g[rows_of(m), span] * geo[m, q : q + 1, :]
            d = DEGREE[m]
            sums[d] = term if sums[d] is None else sums[d] + term
        columns.append(jnp.concatenate([part * value[:, span] for part in sums], 0))
    return jnp.concatenate(columns, 1)


def middle_kernel(*refs, group, per, norm, count, aliased, first):
    geo, nbrs, x, lx, val, s_w, mix_w, cols = refs[:8]
    pieces = refs[8 : 8 + count]
    g, slope_out, x_out, emb_out, val_out, lx_out, env_out, split = refs[
        8 + count + aliased :
    ]
    step = pl.program_id(0)

    @pl.when(step == 0)
    def _():
        fill_split(pieces, split)

    chosen = mark_atoms(nbrs, first + step // per, split.shape[1])
    gathered(split, chosen, g)
    s = contracted(geo, group, g, val[...])
    update, slope = silu_pair(lx[...] + product(s_w[0], s))
    slope_out[...] = slope
    fresh = x[...] + update
    x_out[...] = fresh
    mixed = product(mix_w[1], fresh)
    emb_out[...] = mixed[:TENSORS]
    val_out[...] = mixed[TENSORS : 2 * TENSORS]
    lx_out[...] = mixed[2 * TENSORS :] + cols[:, 1:2]
    add_env(geo, step, per, group, mixed, env_out, norm)


def middle_pass(geo, nbrs, pieces, x, lx, val, s_w, mix_w, cols, slots, group, span, before):
    edges = x.shape[1]
    per = slots // group
    first = span[0] * per
    rows = (HARM * TENSORS, LATENT, LATENT, TENSORS, TENSORS, LATENT)
    ins = 8 + len(pieces)
    columns = sum(p.shape[1] for p in pieces)
    return pl.pallas_call(
        partial(
            middle_kernel, group=group, per=per, norm=1.0 / math.sqrt(slots),
            count=len(pieces), aliased=len(before), first=span[0],
        ),
        grid=((span[1] - span[0]) * per,),
        out_shape=[edge_shape(r, edges) for r in rows]
        + [edge_shape(HARM * TENSORS, (span[1] - span[0]) * UNIT)],
        in_specs=[row_spec(18, group, first), index_spec(group, first)]
        + [edge_spec(r, group, first) for r in (LATENT, LATENT, TENSORS)]
        + [WHOLE] * (3 + len(pieces))
        + [pl.BlockSpec(memory_space=pl.ANY)] * len(before),
        out_specs=[edge_spec(r, group, first) for r in rows]
        + [unit_spec(HARM * TENSORS, per)],
        scratch_shapes=[
            pltpu.VMEM((2 * HARM * TENSORS, columns), BF16),
        ],
        input_output_aliases={ins + n: n for n in range(len(before))},
        compiler_params=params(),
        cost_estimate=effort(8 * HARM * TENSORS * edges * edges // slots),
        name="middle_pass",
    )(geo, nbrs, x, lx, val, s_w, mix_w, cols, *pieces, *before)


def effort(flops):
    return pl.CostEstimate(flops=flops, transcendentals=0, bytes_accessed=flops // 512)


def pull_mixed(geo, group, g, value, ds, chosen, dgeo, wide, across, dg):
    columns = []
    for q in range(group):
        span = lanes_of(q)
        part = value[:, span]
        pulled = [ds[rows_of(d), span] for d in range(3)]
        scaled = [p * part for p in pulled]
        total = None
        for m in range(HARM):
            d = DEGREE[m]
            source = g[rows_of(m), span]
            if m == 0:
                total = source * pulled[0]
                grad = scaled[0]
            else:
                harm = geo[m, q : q + 1, :]
                total = total + source * pulled[d] * harm
                dgeo[m, q : q + 1, :] += jnp.sum(source * scaled[d], axis=0, keepdims=True)
                grad = scaled[d] * harm
            high, low = halves(grad)
            dg[rows_of(m), span] = high
            dg[rows_of(HARM + m), span] = low
        columns.append(total)
    both = dot_nt(dg[...], chosen)
    rows = HARM * TENSORS
    total = both[:rows] + both[rows:]
    wide[...] += total[:, : wide.shape[1]]
    across[...] += total[:, wide.shape[1] :]
    return jnp.concatenate(columns, 1)


def last_kernel(*refs, group, per, norm, count):
    geo, nbrs, x, lx, val, s_w, back_w, cols, base = refs[:9]
    pieces = refs[9 : 9 + count]
    energy, esum, dx_out, dval_out, dgeo, wide, across, split, g, dg = refs[9 + count :]
    step = pl.program_id(0)

    @pl.when(step == 0)
    def _():
        fill_split(pieces, split)
        wide[...] = jnp.zeros_like(wide)
        across[...] = jnp.zeros_like(across)
        esum[...] = jnp.zeros_like(esum)

    @pl.when(step % per == 0)
    def _():
        energy[...] = base[...]

    chosen = mark_atoms(nbrs, step // per, split.shape[1])
    gathered(split, chosen, g)
    value = val[...]
    s = contracted(geo, group, g, value)
    update, slope = silu_pair(lx[...] + product(s_w[1], s))
    fresh = x[...] + update
    weight = cols[:, 2:3]
    read = jnp.sum(fresh * weight, axis=0, keepdims=True) * norm
    cuts = []
    dgeo[...] = jnp.zeros_like(dgeo)
    for q in range(group):
        cut = geo[0, q : q + 1, :]
        cuts.append(cut)
        energy[...] += read[:, lanes_of(q)] * cut
        dgeo[0, q : q + 1, :] = read[:, lanes_of(q)]

    @pl.when(step % per == per - 1)
    def _():
        esum[0:1, :] += energy[...]

    d_fresh = weight * (jnp.concatenate(cuts, 1) * norm)
    pulled = product(back_w[1], d_fresh * slope)
    dx_out[...] = d_fresh + pulled[:LATENT]
    dval_out[...] = pull_mixed(
        geo, group, g, value, pulled[LATENT:], chosen, dgeo, wide, across, dg
    )


def last_pass(geo, nbrs, pieces, x, lx, val, s_w, back_w, cols, base, slots, group):
    edges = x.shape[1]
    per = slots // group
    rows = HARM * TENSORS
    columns = sum(p.shape[1] for p in pieces)
    return pl.pallas_call(
        partial(
            last_kernel, group=group, per=per, norm=1.0 / math.sqrt(slots), count=len(pieces)
        ),
        grid=(geo.shape[1] // group,),
        out_shape=[
            jax.ShapeDtypeStruct(base.shape, F32),
            edge_shape(8, UNIT),
            edge_shape(LATENT, edges),
            edge_shape(TENSORS, edges),
            jax.ShapeDtypeStruct((HARM,) + geo.shape[1:], F32),
            edge_shape(rows, columns - base.shape[1]),
            edge_shape(rows, base.shape[1]),
        ],
        in_specs=[row_spec(18, group, 0), index_spec(group, 0)]
        + [edge_spec(r, group, 0) for r in (LATENT, LATENT, TENSORS)]
        + [WHOLE] * 3
        + [unit_spec(1, per)]
        + [WHOLE] * len(pieces),
        out_specs=[
            unit_spec(1, per),
            WHOLE,
            edge_spec(LATENT, group, 0),
            edge_spec(TENSORS, group, 0),
            row_spec(HARM, group, 0),
            WHOLE,
            WHOLE,
        ],
        scratch_shapes=[
            pltpu.VMEM((2 * rows, columns), BF16),
            pltpu.VMEM((rows, group * UNIT), F32),
            pltpu.VMEM((2 * rows, group * UNIT), BF16),
        ],
        compiler_params=params(),
        cost_estimate=effort(16 * rows * edges * edges // slots),
        name="last_pass",
    )(geo, nbrs, x, lx, val, s_w, back_w, cols, base, *pieces)


def pull_env(geo, group, total, emb, dgeo, norm):
    columns = []
    for q in range(group):
        part = emb[:, lanes_of(q)]
        cut = geo[0, q : q + 1, :] * norm
        grad = None
        for m in range(HARM):
            source = total[rows_of(m), :]
            if m == 0:
                grad = source
            else:
                grad = grad + source * geo[m, q : q + 1, :]
                dgeo[m, q : q + 1, :] += cut * jnp.sum(source * part, axis=0, keepdims=True)
        dgeo[0, q : q + 1, :] += norm * jnp.sum(grad * part, axis=0, keepdims=True)
        columns.append(grad * cut)
    return jnp.concatenate(columns, 1)


def middle_back_kernel(*refs, group, per, norm, aliased, first):
    geo, nbrs, own, low, high, dgeo_in, dx, dval, emb, g, slope, val, ev_w, back_w = refs[:14]
    wide_in, across_in = refs[14:16] if aliased else (None, None)
    dx_out, dval_out, dgeo, wide, across, total, dg = refs[14 + aliased :]
    step = pl.program_id(0)

    @pl.when(step == 0)
    def _():
        wide[...] = wide_in[...] if aliased else jnp.zeros_like(wide)
        across[...] = across_in[...] if aliased else jnp.zeros_like(across)

    @pl.when(step % per == 0)
    def _():
        total[...] = own[...] + low[...] + high[...]

    chosen = mark_atoms(nbrs, first + step // per, wide.shape[1] + across.shape[1])
    dgeo[...] = dgeo_in[...]
    demb = pull_env(geo, group, total, emb, dgeo, norm)
    d_fresh = dx[...] + product(ev_w[1], jnp.concatenate([demb, dval[...]], 0))
    pulled = product(back_w[0], d_fresh * slope[...])
    dx_out[...] = d_fresh + pulled[:LATENT]
    dval_out[...] = pull_mixed(
        geo, group, g, val[...], pulled[LATENT:], chosen, dgeo, wide, across, dg
    )


def middle_back(
    geo, nbrs, grads, dgeo, dx, dval, emb, g, slope, val, ev_w, back_w, slots, group, span, before
):
    edges = dx.shape[1]
    per = slots // group
    first = span[0] * per
    rows = HARM * TENSORS
    atoms = geo.shape[1] // slots * UNIT
    aliased = len(before)
    shapes = [
        edge_shape(LATENT, edges),
        edge_shape(TENSORS, edges),
        jax.ShapeDtypeStruct((HARM,) + geo.shape[1:], F32),
        edge_shape(rows, 3 * atoms),
        edge_shape(rows, atoms),
    ]
    extra = [*before[3:], *before[:3]]
    return pl.pallas_call(
        partial(
            middle_back_kernel, group=group, per=per, norm=1.0 / math.sqrt(slots), aliased=aliased,
            first=span[0],
        ),
        grid=((span[1] - span[0]) * per,),
        out_shape=shapes,
        in_specs=[row_spec(18, group, first), index_spec(group, first)]
        + [unit_spec(rows, per)] * 3
        + [row_spec(HARM, group, first)]
        + [
            edge_spec(r, group, first)
            for r in (LATENT, TENSORS, TENSORS, rows, LATENT, TENSORS)
        ]
        + [WHOLE] * 2
        + ([WHOLE] * 2 + [pl.BlockSpec(memory_space=pl.ANY)] * 3 if before else []),
        out_specs=[
            edge_spec(LATENT, group, first),
            edge_spec(TENSORS, group, first),
            row_spec(HARM, group, first),
            WHOLE,
            WHOLE,
        ],
        scratch_shapes=[
            pltpu.VMEM((rows, UNIT), F32),
            pltpu.VMEM((2 * rows, group * UNIT), BF16),
        ],
        input_output_aliases={16 + n: n for n in range(3)} if before else {},
        compiler_params=params(),
        cost_estimate=effort(8 * rows * edges * edges // slots),
        name="middle_back",
    )(geo, nbrs, *grads, dgeo, dx, dval, emb, g, slope, val, ev_w, back_w, *extra)


def first_back_kernel(
    geo, own, low, high, dgeo_in, dx, dval, emb, slope, ev_w, rad_w, *rest, group, per, norm
):
    dgeo, total = rest[-2:]
    step = pl.program_id(0)

    @pl.when(step % per == 0)
    def _():
        total[...] = own[...] + low[...] + high[...]

    dgeo[0:HARM] = dgeo_in[...]
    demb = pull_env(geo, group, total, emb, dgeo, norm)
    d_fresh = dx[...] + product(ev_w[0], jnp.concatenate([demb, dval[...]], 0))
    radial = product(rad_w[...], d_fresh * slope[...])
    for q in range(group):
        for n in range(BASIS):
            dgeo[HARM + n, q : q + 1, :] = radial[n : n + 1, lanes_of(q)]


def first_back(
    geo, grads, dgeo, dx, dval, emb, slope, ev_w, rad_w, slots, group, span, before
):
    per = slots // group
    first = span[0] * per
    rows = HARM * TENSORS
    return pl.pallas_call(
        partial(first_back_kernel, group=group, per=per, norm=1.0 / math.sqrt(slots)),
        grid=((span[1] - span[0]) * per,),
        out_shape=jax.ShapeDtypeStruct((HARM + BASIS,) + geo.shape[1:], F32),
        in_specs=[row_spec(18, group, first)]
        + [unit_spec(rows, per)] * 3
        + [row_spec(HARM, group, first)]
        + [edge_spec(r, group, first) for r in (LATENT, TENSORS, TENSORS, LATENT)]
        + [WHOLE] * 2
        + [pl.BlockSpec(memory_space=pl.ANY)] * len(before),
        out_specs=row_spec(HARM + BASIS, group, first),
        scratch_shapes=[pltpu.VMEM((rows, UNIT), F32)],
        input_output_aliases={11 + n: n for n in range(len(before))},
        compiler_params=params(),
        cost_estimate=effort(64 * LATENT * LATENT * dx.shape[1]),
        name="first_back",
    )(geo, *grads, dgeo, dx, dval, emb, slope, ev_w, rad_w, *before)


def geometry_back_kernel(vec, dgeo, nbrs, wide_out, across_out, dvec, *, slots):
    rows_total = vec.shape[1]
    units = rows_total // slots
    for group in range(rows_total // 8):
        up = slice(group * 8, group * 8 + 8)
        vx, vy, vz = (vec[axis, up, :] for axis in range(3))
        inverse, cut, slope, sine, cosine = distances(vx, vy, vz)
        ux, uy, uz = vx * inverse, vy * inverse, vz * inverse
        _, h1, h2, h3, h4, h5, h6, h7, h8 = (dgeo[m, up, :] for m in range(HARM))
        dux = h1 + ROOT3 * (uy * h4 + uz * h7 + ux * h8)
        duy = h2 + ROOT3 * (ux * h4 + uz * h5 - uy * h8)
        duz = h3 + ROOT3 * (uy * h5 + ux * h7) + 3.0 * uz * h6
        along = ux * dux + uy * duy + uz * duz
        scale = math.sqrt(2.0 / CUTOFF) * inverse
        by_wave = jnp.zeros_like(sine)
        by_angle = jnp.zeros_like(sine)
        before, now = jnp.zeros_like(sine), sine
        before_c, now_c = jnp.ones_like(sine), cosine
        for n in range(BASIS):
            pulled = dgeo[HARM + n, up, :]
            by_wave = by_wave + pulled * now
            by_angle = by_angle + (n + 1.0) * (pulled * now_c)
            before, now = now, 2.0 * cosine * now - before
            before_c, now_c = now_c, 2.0 * cosine * now_c - before_c
        d_dist = slope * dgeo[0, up, :] + scale * (
            (math.pi / CUTOFF) * by_angle * cut + by_wave * (slope - inverse * cut)
        )
        dvec[0, up, :] = (dux - ux * along) * inverse + ux * d_dist
        dvec[1, up, :] = (duy - uy * along) * inverse + uy * d_dist
        dvec[2, up, :] = (duz - uz * along) * inverse + uz * d_dist
    total = jnp.zeros((2 * 48, UNIT), F32)
    rows = lax.broadcasted_iota(jnp.int32, (16, UNIT), 0)
    lane = lax.broadcasted_iota(jnp.int32, (UNIT, UNIT), 0)
    for group in range(rows_total // 4):
        spreads, picks = [], []
        for k in range(group * 4, group * 4 + 4):
            index = nbrs[k : k + 1, :]
            here = rows == lax.shift_right_arithmetic(index, 7)
            spreads.append(
                jnp.concatenate(
                    [jnp.where(here, dvec[axis, k : k + 1, :], 0.0) for axis in range(3)], 0
                )
            )
            picks.append((lane == (index & 127)).astype(F32).astype(BF16))
        spread = jnp.concatenate(spreads, 1)
        total = total + dot_nt(stacked(spread), jnp.concatenate(picks, 1))
    total = total[:48] + total[48:]
    wide_out[...] = jnp.zeros_like(wide_out)
    across_out[...] = jnp.zeros_like(across_out)
    for axis in range(3):
        for block in range(4 * units):
            row = axis * 16 + block
            out, place = (wide_out, block) if block < 3 * units else (across_out, block - 3 * units)
            out[axis : axis + 1, lanes_of(place)] = total[row : row + 1]
        for unit in range(units):
            part = dvec[axis, unit * slots : (unit + 1) * slots, :]
            wide_out[axis : axis + 1, lanes_of(unit)] -= jnp.sum(part, axis=0, keepdims=True)


def geometry_back(vec, dgeo, nbrs, slots):
    atoms = vec.shape[1] // slots * UNIT
    return pl.pallas_call(
        partial(geometry_back_kernel, slots=slots),
        out_shape=[edge_shape(8, 3 * atoms), edge_shape(8, atoms)],
        in_specs=[WHOLE] * 3,
        out_specs=[WHOLE] * 2,
        scratch_shapes=[pltpu.VMEM(vec.shape, F32)],
        compiler_params=params(),
        name="geometry_back",
    )(vec, dgeo, nbrs)


def swap_y(rows, face):
    if lax.axis_size("gy") == 2:
        return passed_along(rows, "gy", 1)
    up = passed_along(rows[:, :face], "gy", 1)
    down = passed_along(rows[:, face:], "gy", -1)
    return jnp.concatenate([up, down], 1)


def return_y(rows, face):
    if lax.axis_size("gy") == 2:
        return passed_along(rows, "gy", 1)
    up = passed_along(rows[:, :face], "gy", -1)
    down = passed_along(rows[:, face:], "gy", 1)
    return jnp.concatenate([up, down], 1)


def ghost_rows(parts, wanted, face):
    below, above = [], []
    for part in parts:
        if below:
            part, below[-1], above[-1] = lax.optimization_barrier((part, below[-1], above[-1]))
        below.append(passed_along(part, "gx", 1))
        above.append(passed_along(part, "gx", -1))
    pieces = [*parts, *below, *above]
    return pieces + [swap_y(lend_env(wanted, pieces), face)]


def owned_grads(wide, across, wanted, face, widths, total, steps, hops):
    across, total = lax.optimization_barrier((across, total))
    returned = return_y(across, face)
    for _ in range(hops):
        total = sum_step(total, steps)
    own, below, above = take_back(returned, wanted, wide, widths)
    found = []
    for number in range(len(widths)):
        send = below[number], above[number]
        if found:
            send, found[-1], total = lax.optimization_barrier((send, found[-1], total))
        found.append(
            [own[number], passed_along(send[0], "gx", -1), passed_along(send[1], "gx", 1)]
        )
    return found, total


def sum_steps():
    count = lax.axis_size("gx")
    if count & (count - 1) or lax.axis_size("gy") != 2:
        return None
    return [("gx", 1 << n) for n in range(count.bit_length() - 1)] + [("gy", 1)]


def sum_step(total, steps):
    if steps:
        axis, by = steps.pop(0)
        total = total + passed_along(total, axis, by)
    return total


def per_device(
    positions,
    species,
    neighbours,
    send_x,
    send_y,
    two_weight,
    two_bias,
    env_weight,
    value_weight,
    latent_weight,
    latent_bias,
    out_weight,
    species_shift,
):
    group = 16
    nbrs = neighbours[0, 0]
    atoms = nbrs.shape[1]
    face = send_y.shape[3]
    rows, wanted = pack_rows(positions[0, 0], species[0], send_x[0, 0], send_y[0, 0])
    below = passed_along(rows, "gx", 1)
    above = passed_along(rows, "gx", -1)
    two_w, mix_w, s_w, back_w, ev_w, rad_w, cols = prepare_weights(
        two_weight, two_bias, env_weight, value_weight, latent_weight, latent_bias, out_weight
    )
    lent, wanted = lend_rows(rows, below, above, wanted)
    across = swap_y(lent, face)
    slots = nbrs.shape[0]
    units = atoms // UNIT
    vec, geo, nbrs, base = geometry(rows, below, above, across, nbrs, species_shift, face)
    parts, before = [], []
    for span in ((0, 1), (1, units)):
        *before, part = first_pass(
            geo, rows, two_w, mix_w, cols, slots, group, span, before
        )
        parts.append(part)
    x0, slope_a, emb0, val0, lx0 = before
    pieces = ghost_rows(parts, wanted, face)
    parts, before = [], []
    for span in ((0, units - 1), (units - 1, units)):
        *before, part = middle_pass(
            geo, nbrs, pieces, x0, lx0, val0, s_w, mix_w, cols, slots, group, span, before
        )
        parts.append(part)
    g0, slope0, x1, emb1, val1, lx1 = before
    pieces = ghost_rows(parts, wanted, face)
    energy, total, dx, dval, dgeo, wide, across = last_pass(
        geo, nbrs, pieces, x1, lx1, val1, s_w, back_w, cols, base, slots, group
    )
    steps = sum_steps()
    if steps is None:
        total = lax.psum(total, ("gx", "gy"))
    grads, total = owned_grads(wide, across, wanted, face, (UNIT, atoms - UNIT), total, steps, 1)
    before = []
    for number, span in enumerate(((0, 1), (1, units))):
        before = middle_back(
            geo, nbrs, grads[number], dgeo, dx, dval, emb1, g0, slope0, val0, ev_w, back_w,
            slots, group, span, before,
        )
    dx, dval, dgeo, wide, across = before
    grads, total = owned_grads(wide, across, wanted, face, (atoms - UNIT, UNIT), total, steps, 2)
    before = []
    for number, span in enumerate(((0, units - 1), (units - 1, units))):
        before = [
            first_back(
                geo, grads[number], dgeo, dx, dval, emb0, slope_a, ev_w, rad_w, slots, group,
                span, before,
            )
        ]
    wide, across = geometry_back(vec, before[0], nbrs, slots)
    grads, total = owned_grads(wide, across, wanted, face, (atoms,), total, steps, 1)
    while steps:
        total = sum_step(total, steps)
    mean_energy = jnp.sum(total) / (atoms * lax.axis_size("gx") * lax.axis_size("gy"))
    forces = -(grads[0][0] + grads[0][1] + grads[0][2])[:3]
    return (energy[None], forces[None, None], mean_energy.reshape(1))


def solution(mesh):
    placed = (
        P(("groups", "gx"), "gy", None, None),
        P(("groups", "gx"), "gy", None),
        P(("groups", "gx"), "gy", None, None),
        P(("groups", "gx"), "gy", None, None),
        P(("groups", "gx"), "gy", None, None),
        P(),
        P(),
        P(),
        P(),
        P(),
        P(),
        P(),
        P(),
    )
    return jax.shard_map(
        per_device,
        mesh=mesh,
        in_specs=placed,
        out_specs=(
            P(("groups", "gx"), "gy", None),
            P(("groups", "gx"), "gy", None, None),
            P("groups"),
        ),
        check_vma=False,
    )
```

```python
from functools import partial
import math

import jax
import jax.numpy as jnp
from jax import lax
from jax.experimental import pallas as pl
from jax.experimental.pallas import tpu as pltpu
from jax.sharding import PartitionSpec as P

BASIS = 8
SPECIES = 5
SITES_X = 2
SITES_Y = 16
CUTOFF = 2.5
LATENT = 128
TENSORS = 32
HARM = 9
UNIT = 128
ROOT3 = math.sqrt(3.0)
DEGREE = (0, 1, 1, 1, 2, 2, 2, 2, 2)
F32 = jnp.float32
BF16 = jnp.bfloat16
WHOLE = pl.BlockSpec(memory_space=pltpu.VMEM)
SCALARS = pl.BlockSpec(memory_space=pltpu.SMEM)


def params():
    return pltpu.CompilerParams(vmem_limit_bytes=44 << 20)


def passed_along(value, axis, by):
    count = lax.axis_size(axis)
    return lax.ppermute(value, axis, [(i, (i + by) % count) for i in range(count)])


def dot(a, b):
    return jnp.dot(a, b, preferred_element_type=F32)


def dot_nt(a, b):
    return lax.dot_general(a, b, (((1,), (1,)), ((), ())), preferred_element_type=F32)


def halves(value):
    high = value.astype(BF16)
    return high, (value - high.astype(F32)).astype(BF16)


def stacked(value):
    return jnp.concatenate(halves(value), 0)


def product(weights, value):
    rows = weights.shape[0] // 2
    both = dot(weights, stacked(value))
    return both[:rows] + both[rows:]


def rounded(value):
    high = value.astype(BF16).astype(F32)
    return high, value - high


def weights_kernel(two, bias, env, val, lat, lat_bias, out_w, *outs):
    two_out, mix_out, s_out, back_out, ev_out, rad_out, cols = outs

    def depth_stack(piece):
        high, low = rounded(piece)
        top = jnp.concatenate([high, high], 0)
        bottom = jnp.concatenate([low, jnp.zeros_like(low)], 0)
        return top.T, bottom.T

    def lane_stack(piece):
        high, low = rounded(piece)
        top = jnp.concatenate([high, high], 1)
        return top, jnp.concatenate([low, jnp.zeros_like(low)], 1)

    def join(pieces):
        tops, bottoms = zip(*pieces)
        return jnp.concatenate(list(tops) + list(bottoms), 0).astype(BF16)

    def wide_stack(piece):
        return jnp.concatenate(lane_stack(piece), 0).astype(BF16)

    width = two.shape[1]
    first = jnp.concatenate(
        [
            two[0:SPECIES, :],
            bias[...],
            jnp.zeros((2, width), F32),
            two[SPECIES : 2 * SPECIES, :],
            jnp.zeros((3, width), F32),
            two[2 * SPECIES :, :],
        ],
        0,
    )
    two_out[...] = join([depth_stack(first)])
    rad_out[...] = wide_stack(two[2 * SPECIES :, :])
    for layer in range(env.shape[0]):
        latent = lat[layer]
        mix_out[layer] = join(
            [lane_stack(env[layer]), lane_stack(val[layer]), depth_stack(latent[:width])]
        )
        s_out[layer] = join([depth_stack(latent[width:])])
        back_out[layer] = wide_stack(latent)
        high = [rounded(env[layer]), rounded(val[layer])]
        top = jnp.concatenate([high[0][0], high[1][0]] * 2, 0).T
        bottom = jnp.concatenate([high[0][1], high[1][1]] + [jnp.zeros_like(high[0][1])] * 2, 0).T
        ev_out[layer] = jnp.concatenate([top, bottom], 0).astype(BF16)
    columns = jnp.concatenate(
        [lat_bias[...], out_w[...], jnp.zeros((8 - lat_bias.shape[0] - 1, width), F32)], 0
    )
    cols[...] = columns.T


def prepare_weights(two, bias, env, val, lat, lat_bias, out_w):
    layers = env.shape[0]
    shapes = [
        (2 * LATENT, 48),
        (layers, 2 * (LATENT + 2 * TENSORS), 2 * LATENT),
        (layers, 2 * LATENT, 6 * TENSORS),
        (layers, 2 * (LATENT + 3 * TENSORS), 2 * LATENT),
        (layers, 2 * LATENT, 4 * TENSORS),
        (2 * BASIS, 2 * LATENT),
    ]
    out_shape = [jax.ShapeDtypeStruct(s, BF16) for s in shapes]
    out_shape.append(jax.ShapeDtypeStruct((LATENT, 8), F32))
    return pl.pallas_call(
        weights_kernel,
        out_shape=out_shape,
        in_specs=[WHOLE] * 7,
        out_specs=[WHOLE] * 7,
        compiler_params=params(),
        name="prepare_weights",
    )(two, bias[None], env.swapaxes(1, 2), val.swapaxes(1, 2), lat, lat_bias, out_w[None])


def shifted(rows, by_x, by_y):
    lane_row = lax.broadcasted_iota(jnp.int32, rows.shape, 0)
    return rows + jnp.where(lane_row == 0, by_x, jnp.where(lane_row == 1, by_y, 0.0))


def lane_pick(table, row, index, blocks):
    low = index & 127
    high = lax.shift_right_arithmetic(index, 7)
    found = jnp.zeros(index.shape, F32)
    for block in range(blocks):
        span = slice(block * 128, block * 128 + 128)
        source = table[...][:, span] if row is None else table[row : row + 1, span]
        source = jnp.broadcast_to(source, index.shape)
        taken = jnp.take_along_axis(source, low, axis=1)
        found = jnp.where(high == block, taken, found)
    return found


def fill_wide(own, below, above, table, remap):
    atoms = own.shape[1]
    table[:, 0:atoms] = own[...]
    table[:, atoms : 2 * atoms] = shifted(below[...], -float(SITES_X), 0.0)
    table[:, 2 * atoms : 3 * atoms] = shifted(above[...], float(SITES_X), 0.0)
    lanes = lax.broadcasted_iota(jnp.int32, (1, atoms), 1).astype(F32)
    remap[:, 0:atoms] = lanes
    remap[:, atoms : 2 * atoms] = below[5:6, :] + float(atoms)
    remap[:, 2 * atoms : 3 * atoms] = above[4:5, :] + float(2 * atoms)


def lend_kernel(own, below, above, wanted, rows_out, wanted_out, table, remap):
    atoms = own.shape[1]
    blocks = 3 * atoms // 128
    fill_wide(own, below, above, table, remap)
    for tile in range(wanted.shape[1] // 128):
        span = slice(tile * 128, tile * 128 + 128)
        index = jnp.broadcast_to(wanted[:, span], (8, 128))
        place = lane_pick(remap, 0, index, blocks).astype(jnp.int32)
        place = jnp.where(index < 0, -1, place)
        wanted_out[:, span] = place[0:1]
        rows_out[:, span] = lane_pick(table, None, place, blocks)


def pack_kernel(coords, species, lend_x, lend_y, rows, wanted):
    face = lend_y.shape[1]
    rows[...] = jnp.zeros_like(rows)
    rows[0:3, :] = coords[...]
    rows[3:4, :] = species[...].astype(F32)
    rows[4:6, :] = lend_x[...].astype(F32)
    wanted[...] = jnp.full(wanted.shape, -1, jnp.int32)
    wanted[:, 0:face] = lend_y[1:2, :]
    wanted[:, face : 2 * face] = lend_y[0:1, :]


def pack_rows(coords, species, lend_x, lend_y):
    atoms = coords.shape[1]
    return pl.pallas_call(
        pack_kernel,
        out_shape=[edge_shape(8, atoms), jax.ShapeDtypeStruct((1, atoms), jnp.int32)],
        in_specs=[WHOLE] * 4,
        out_specs=[WHOLE] * 2,
        compiler_params=params(),
        name="pack_rows",
    )(coords, species, lend_x, lend_y)


def lend_rows(own, below, above, wanted):
    atoms = own.shape[1]
    return pl.pallas_call(
        lend_kernel,
        out_shape=[
            jax.ShapeDtypeStruct(wanted.shape[:0] + (8, wanted.shape[1]), F32),
            jax.ShapeDtypeStruct(wanted.shape, jnp.int32),
        ],
        in_specs=[WHOLE] * 4,
        out_specs=[WHOLE] * 2,
        scratch_shapes=[pltpu.VMEM((8, 3 * atoms), F32), pltpu.VMEM((1, 3 * atoms), F32)],
        compiler_params=params(),
        name="lend_rows",
    )(own, below, above, wanted)


def distances(vx, vy, vz):
    dist = jnp.sqrt(vx * vx + vy * vy + vz * vz)
    inverse = 1.0 / dist
    scaled = jnp.minimum(dist * (1.0 / CUTOFF), 1.0)
    second = scaled * scaled
    fourth = second * second
    sixth = fourth * second
    cut = 1.0 - 28.0 * sixth + 48.0 * (sixth * scaled) - 21.0 * (sixth * second)
    rest = 1.0 - scaled
    slope = (-168.0 / CUTOFF) * (fourth * scaled) * (rest * rest)
    angle = scaled * math.pi
    return inverse, cut, slope, jnp.sin(angle), jnp.cos(angle)


def geometry_kernel(
    own, below, above, across, nbrs, shift, vec_out, geo_out, nbr_out, base_out, table, remap, face
):
    atoms = own.shape[1]
    slots = nbrs.shape[0]
    blocks = table.shape[1] // 128
    fill_wide(own, below, above, table, remap)
    lanes = lax.broadcasted_iota(jnp.int32, (8, atoms), 1)
    rows = lax.broadcasted_iota(jnp.int32, (8, atoms), 0)
    moved = across[...] + jnp.where(
        rows == 1, jnp.where(lanes < face, -float(SITES_Y), float(SITES_Y)), 0.0
    )
    empty = jnp.where(rows == 2, -1000.0, jnp.where(rows == 3, -1.0, 0.0))
    table[:, 3 * atoms : 4 * atoms] = jnp.where(lanes < 2 * face, moved, empty)
    remap[:, 3 * atoms : 4 * atoms] = (
        lax.broadcasted_iota(jnp.int32, (1, atoms), 1) + 3 * atoms
    ).astype(F32)
    base = jnp.zeros((1, atoms), F32)
    for kind in range(SPECIES):
        base = base + jnp.where(own[3:4, :] == float(kind), shift[kind], 0.0)
    base_out[...] = base
    for group in range(slots // 8):
        for tile in range(atoms // UNIT):
            span = slice(tile * UNIT, tile * UNIT + UNIT)
            index = nbrs[group * 8 : group * 8 + 8, span]
            up = slice(tile * slots + group * 8, tile * slots + group * 8 + 8)
            index = lane_pick(remap, 0, index, blocks).astype(jnp.int32)
            nbr_out[up, :] = index
            vx = lane_pick(table, 0, index, blocks) - own[0:1, span]
            vy = lane_pick(table, 1, index, blocks) - own[1:2, span]
            vz = lane_pick(table, 2, index, blocks) - own[2:3, span]
            kind = lane_pick(table, 3, index, blocks)
            vec_out[0, up, :] = vx
            vec_out[1, up, :] = vy
            vec_out[2, up, :] = vz
            inverse, cut, _, sine, cosine = distances(vx, vy, vz)
            ux, uy, uz = vx * inverse, vy * inverse, vz * inverse
            harm = [
                ux,
                uy,
                uz,
                ROOT3 * ux * uy,
                ROOT3 * uy * uz,
                0.5 * (3.0 * uz * uz - 1.0),
                ROOT3 * ux * uz,
                0.5 * ROOT3 * (ux * ux - uy * uy),
            ]
            geo_out[0, up, :] = cut
            for number, value in enumerate(harm):
                geo_out[1 + number, up, :] = value
            scale = math.sqrt(2.0 / CUTOFF) * inverse * cut
            before, now = jnp.zeros_like(sine), sine
            for number in range(BASIS):
                geo_out[9 + number, up, :] = now * scale
                before, now = now, 2.0 * cosine * now - before
            geo_out[17, up, :] = kind


def geometry(own, below, above, across, nbrs, shift, face):
    slots, atoms = nbrs.shape
    return pl.pallas_call(
        partial(geometry_kernel, face=face),
        out_shape=[
            jax.ShapeDtypeStruct((3, slots * atoms // UNIT, UNIT), F32),
            jax.ShapeDtypeStruct((18, slots * atoms // UNIT, UNIT), F32),
            jax.ShapeDtypeStruct((slots * atoms // UNIT, UNIT), jnp.int32),
            jax.ShapeDtypeStruct((1, atoms), F32),
        ],
        in_specs=[WHOLE] * 5 + [SCALARS],
        out_specs=[WHOLE] * 4,
        scratch_shapes=[pltpu.VMEM((8, 4 * atoms), F32), pltpu.VMEM((1, 4 * atoms), F32)],
        compiler_params=params(),
        name="geometry",
    )(own, below, above, across, nbrs, shift)


def silu_pair(pre):
    gate = 1.0 / (1.0 + jnp.exp(-pre))
    value = pre * gate
    return value, gate + value * (1.0 - gate)


def row_spec(count, group, first):
    return pl.BlockSpec((count, group, UNIT), lambda i: (0, first + i, 0))


def index_spec(group, first):
    return pl.BlockSpec((group, UNIT), lambda i: (first + i, 0))


def edge_spec(rows, group, first):
    return pl.BlockSpec((rows, group * UNIT), lambda i: (0, first + i))


def unit_spec(rows, per):
    return pl.BlockSpec((rows, UNIT), lambda i: (0, i // per))


def edge_shape(rows, edges):
    return jax.ShapeDtypeStruct((rows, edges), F32)


def lanes_of(q):
    return slice(q * UNIT, (q + 1) * UNIT)


def rows_of(m):
    return slice(m * TENSORS, (m + 1) * TENSORS)


def add_env(geo, step, per, group, embed, env_out, norm):
    @pl.when(step % per == 0)
    def _():
        env_out[...] = jnp.zeros_like(env_out)

    cuts = [geo[0, q : q + 1, :] * norm for q in range(group)]
    for m in range(HARM):
        total = env_out[rows_of(m), :]
        for q in range(group):
            factor = cuts[q] if m == 0 else cuts[q] * geo[m, q : q + 1, :]
            total = total + embed[:TENSORS, lanes_of(q)] * factor
        env_out[rows_of(m), :] = total


def first_kernel(
    geo, own, two_w, mix_w, cols, *outs, group, per, norm
):
    x_out, slope_out, emb_out, val_out, lx_out, env_out = outs[-6:]
    step = pl.program_id(0)
    kinds = lax.broadcasted_iota(jnp.int32, (8, UNIT), 0)
    kinds_f = kinds.astype(F32)
    centre = jnp.where((own[3:4, :] == kinds_f) & (kinds < SPECIES), 1.0, 0.0)
    centre = jnp.where(kinds == SPECIES, 1.0, centre)
    parts = []
    for q in range(group):
        other = jnp.where(geo[17, q : q + 1, :] == kinds_f, 1.0, 0.0)
        radial = [geo[9 + n, q : q + 1, :] for n in range(BASIS)]
        parts.append(jnp.concatenate([centre, other] + radial, 0))
    features = jnp.concatenate(parts, 1)
    x, slope = silu_pair(product(two_w[...], features))
    x_out[...] = x
    slope_out[...] = slope
    mixed = product(mix_w[0], x)
    emb_out[...] = mixed[:TENSORS]
    val_out[...] = mixed[TENSORS : 2 * TENSORS]
    lx_out[...] = mixed[2 * TENSORS :] + cols[:, 0:1]
    add_env(geo, step, per, group, mixed, env_out, norm)


def wide_unit_spec(rows, per, first):
    return pl.BlockSpec((rows, UNIT), lambda i: (0, first + i // per))


def first_pass(geo, own, two_w, mix_w, cols, slots, group, span, before):
    edges = geo.shape[1] * UNIT
    per = slots // group
    first = span[0] * per
    rows = (LATENT, LATENT, TENSORS, TENSORS, LATENT)
    return pl.pallas_call(
        partial(first_kernel, group=group, per=per, norm=1.0 / math.sqrt(slots)),
        grid=((span[1] - span[0]) * per,),
        out_shape=[edge_shape(r, edges) for r in rows]
        + [edge_shape(HARM * TENSORS, (span[1] - span[0]) * UNIT)],
        in_specs=[row_spec(18, group, first), wide_unit_spec(8, per, span[0])]
        + [WHOLE] * 3
        + [pl.BlockSpec(memory_space=pl.ANY)] * len(before),
        out_specs=[edge_spec(r, group, first) for r in rows]
        + [unit_spec(HARM * TENSORS, per)],
        input_output_aliases={5 + n: n for n in range(len(before))},
        compiler_params=params(),
        cost_estimate=effort(64 * LATENT * LATENT * edges),
        name="first_pass",
    )(geo, own, two_w, mix_w, cols, *before)


def chosen_rows(index, columns, start):
    rows = lax.broadcasted_iota(jnp.int32, (columns, index.shape[1]), 0) + start
    return (rows == index).astype(F32).astype(BF16)


def mark_atoms(nbrs, unit, columns):
    own = columns // 4
    centre = lax.broadcasted_iota(jnp.int32, (1, UNIT), 1) + unit * UNIT
    here = lax.broadcasted_iota(jnp.int32, (own, UNIT), 0)
    away = lax.broadcasted_iota(jnp.int32, (columns - own, UNIT), 0) + own
    parts = []
    for q in range(nbrs.shape[0]):
        index = nbrs[q : q + 1, :]
        top = (here == index).astype(F32) + (here == centre).astype(F32)
        rest = (away == index).astype(F32)
        parts.append(jnp.concatenate([top, rest], 0).astype(BF16))
    return jnp.concatenate(parts, 1)


def lend_env_kernel(wanted, *refs):
    out = refs[-1]
    rows = out.shape[0]
    total = jnp.zeros((2 * rows, out.shape[1]), F32)
    start = 0
    for block in refs[:-1]:
        chosen = chosen_rows(wanted[...], block.shape[1], start)
        total = total + dot(stacked(block[...]), chosen)
        start += block.shape[1]
    out[...] = total[:rows] + total[rows:]


def lend_env(wanted, pieces):
    return pl.pallas_call(
        lend_env_kernel,
        out_shape=jax.ShapeDtypeStruct((HARM * TENSORS, wanted.shape[1]), F32),
        in_specs=[WHOLE] * (1 + len(pieces)),
        out_specs=WHOLE,
        compiler_params=params(),
        name="lend_env",
    )(wanted, *pieces)


def take_back_kernel(returned, wanted, wide, *outs, widths):
    atoms = wide.shape[1] // 3
    rows = returned.shape[0]
    value = stacked(returned[...])
    for place in range(3):
        chosen = chosen_rows(wanted[...], atoms, place * atoms)
        both = dot_nt(value, chosen)
        total = wide[:, place * atoms : (place + 1) * atoms] + both[:rows] + both[rows:]
        start = 0
        for number, width in enumerate(widths):
            outs[place * len(widths) + number][...] = total[:, start : start + width]
            start += width


def take_back(returned, wanted, wide, widths):
    outs = pl.pallas_call(
        partial(take_back_kernel, widths=widths),
        out_shape=[edge_shape(wide.shape[0], w) for w in widths] * 3,
        in_specs=[WHOLE] * 3,
        out_specs=[WHOLE] * (3 * len(widths)),
        compiler_params=params(),
        name="take_back",
    )(returned, wanted, wide)
    count = len(widths)
    return [list(outs[place * count : (place + 1) * count]) for place in range(3)]


def fill_split(pieces, split):
    rows = pieces[0].shape[0]
    start = 0
    for block in pieces:
        span = slice(start, start + block.shape[1])
        high, low = halves(block[...])
        split[:rows, span] = high
        split[rows:, span] = low
        start += block.shape[1]


def gathered(split, chosen, g):
    rows = HARM * TENSORS
    both = dot(split[...], chosen)
    g[...] = both[:rows] + both[rows:]


def contracted(geo, group, g, value):
    columns = []
    for q in range(group):
        span = lanes_of(q)
        sums = [g[0:TENSORS, span], None, None]
        for m in range(1, HARM):
            term = g[rows_of(m), span] * geo[m, q : q + 1, :]
            d = DEGREE[m]
            sums[d] = term if sums[d] is None else sums[d] + term
        columns.append(jnp.concatenate([part * value[:, span] for part in sums], 0))
    return jnp.concatenate(columns, 1)


def middle_kernel(*refs, group, per, norm, count, aliased, first):
    geo, nbrs, x, lx, val, s_w, mix_w, cols = refs[:8]
    pieces = refs[8 : 8 + count]
    g, slope_out, x_out, emb_out, val_out, lx_out, env_out, split = refs[
        8 + count + aliased :
    ]
    step = pl.program_id(0)

    @pl.when(step == 0)
    def _():
        fill_split(pieces, split)

    chosen = mark_atoms(nbrs, first + step // per, split.shape[1])
    gathered(split, chosen, g)
    s = contracted(geo, group, g, val[...])
    update, slope = silu_pair(lx[...] + product(s_w[0], s))
    slope_out[...] = slope
    fresh = x[...] + update
    x_out[...] = fresh
    mixed = product(mix_w[1], fresh)
    emb_out[...] = mixed[:TENSORS]
    val_out[...] = mixed[TENSORS : 2 * TENSORS]
    lx_out[...] = mixed[2 * TENSORS :] + cols[:, 1:2]
    add_env(geo, step, per, group, mixed, env_out, norm)


def middle_pass(geo, nbrs, pieces, x, lx, val, s_w, mix_w, cols, slots, group, span, before):
    edges = x.shape[1]
    per = slots // group
    first = span[0] * per
    rows = (HARM * TENSORS, LATENT, LATENT, TENSORS, TENSORS, LATENT)
    ins = 8 + len(pieces)
    columns = sum(p.shape[1] for p in pieces)
    return pl.pallas_call(
        partial(
            middle_kernel, group=group, per=per, norm=1.0 / math.sqrt(slots),
            count=len(pieces), aliased=len(before), first=span[0],
        ),
        grid=((span[1] - span[0]) * per,),
        out_shape=[edge_shape(r, edges) for r in rows]
        + [edge_shape(HARM * TENSORS, (span[1] - span[0]) * UNIT)],
        in_specs=[row_spec(18, group, first), index_spec(group, first)]
        + [edge_spec(r, group, first) for r in (LATENT, LATENT, TENSORS)]
        + [WHOLE] * (3 + len(pieces))
        + [pl.BlockSpec(memory_space=pl.ANY)] * len(before),
        out_specs=[edge_spec(r, group, first) for r in rows]
        + [unit_spec(HARM * TENSORS, per)],
        scratch_shapes=[
            pltpu.VMEM((2 * HARM * TENSORS, columns), BF16),
        ],
        input_output_aliases={ins + n: n for n in range(len(before))},
        compiler_params=params(),
        cost_estimate=effort(8 * HARM * TENSORS * edges * edges // slots),
        name="middle_pass",
    )(geo, nbrs, x, lx, val, s_w, mix_w, cols, *pieces, *before)


def effort(flops):
    return pl.CostEstimate(flops=flops, transcendentals=0, bytes_accessed=flops // 512)


def pull_mixed(geo, group, g, value, ds, chosen, dgeo, wide, across, dg):
    columns = []
    for q in range(group):
        span = lanes_of(q)
        part = value[:, span]
        pulled = [ds[rows_of(d), span] for d in range(3)]
        scaled = [p * part for p in pulled]
        total = None
        for m in range(HARM):
            d = DEGREE[m]
            source = g[rows_of(m), span]
            if m == 0:
                total = source * pulled[0]
                grad = scaled[0]
            else:
                harm = geo[m, q : q + 1, :]
                total = total + source * pulled[d] * harm
                dgeo[m, q : q + 1, :] += jnp.sum(source * scaled[d], axis=0, keepdims=True)
                grad = scaled[d] * harm
            high, low = halves(grad)
            dg[rows_of(m), span] = high
            dg[rows_of(HARM + m), span] = low
        columns.append(total)
    both = dot_nt(dg[...], chosen)
    rows = HARM * TENSORS
    total = both[:rows] + both[rows:]
    wide[...] += total[:, : wide.shape[1]]
    across[...] += total[:, wide.shape[1] :]
    return jnp.concatenate(columns, 1)


def last_kernel(*refs, group, per, norm, count):
    geo, nbrs, x, lx, val, s_w, back_w, cols, base = refs[:9]
    pieces = refs[9 : 9 + count]
    energy, esum, dx_out, dval_out, dgeo, wide, across, split, g, dg = refs[9 + count :]
    step = pl.program_id(0)

    @pl.when(step == 0)
    def _():
        fill_split(pieces, split)
        wide[...] = jnp.zeros_like(wide)
        across[...] = jnp.zeros_like(across)
        esum[...] = jnp.zeros_like(esum)

    @pl.when(step % per == 0)
    def _():
        energy[...] = base[...]

    chosen = mark_atoms(nbrs, step // per, split.shape[1])
    gathered(split, chosen, g)
    value = val[...]
    s = contracted(geo, group, g, value)
    update, slope = silu_pair(lx[...] + product(s_w[1], s))
    fresh = x[...] + update
    weight = cols[:, 2:3]
    read = jnp.sum(fresh * weight, axis=0, keepdims=True) * norm
    cuts = []
    dgeo[...] = jnp.zeros_like(dgeo)
    for q in range(group):
        cut = geo[0, q : q + 1, :]
        cuts.append(cut)
        energy[...] += read[:, lanes_of(q)] * cut
        dgeo[0, q : q + 1, :] = read[:, lanes_of(q)]

    @pl.when(step % per == per - 1)
    def _():
        esum[0:1, :] += energy[...]

    d_fresh = weight * (jnp.concatenate(cuts, 1) * norm)
    pulled = product(back_w[1], d_fresh * slope)
    dx_out[...] = d_fresh + pulled[:LATENT]
    dval_out[...] = pull_mixed(
        geo, group, g, value, pulled[LATENT:], chosen, dgeo, wide, across, dg
    )


def last_pass(geo, nbrs, pieces, x, lx, val, s_w, back_w, cols, base, slots, group):
    edges = x.shape[1]
    per = slots // group
    rows = HARM * TENSORS
    columns = sum(p.shape[1] for p in pieces)
    return pl.pallas_call(
        partial(
            last_kernel, group=group, per=per, norm=1.0 / math.sqrt(slots), count=len(pieces)
        ),
        grid=(geo.shape[1] // group,),
        out_shape=[
            jax.ShapeDtypeStruct(base.shape, F32),
            edge_shape(8, UNIT),
            edge_shape(LATENT, edges),
            edge_shape(TENSORS, edges),
            jax.ShapeDtypeStruct((HARM,) + geo.shape[1:], F32),
            edge_shape(rows, columns - base.shape[1]),
            edge_shape(rows, base.shape[1]),
        ],
        in_specs=[row_spec(18, group, 0), index_spec(group, 0)]
        + [edge_spec(r, group, 0) for r in (LATENT, LATENT, TENSORS)]
        + [WHOLE] * 3
        + [unit_spec(1, per)]
        + [WHOLE] * len(pieces),
        out_specs=[
            unit_spec(1, per),
            WHOLE,
            edge_spec(LATENT, group, 0),
            edge_spec(TENSORS, group, 0),
            row_spec(HARM, group, 0),
            WHOLE,
            WHOLE,
        ],
        scratch_shapes=[
            pltpu.VMEM((2 * rows, columns), BF16),
            pltpu.VMEM((rows, group * UNIT), F32),
            pltpu.VMEM((2 * rows, group * UNIT), BF16),
        ],
        compiler_params=params(),
        cost_estimate=effort(16 * rows * edges * edges // slots),
        name="last_pass",
    )(geo, nbrs, x, lx, val, s_w, back_w, cols, base, *pieces)


def pull_env(geo, group, total, emb, dgeo, norm):
    columns = []
    for q in range(group):
        part = emb[:, lanes_of(q)]
        cut = geo[0, q : q + 1, :] * norm
        grad = None
        for m in range(HARM):
            source = total[rows_of(m), :]
            if m == 0:
                grad = source
            else:
                grad = grad + source * geo[m, q : q + 1, :]
                dgeo[m, q : q + 1, :] += cut * jnp.sum(source * part, axis=0, keepdims=True)
        dgeo[0, q : q + 1, :] += norm * jnp.sum(grad * part, axis=0, keepdims=True)
        columns.append(grad * cut)
    return jnp.concatenate(columns, 1)


def middle_back_kernel(*refs, group, per, norm, aliased, first):
    geo, nbrs, own, low, high, dgeo_in, dx, dval, emb, g, slope, val, ev_w, back_w = refs[:14]
    wide_in, across_in = refs[14:16] if aliased else (None, None)
    dx_out, dval_out, dgeo, wide, across, total, dg = refs[14 + aliased :]
    step = pl.program_id(0)

    @pl.when(step == 0)
    def _():
        wide[...] = wide_in[...] if aliased else jnp.zeros_like(wide)
        across[...] = across_in[...] if aliased else jnp.zeros_like(across)

    @pl.when(step % per == 0)
    def _():
        total[...] = own[...] + low[...] + high[...]

    chosen = mark_atoms(nbrs, first + step // per, wide.shape[1] + across.shape[1])
    dgeo[...] = dgeo_in[...]
    demb = pull_env(geo, group, total, emb, dgeo, norm)
    d_fresh = dx[...] + product(ev_w[1], jnp.concatenate([demb, dval[...]], 0))
    pulled = product(back_w[0], d_fresh * slope[...])
    dx_out[...] = d_fresh + pulled[:LATENT]
    dval_out[...] = pull_mixed(
        geo, group, g, val[...], pulled[LATENT:], chosen, dgeo, wide, across, dg
    )


def middle_back(
    geo, nbrs, grads, dgeo, dx, dval, emb, g, slope, val, ev_w, back_w, slots, group, span, before
):
    edges = dx.shape[1]
    per = slots // group
    first = span[0] * per
    rows = HARM * TENSORS
    atoms = geo.shape[1] // slots * UNIT
    aliased = len(before)
    shapes = [
        edge_shape(LATENT, edges),
        edge_shape(TENSORS, edges),
        jax.ShapeDtypeStruct((HARM,) + geo.shape[1:], F32),
        edge_shape(rows, 3 * atoms),
        edge_shape(rows, atoms),
    ]
    extra = [*before[3:], *before[:3]]
    return pl.pallas_call(
        partial(
            middle_back_kernel, group=group, per=per, norm=1.0 / math.sqrt(slots), aliased=aliased,
            first=span[0],
        ),
        grid=((span[1] - span[0]) * per,),
        out_shape=shapes,
        in_specs=[row_spec(18, group, first), index_spec(group, first)]
        + [unit_spec(rows, per)] * 3
        + [row_spec(HARM, group, first)]
        + [
            edge_spec(r, group, first)
            for r in (LATENT, TENSORS, TENSORS, rows, LATENT, TENSORS)
        ]
        + [WHOLE] * 2
        + ([WHOLE] * 2 + [pl.BlockSpec(memory_space=pl.ANY)] * 3 if before else []),
        out_specs=[
            edge_spec(LATENT, group, first),
            edge_spec(TENSORS, group, first),
            row_spec(HARM, group, first),
            WHOLE,
            WHOLE,
        ],
        scratch_shapes=[
            pltpu.VMEM((rows, UNIT), F32),
            pltpu.VMEM((2 * rows, group * UNIT), BF16),
        ],
        input_output_aliases={16 + n: n for n in range(3)} if before else {},
        compiler_params=params(),
        cost_estimate=effort(8 * rows * edges * edges // slots),
        name="middle_back",
    )(geo, nbrs, *grads, dgeo, dx, dval, emb, g, slope, val, ev_w, back_w, *extra)


def first_back_kernel(
    geo, own, low, high, dgeo_in, dx, dval, emb, slope, ev_w, rad_w, *rest, group, per, norm
):
    dgeo, total = rest[-2:]
    step = pl.program_id(0)

    @pl.when(step % per == 0)
    def _():
        total[...] = own[...] + low[...] + high[...]

    dgeo[0:HARM] = dgeo_in[...]
    demb = pull_env(geo, group, total, emb, dgeo, norm)
    d_fresh = dx[...] + product(ev_w[0], jnp.concatenate([demb, dval[...]], 0))
    radial = product(rad_w[...], d_fresh * slope[...])
    for q in range(group):
        for n in range(BASIS):
            dgeo[HARM + n, q : q + 1, :] = radial[n : n + 1, lanes_of(q)]


def first_back(
    geo, grads, dgeo, dx, dval, emb, slope, ev_w, rad_w, slots, group, span, before
):
    per = slots // group
    first = span[0] * per
    rows = HARM * TENSORS
    return pl.pallas_call(
        partial(first_back_kernel, group=group, per=per, norm=1.0 / math.sqrt(slots)),
        grid=((span[1] - span[0]) * per,),
        out_shape=jax.ShapeDtypeStruct((HARM + BASIS,) + geo.shape[1:], F32),
        in_specs=[row_spec(18, group, first)]
        + [unit_spec(rows, per)] * 3
        + [row_spec(HARM, group, first)]
        + [edge_spec(r, group, first) for r in (LATENT, TENSORS, TENSORS, LATENT)]
        + [WHOLE] * 2
        + [pl.BlockSpec(memory_space=pl.ANY)] * len(before),
        out_specs=row_spec(HARM + BASIS, group, first),
        scratch_shapes=[pltpu.VMEM((rows, UNIT), F32)],
        input_output_aliases={11 + n: n for n in range(len(before))},
        compiler_params=params(),
        cost_estimate=effort(64 * LATENT * LATENT * dx.shape[1]),
        name="first_back",
    )(geo, *grads, dgeo, dx, dval, emb, slope, ev_w, rad_w, *before)


def geometry_back_kernel(vec, dgeo, nbrs, wide_out, across_out, dvec, *, slots):
    rows_total = vec.shape[1]
    units = rows_total // slots
    for group in range(rows_total // 8):
        up = slice(group * 8, group * 8 + 8)
        vx, vy, vz = (vec[axis, up, :] for axis in range(3))
        inverse, cut, slope, sine, cosine = distances(vx, vy, vz)
        ux, uy, uz = vx * inverse, vy * inverse, vz * inverse
        _, h1, h2, h3, h4, h5, h6, h7, h8 = (dgeo[m, up, :] for m in range(HARM))
        dux = h1 + ROOT3 * (uy * h4 + uz * h7 + ux * h8)
        duy = h2 + ROOT3 * (ux * h4 + uz * h5 - uy * h8)
        duz = h3 + ROOT3 * (uy * h5 + ux * h7) + 3.0 * uz * h6
        along = ux * dux + uy * duy + uz * duz
        scale = math.sqrt(2.0 / CUTOFF) * inverse
        by_wave = jnp.zeros_like(sine)
        by_angle = jnp.zeros_like(sine)
        before, now = jnp.zeros_like(sine), sine
        before_c, now_c = jnp.ones_like(sine), cosine
        for n in range(BASIS):
            pulled = dgeo[HARM + n, up, :]
            by_wave = by_wave + pulled * now
            by_angle = by_angle + (n + 1.0) * (pulled * now_c)
            before, now = now, 2.0 * cosine * now - before
            before_c, now_c = now_c, 2.0 * cosine * now_c - before_c
        d_dist = slope * dgeo[0, up, :] + scale * (
            (math.pi / CUTOFF) * by_angle * cut + by_wave * (slope - inverse * cut)
        )
        dvec[0, up, :] = (dux - ux * along) * inverse + ux * d_dist
        dvec[1, up, :] = (duy - uy * along) * inverse + uy * d_dist
        dvec[2, up, :] = (duz - uz * along) * inverse + uz * d_dist
    total = jnp.zeros((2 * 48, UNIT), F32)
    rows = lax.broadcasted_iota(jnp.int32, (16, UNIT), 0)
    lane = lax.broadcasted_iota(jnp.int32, (UNIT, UNIT), 0)
    for group in range(rows_total // 4):
        spreads, picks = [], []
        for k in range(group * 4, group * 4 + 4):
            index = nbrs[k : k + 1, :]
            here = rows == lax.shift_right_arithmetic(index, 7)
            spreads.append(
                jnp.concatenate(
                    [jnp.where(here, dvec[axis, k : k + 1, :], 0.0) for axis in range(3)], 0
                )
            )
            picks.append((lane == (index & 127)).astype(F32).astype(BF16))
        spread = jnp.concatenate(spreads, 1)
        total = total + dot_nt(stacked(spread), jnp.concatenate(picks, 1))
    total = total[:48] + total[48:]
    wide_out[...] = jnp.zeros_like(wide_out)
    across_out[...] = jnp.zeros_like(across_out)
    for axis in range(3):
        for block in range(4 * units):
            row = axis * 16 + block
            out, place = (wide_out, block) if block < 3 * units else (across_out, block - 3 * units)
            out[axis : axis + 1, lanes_of(place)] = total[row : row + 1]
        for unit in range(units):
            part = dvec[axis, unit * slots : (unit + 1) * slots, :]
            wide_out[axis : axis + 1, lanes_of(unit)] -= jnp.sum(part, axis=0, keepdims=True)


def geometry_back(vec, dgeo, nbrs, slots):
    atoms = vec.shape[1] // slots * UNIT
    return pl.pallas_call(
        partial(geometry_back_kernel, slots=slots),
        out_shape=[edge_shape(8, 3 * atoms), edge_shape(8, atoms)],
        in_specs=[WHOLE] * 3,
        out_specs=[WHOLE] * 2,
        scratch_shapes=[pltpu.VMEM(vec.shape, F32)],
        compiler_params=params(),
        name="geometry_back",
    )(vec, dgeo, nbrs)


def swap_y(rows, face):
    if lax.axis_size("gy") == 2:
        return passed_along(rows, "gy", 1)
    up = passed_along(rows[:, :face], "gy", 1)
    down = passed_along(rows[:, face:], "gy", -1)
    return jnp.concatenate([up, down], 1)


def return_y(rows, face):
    if lax.axis_size("gy") == 2:
        return passed_along(rows, "gy", 1)
    up = passed_along(rows[:, :face], "gy", -1)
    down = passed_along(rows[:, face:], "gy", 1)
    return jnp.concatenate([up, down], 1)


def ghost_rows(parts, wanted, face):
    below, above = [], []
    for part in parts:
        if below:
            part, below[-1], above[-1] = lax.optimization_barrier((part, below[-1], above[-1]))
        below.append(passed_along(part, "gx", 1))
        above.append(passed_along(part, "gx", -1))
    pieces = [*parts, *below, *above]
    return pieces + [swap_y(lend_env(wanted, pieces), face)]


def owned_grads(wide, across, wanted, face, widths, total, steps, hops):
    across, total = lax.optimization_barrier((across, total))
    returned = return_y(across, face)
    for _ in range(hops):
        total = sum_step(total, steps)
    own, below, above = take_back(returned, wanted, wide, widths)
    found = []
    for number in range(len(widths)):
        send = below[number], above[number]
        if found:
            send, found[-1], total = lax.optimization_barrier((send, found[-1], total))
        found.append(
            [own[number], passed_along(send[0], "gx", -1), passed_along(send[1], "gx", 1)]
        )
    return found, total


def sum_steps():
    count = lax.axis_size("gx")
    if count & (count - 1) or lax.axis_size("gy") != 2:
        return None
    return [("gx", 1 << n) for n in range(count.bit_length() - 1)] + [("gy", 1)]


def sum_step(total, steps):
    if steps:
        axis, by = steps.pop(0)
        total = total + passed_along(total, axis, by)
    return total


def per_device(
    positions,
    species,
    neighbours,
    send_x,
    send_y,
    two_weight,
    two_bias,
    env_weight,
    value_weight,
    latent_weight,
    latent_bias,
    out_weight,
    species_shift,
):
    group = 16
    nbrs = neighbours[0, 0]
    atoms = nbrs.shape[1]
    face = send_y.shape[3]
    rows, wanted = pack_rows(positions[0, 0], species[0], send_x[0, 0], send_y[0, 0])
    below = passed_along(rows, "gx", 1)
    above = passed_along(rows, "gx", -1)
    two_w, mix_w, s_w, back_w, ev_w, rad_w, cols = prepare_weights(
        two_weight, two_bias, env_weight, value_weight, latent_weight, latent_bias, out_weight
    )
    lent, wanted = lend_rows(rows, below, above, wanted)
    across = swap_y(lent, face)
    slots = nbrs.shape[0]
    units = atoms // UNIT
    vec, geo, nbrs, base = geometry(rows, below, above, across, nbrs, species_shift, face)
    parts, before = [], []
    for span in ((0, 1), (1, units)):
        *before, part = first_pass(
            geo, rows, two_w, mix_w, cols, slots, group, span, before
        )
        parts.append(part)
    x0, slope_a, emb0, val0, lx0 = before
    pieces = ghost_rows(parts, wanted, face)
    parts, before = [], []
    for span in ((0, units - 1), (units - 1, units)):
        *before, part = middle_pass(
            geo, nbrs, pieces, x0, lx0, val0, s_w, mix_w, cols, slots, group, span, before
        )
        parts.append(part)
    g0, slope0, x1, emb1, val1, lx1 = before
    pieces = ghost_rows(parts, wanted, face)
    energy, total, dx, dval, dgeo, wide, across = last_pass(
        geo, nbrs, pieces, x1, lx1, val1, s_w, back_w, cols, base, slots, group
    )
    steps = sum_steps()
    if steps is None:
        total = lax.psum(total, ("gx", "gy"))
    grads, total = owned_grads(wide, across, wanted, face, (UNIT, atoms - UNIT), total, steps, 1)
    before = []
    for number, span in enumerate(((0, 1), (1, units))):
        before = middle_back(
            geo, nbrs, grads[number], dgeo, dx, dval, emb1, g0, slope0, val0, ev_w, back_w,
            slots, group, span, before,
        )
    dx, dval, dgeo, wide, across = before
    grads, total = owned_grads(wide, across, wanted, face, (atoms - UNIT, UNIT), total, steps, 2)
    before = []
    for number, span in enumerate(((0, units - 1), (units - 1, units))):
        before = [
            first_back(
                geo, grads[number], dgeo, dx, dval, emb0, slope_a, ev_w, rad_w, slots, group,
                span, before,
            )
        ]
    wide, across = geometry_back(vec, before[0], nbrs, slots)
    grads, total = owned_grads(wide, across, wanted, face, (atoms,), total, steps, 1)
    while steps:
        total = sum_step(total, steps)
    mean_energy = jnp.sum(total) / (atoms * lax.axis_size("gx") * lax.axis_size("gy"))
    forces = -(grads[0][0] + grads[0][1] + grads[0][2])[:3]
    return (energy[None], forces[None, None], mean_energy.reshape(1))


def solution(mesh):
    placed = (
        P(("groups", "gx"), "gy", None, None),
        P(("groups", "gx"), "gy", None),
        P(("groups", "gx"), "gy", None, None),
        P(("groups", "gx"), "gy", None, None),
        P(("groups", "gx"), "gy", None, None),
        P(),
        P(),
        P(),
        P(),
        P(),
        P(),
        P(),
        P(),
    )
    return jax.shard_map(
        per_device,
        mesh=mesh,
        in_specs=placed,
        out_specs=(
            P(("groups", "gx"), "gy", None),
            P(("groups", "gx"), "gy", None, None),
            P("groups"),
        ),
        check_vma=False,
    )
```

```python
from functools import partial
import math

import jax
import jax.numpy as jnp
from jax import lax
from jax.experimental import pallas as pl
from jax.experimental.pallas import tpu as pltpu
from jax.sharding import PartitionSpec as P

BASIS = 8
SPECIES = 5
SITES_X = 2
SITES_Y = 16
CUTOFF = 2.5
LATENT = 128
TENSORS = 32
HARM = 9
UNIT = 128
ROOT3 = math.sqrt(3.0)
DEGREE = (0, 1, 1, 1, 2, 2, 2, 2, 2)
F32 = jnp.float32
BF16 = jnp.bfloat16
WHOLE = pl.BlockSpec(memory_space=pltpu.VMEM)
SCALARS = pl.BlockSpec(memory_space=pltpu.SMEM)


def params(mib=44):
    return pltpu.CompilerParams(vmem_limit_bytes=mib << 20)


def passed_along(value, axis, by):
    count = lax.axis_size(axis)
    return lax.ppermute(value, axis, [(i, (i + by) % count) for i in range(count)])


def dot(a, b):
    return jnp.dot(a, b, preferred_element_type=F32)


def dot_nt(a, b):
    return lax.dot_general(a, b, (((1,), (1,)), ((), ())), preferred_element_type=F32)


def halves(value):
    high = value.astype(BF16)
    return high, (value - high.astype(F32)).astype(BF16)


def stacked(value):
    return jnp.concatenate(halves(value), 0)


def product(weights, value):
    rows = weights.shape[0] // 2
    both = dot(weights, stacked(value))
    return both[:rows] + both[rows:]


def rounded(value):
    high = value.astype(BF16).astype(F32)
    return high, value - high


def weights_kernel(two, bias, env, val, lat, lat_bias, out_w, *outs):
    two_out, mix_out, s_out, back_out, ev_out, rad_out, cols = outs

    def depth_stack(piece):
        high, low = rounded(piece)
        top = jnp.concatenate([high, high], 0)
        bottom = jnp.concatenate([low, jnp.zeros_like(low)], 0)
        return top.T, bottom.T

    def lane_stack(piece):
        high, low = rounded(piece)
        top = jnp.concatenate([high, high], 1)
        return top, jnp.concatenate([low, jnp.zeros_like(low)], 1)

    def join(pieces):
        tops, bottoms = zip(*pieces)
        return jnp.concatenate(list(tops) + list(bottoms), 0).astype(BF16)

    def wide_stack(piece):
        return jnp.concatenate(lane_stack(piece), 0).astype(BF16)

    width = two.shape[1]
    first = jnp.concatenate(
        [
            two[0:SPECIES, :],
            bias[...],
            jnp.zeros((2, width), F32),
            two[SPECIES : 2 * SPECIES, :],
            jnp.zeros((3, width), F32),
            two[2 * SPECIES :, :],
        ],
        0,
    )
    two_out[...] = join([depth_stack(first)])
    rad_out[...] = wide_stack(two[2 * SPECIES :, :])
    for layer in range(env.shape[0]):
        latent = lat[layer]
        mix_out[layer] = join(
            [lane_stack(env[layer]), lane_stack(val[layer]), depth_stack(latent[:width])]
        )
        s_out[layer] = join([depth_stack(latent[width:])])
        back_out[layer] = wide_stack(latent)
        high = [rounded(env[layer]), rounded(val[layer])]
        top = jnp.concatenate([high[0][0], high[1][0]] * 2, 0).T
        bottom = jnp.concatenate([high[0][1], high[1][1]] + [jnp.zeros_like(high[0][1])] * 2, 0).T
        ev_out[layer] = jnp.concatenate([top, bottom], 0).astype(BF16)
    columns = jnp.concatenate(
        [lat_bias[...], out_w[...], jnp.zeros((8 - lat_bias.shape[0] - 1, width), F32)], 0
    )
    cols[...] = columns.T


def prepare_weights(two, bias, env, val, lat, lat_bias, out_w):
    layers = env.shape[0]
    shapes = [
        (2 * LATENT, 48),
        (layers, 2 * (LATENT + 2 * TENSORS), 2 * LATENT),
        (layers, 2 * LATENT, 6 * TENSORS),
        (layers, 2 * (LATENT + 3 * TENSORS), 2 * LATENT),
        (layers, 2 * LATENT, 4 * TENSORS),
        (2 * BASIS, 2 * LATENT),
    ]
    out_shape = [jax.ShapeDtypeStruct(s, BF16) for s in shapes]
    out_shape.append(jax.ShapeDtypeStruct((LATENT, 8), F32))
    return pl.pallas_call(
        weights_kernel,
        out_shape=out_shape,
        in_specs=[WHOLE] * 7,
        out_specs=[WHOLE] * 7,
        compiler_params=params(60),
        name="prepare_weights",
    )(two, bias[None], env.swapaxes(1, 2), val.swapaxes(1, 2), lat, lat_bias, out_w[None])


def shifted(rows, by_x, by_y):
    lane_row = lax.broadcasted_iota(jnp.int32, rows.shape, 0)
    return rows + jnp.where(lane_row == 0, by_x, jnp.where(lane_row == 1, by_y, 0.0))


def lane_pick(table, row, index, blocks):
    low = index & 127
    high = lax.shift_right_arithmetic(index, 7)
    found = jnp.zeros(index.shape, F32)
    for block in range(blocks):
        span = slice(block * 128, block * 128 + 128)
        source = table[...][:, span] if row is None else table[row : row + 1, span]
        source = jnp.broadcast_to(source, index.shape)
        taken = jnp.take_along_axis(source, low, axis=1)
        found = jnp.where(high == block, taken, found)
    return found


def fill_wide(own, below, above, table, remap):
    atoms = own.shape[1]
    table[:, 0:atoms] = own[...]
    table[:, atoms : 2 * atoms] = shifted(below[...], -float(SITES_X), 0.0)
    table[:, 2 * atoms : 3 * atoms] = shifted(above[...], float(SITES_X), 0.0)
    lanes = lax.broadcasted_iota(jnp.int32, (1, atoms), 1).astype(F32)
    remap[:, 0:atoms] = lanes
    remap[:, atoms : 2 * atoms] = below[5:6, :] + float(atoms)
    remap[:, 2 * atoms : 3 * atoms] = above[4:5, :] + float(2 * atoms)


def lend_kernel(own, below, above, wanted, rows_out, wanted_out, table, remap):
    atoms = own.shape[1]
    blocks = 3 * atoms // 128
    fill_wide(own, below, above, table, remap)
    for tile in range(wanted.shape[1] // 128):
        span = slice(tile * 128, tile * 128 + 128)
        index = jnp.broadcast_to(wanted[:, span], (8, 128))
        place = lane_pick(remap, 0, index, blocks).astype(jnp.int32)
        place = jnp.where(index < 0, -1, place)
        wanted_out[:, span] = place[0:1]
        rows_out[:, span] = lane_pick(table, None, place, blocks)


def pack_kernel(coords, species, lend_x, lend_y, rows, wanted):
    face = lend_y.shape[1]
    rows[...] = jnp.zeros_like(rows)
    rows[0:3, :] = coords[...]
    rows[3:4, :] = species[...].astype(F32)
    rows[4:6, :] = lend_x[...].astype(F32)
    wanted[...] = jnp.full(wanted.shape, -1, jnp.int32)
    wanted[:, 0:face] = lend_y[1:2, :]
    wanted[:, face : 2 * face] = lend_y[0:1, :]


def pack_rows(coords, species, lend_x, lend_y):
    atoms = coords.shape[1]
    return pl.pallas_call(
        pack_kernel,
        out_shape=[edge_shape(8, atoms), jax.ShapeDtypeStruct((1, atoms), jnp.int32)],
        in_specs=[WHOLE] * 4,
        out_specs=[WHOLE] * 2,
        compiler_params=params(60),
        name="pack_rows",
    )(coords, species, lend_x, lend_y)


def lend_rows(own, below, above, wanted):
    atoms = own.shape[1]
    return pl.pallas_call(
        lend_kernel,
        out_shape=[
            jax.ShapeDtypeStruct(wanted.shape[:0] + (8, wanted.shape[1]), F32),
            jax.ShapeDtypeStruct(wanted.shape, jnp.int32),
        ],
        in_specs=[WHOLE] * 4,
        out_specs=[WHOLE] * 2,
        scratch_shapes=[pltpu.VMEM((8, 3 * atoms), F32), pltpu.VMEM((1, 3 * atoms), F32)],
        compiler_params=params(),
        name="lend_rows",
    )(own, below, above, wanted)


def distances(vx, vy, vz):
    dist = jnp.sqrt(vx * vx + vy * vy + vz * vz)
    inverse = 1.0 / dist
    scaled = jnp.minimum(dist * (1.0 / CUTOFF), 1.0)
    second = scaled * scaled
    fourth = second * second
    sixth = fourth * second
    cut = 1.0 - 28.0 * sixth + 48.0 * (sixth * scaled) - 21.0 * (sixth * second)
    rest = 1.0 - scaled
    slope = (-168.0 / CUTOFF) * (fourth * scaled) * (rest * rest)
    angle = scaled * math.pi
    return inverse, cut, slope, jnp.sin(angle), jnp.cos(angle)


def geometry_kernel(
    own, below, above, across, nbrs, shift, vec_out, geo_out, nbr_out, base_out, table, remap, face
):
    atoms = own.shape[1]
    slots = nbrs.shape[0]
    blocks = table.shape[1] // 128
    fill_wide(own, below, above, table, remap)
    lanes = lax.broadcasted_iota(jnp.int32, (8, atoms), 1)
    rows = lax.broadcasted_iota(jnp.int32, (8, atoms), 0)
    moved = across[...] + jnp.where(
        rows == 1, jnp.where(lanes < face, -float(SITES_Y), float(SITES_Y)), 0.0
    )
    empty = jnp.where(rows == 2, -1000.0, jnp.where(rows == 3, -1.0, 0.0))
    table[:, 3 * atoms : 4 * atoms] = jnp.where(lanes < 2 * face, moved, empty)
    remap[:, 3 * atoms : 4 * atoms] = (
        lax.broadcasted_iota(jnp.int32, (1, atoms), 1) + 3 * atoms
    ).astype(F32)
    base = jnp.zeros((1, atoms), F32)
    for kind in range(SPECIES):
        base = base + jnp.where(own[3:4, :] == float(kind), shift[kind], 0.0)
    base_out[...] = base
    for group in range(slots // 8):
        for tile in range(atoms // UNIT):
            span = slice(tile * UNIT, tile * UNIT + UNIT)
            index = nbrs[group * 8 : group * 8 + 8, span]
            up = slice(tile * slots + group * 8, tile * slots + group * 8 + 8)
            index = lane_pick(remap, 0, index, blocks).astype(jnp.int32)
            nbr_out[up, :] = index
            vx = lane_pick(table, 0, index, blocks) - own[0:1, span]
            vy = lane_pick(table, 1, index, blocks) - own[1:2, span]
            vz = lane_pick(table, 2, index, blocks) - own[2:3, span]
            kind = lane_pick(table, 3, index, blocks)
            vec_out[0, up, :] = vx
            vec_out[1, up, :] = vy
            vec_out[2, up, :] = vz
            inverse, cut, _, sine, cosine = distances(vx, vy, vz)
            ux, uy, uz = vx * inverse, vy * inverse, vz * inverse
            harm = [
                ux,
                uy,
                uz,
                ROOT3 * ux * uy,
                ROOT3 * uy * uz,
                0.5 * (3.0 * uz * uz - 1.0),
                ROOT3 * ux * uz,
                0.5 * ROOT3 * (ux * ux - uy * uy),
            ]
            geo_out[0, up, :] = cut
            for number, value in enumerate(harm):
                geo_out[1 + number, up, :] = value
            scale = math.sqrt(2.0 / CUTOFF) * inverse * cut
            before, now = jnp.zeros_like(sine), sine
            for number in range(BASIS):
                geo_out[9 + number, up, :] = now * scale
                before, now = now, 2.0 * cosine * now - before
            geo_out[17, up, :] = kind


def geometry(own, below, above, across, nbrs, shift, face):
    slots, atoms = nbrs.shape
    return pl.pallas_call(
        partial(geometry_kernel, face=face),
        out_shape=[
            jax.ShapeDtypeStruct((3, slots * atoms // UNIT, UNIT), F32),
            jax.ShapeDtypeStruct((18, slots * atoms // UNIT, UNIT), F32),
            jax.ShapeDtypeStruct((slots * atoms // UNIT, UNIT), jnp.int32),
            jax.ShapeDtypeStruct((1, atoms), F32),
        ],
        in_specs=[WHOLE] * 5 + [SCALARS],
        out_specs=[WHOLE] * 4,
        scratch_shapes=[pltpu.VMEM((8, 4 * atoms), F32), pltpu.VMEM((1, 4 * atoms), F32)],
        compiler_params=params(),
        name="geometry",
    )(own, below, above, across, nbrs, shift)


def silu_pair(pre):
    gate = 1.0 / (1.0 + jnp.exp(-pre))
    value = pre * gate
    return value, gate + value * (1.0 - gate)


def row_spec(count, group, first):
    return pl.BlockSpec((count, group, UNIT), lambda i: (0, first + i, 0))


def index_spec(group, first):
    return pl.BlockSpec((group, UNIT), lambda i: (first + i, 0))


def edge_spec(rows, group, first):
    return pl.BlockSpec((rows, group * UNIT), lambda i: (0, first + i))


def unit_spec(rows, per):
    return pl.BlockSpec((rows, UNIT), lambda i: (0, i // per))


def edge_shape(rows, edges):
    return jax.ShapeDtypeStruct((rows, edges), F32)


def lanes_of(q):
    return slice(q * UNIT, (q + 1) * UNIT)


def rows_of(m):
    return slice(m * TENSORS, (m + 1) * TENSORS)


def add_env(geo, step, per, group, embed, env_out, norm):
    @pl.when(step % per == 0)
    def _():
        env_out[...] = jnp.zeros_like(env_out)

    cuts = [geo[0, q : q + 1, :] * norm for q in range(group)]
    for m in range(HARM):
        total = env_out[rows_of(m), :]
        for q in range(group):
            factor = cuts[q] if m == 0 else cuts[q] * geo[m, q : q + 1, :]
            total = total + embed[:TENSORS, lanes_of(q)] * factor
        env_out[rows_of(m), :] = total


def first_kernel(
    geo, own, two_w, mix_w, cols, *outs, group, per, norm
):
    x_out, slope_out, emb_out, val_out, lx_out, env_out = outs[-6:]
    step = pl.program_id(0)
    kinds = lax.broadcasted_iota(jnp.int32, (8, UNIT), 0)
    kinds_f = kinds.astype(F32)
    centre = jnp.where((own[3:4, :] == kinds_f) & (kinds < SPECIES), 1.0, 0.0)
    centre = jnp.where(kinds == SPECIES, 1.0, centre)
    parts = []
    for q in range(group):
        other = jnp.where(geo[17, q : q + 1, :] == kinds_f, 1.0, 0.0)
        radial = [geo[9 + n, q : q + 1, :] for n in range(BASIS)]
        parts.append(jnp.concatenate([centre, other] + radial, 0))
    features = jnp.concatenate(parts, 1)
    x, slope = silu_pair(product(two_w[...], features))
    x_out[...] = x
    slope_out[...] = slope
    mixed = product(mix_w[0], x)
    emb_out[...] = mixed[:TENSORS]
    val_out[...] = mixed[TENSORS : 2 * TENSORS]
    lx_out[...] = mixed[2 * TENSORS :] + cols[:, 0:1]
    add_env(geo, step, per, group, mixed, env_out, norm)


def wide_unit_spec(rows, per, first):
    return pl.BlockSpec((rows, UNIT), lambda i: (0, first + i // per))


def first_pass(geo, own, two_w, mix_w, cols, slots, group, span, before):
    edges = geo.shape[1] * UNIT
    per = slots // group
    first = span[0] * per
    rows = (LATENT, LATENT, TENSORS, TENSORS, LATENT)
    return pl.pallas_call(
        partial(first_kernel, group=group, per=per, norm=1.0 / math.sqrt(slots)),
        grid=((span[1] - span[0]) * per,),
        out_shape=[edge_shape(r, edges) for r in rows]
        + [edge_shape(HARM * TENSORS, (span[1] - span[0]) * UNIT)],
        in_specs=[row_spec(18, group, first), wide_unit_spec(8, per, span[0])]
        + [WHOLE] * 3
        + [pl.BlockSpec(memory_space=pl.ANY)] * len(before),
        out_specs=[edge_spec(r, group, first) for r in rows]
        + [unit_spec(HARM * TENSORS, per)],
        input_output_aliases={5 + n: n for n in range(len(before))},
        compiler_params=params(),
        cost_estimate=effort(64 * LATENT * LATENT * edges),
        name="first_pass",
    )(geo, own, two_w, mix_w, cols, *before)


def chosen_rows(index, columns, start):
    rows = lax.broadcasted_iota(jnp.int32, (columns, index.shape[1]), 0) + start
    return (rows == index).astype(F32).astype(BF16)


def mark_atoms(nbrs, unit, columns):
    own = columns // 4
    centre = lax.broadcasted_iota(jnp.int32, (1, UNIT), 1) + unit * UNIT
    here = lax.broadcasted_iota(jnp.int32, (own, UNIT), 0)
    away = lax.broadcasted_iota(jnp.int32, (columns - own, UNIT), 0) + own
    parts = []
    for q in range(nbrs.shape[0]):
        index = nbrs[q : q + 1, :]
        top = (here == index).astype(F32) + (here == centre).astype(F32)
        rest = (away == index).astype(F32)
        parts.append(jnp.concatenate([top, rest], 0).astype(BF16))
    return jnp.concatenate(parts, 1)


def lend_env_kernel(wanted, *refs):
    out = refs[-1]
    rows = out.shape[0]
    total = jnp.zeros((2 * rows, out.shape[1]), F32)
    start = 0
    for block in refs[:-1]:
        chosen = chosen_rows(wanted[...], block.shape[1], start)
        total = total + dot(stacked(block[...]), chosen)
        start += block.shape[1]
    out[...] = total[:rows] + total[rows:]


def lend_env(wanted, pieces):
    return pl.pallas_call(
        lend_env_kernel,
        out_shape=jax.ShapeDtypeStruct((HARM * TENSORS, wanted.shape[1]), F32),
        in_specs=[WHOLE] * (1 + len(pieces)),
        out_specs=WHOLE,
        compiler_params=params(),
        name="lend_env",
    )(wanted, *pieces)


def take_back_kernel(returned, wanted, wide, *outs, widths):
    atoms = wide.shape[1] // 3
    rows = returned.shape[0]
    value = stacked(returned[...])
    for place in range(3):
        chosen = chosen_rows(wanted[...], atoms, place * atoms)
        both = dot_nt(value, chosen)
        total = wide[:, place * atoms : (place + 1) * atoms] + both[:rows] + both[rows:]
        start = 0
        for number, width in enumerate(widths):
            outs[place * len(widths) + number][...] = total[:, start : start + width]
            start += width


def take_back(returned, wanted, wide, widths):
    outs = pl.pallas_call(
        partial(take_back_kernel, widths=widths),
        out_shape=[edge_shape(wide.shape[0], w) for w in widths] * 3,
        in_specs=[WHOLE] * 3,
        out_specs=[WHOLE] * (3 * len(widths)),
        compiler_params=params(),
        name="take_back",
    )(returned, wanted, wide)
    count = len(widths)
    return [list(outs[place * count : (place + 1) * count]) for place in range(3)]


def fill_split(pieces, split):
    rows = pieces[0].shape[0]
    start = 0
    for block in pieces:
        span = slice(start, start + block.shape[1])
        high, low = halves(block[...])
        split[:rows, span] = high
        split[rows:, span] = low
        start += block.shape[1]


def gathered(split, chosen, g):
    rows = HARM * TENSORS
    both = dot(split[...], chosen)
    g[...] = both[:rows] + both[rows:]


def contracted(geo, group, g, value):
    columns = []
    for q in range(group):
        span = lanes_of(q)
        sums = [g[0:TENSORS, span], None, None]
        for m in range(1, HARM):
            term = g[rows_of(m), span] * geo[m, q : q + 1, :]
            d = DEGREE[m]
            sums[d] = term if sums[d] is None else sums[d] + term
        columns.append(jnp.concatenate([part * value[:, span] for part in sums], 0))
    return jnp.concatenate(columns, 1)


def middle_kernel(*refs, group, per, norm, count, aliased, first):
    geo, nbrs, x, lx, val, s_w, mix_w, cols = refs[:8]
    pieces = refs[8 : 8 + count]
    g, slope_out, x_out, emb_out, val_out, lx_out, env_out, split = refs[
        8 + count + aliased :
    ]
    step = pl.program_id(0)

    @pl.when(step == 0)
    def _():
        fill_split(pieces, split)

    chosen = mark_atoms(nbrs, first + step // per, split.shape[1])
    gathered(split, chosen, g)
    s = contracted(geo, group, g, val[...])
    update, slope = silu_pair(lx[...] + product(s_w[0], s))
    slope_out[...] = slope
    fresh = x[...] + update
    x_out[...] = fresh
    mixed = product(mix_w[1], fresh)
    emb_out[...] = mixed[:TENSORS]
    val_out[...] = mixed[TENSORS : 2 * TENSORS]
    lx_out[...] = mixed[2 * TENSORS :] + cols[:, 1:2]
    add_env(geo, step, per, group, mixed, env_out, norm)


def middle_pass(geo, nbrs, pieces, x, lx, val, s_w, mix_w, cols, slots, group, span, before):
    edges = x.shape[1]
    per = slots // group
    first = span[0] * per
    rows = (HARM * TENSORS, LATENT, LATENT, TENSORS, TENSORS, LATENT)
    ins = 8 + len(pieces)
    columns = sum(p.shape[1] for p in pieces)
    return pl.pallas_call(
        partial(
            middle_kernel, group=group, per=per, norm=1.0 / math.sqrt(slots),
            count=len(pieces), aliased=len(before), first=span[0],
        ),
        grid=((span[1] - span[0]) * per,),
        out_shape=[edge_shape(r, edges) for r in rows]
        + [edge_shape(HARM * TENSORS, (span[1] - span[0]) * UNIT)],
        in_specs=[row_spec(18, group, first), index_spec(group, first)]
        + [edge_spec(r, group, first) for r in (LATENT, LATENT, TENSORS)]
        + [WHOLE] * (3 + len(pieces))
        + [pl.BlockSpec(memory_space=pl.ANY)] * len(before),
        out_specs=[edge_spec(r, group, first) for r in rows]
        + [unit_spec(HARM * TENSORS, per)],
        scratch_shapes=[
            pltpu.VMEM((2 * HARM * TENSORS, columns), BF16),
        ],
        input_output_aliases={ins + n: n for n in range(len(before))},
        compiler_params=params(),
        cost_estimate=effort(8 * HARM * TENSORS * edges * edges // slots),
        name="middle_pass",
    )(geo, nbrs, x, lx, val, s_w, mix_w, cols, *pieces, *before)


def effort(flops):
    return pl.CostEstimate(flops=flops, transcendentals=0, bytes_accessed=flops // 512)


def pull_mixed(geo, group, g, value, ds, chosen, dgeo, wide, across, dg):
    columns = []
    for q in range(group):
        span = lanes_of(q)
        part = value[:, span]
        pulled = [ds[rows_of(d), span] for d in range(3)]
        scaled = [p * part for p in pulled]
        total = None
        for m in range(HARM):
            d = DEGREE[m]
            source = g[rows_of(m), span]
            if m == 0:
                total = source * pulled[0]
                grad = scaled[0]
            else:
                harm = geo[m, q : q + 1, :]
                total = total + source * pulled[d] * harm
                dgeo[m, q : q + 1, :] += jnp.sum(source * scaled[d], axis=0, keepdims=True)
                grad = scaled[d] * harm
            high, low = halves(grad)
            dg[rows_of(m), span] = high
            dg[rows_of(HARM + m), span] = low
        columns.append(total)
    both = dot_nt(dg[...], chosen)
    rows = HARM * TENSORS
    total = both[:rows] + both[rows:]
    wide[...] += total[:, : wide.shape[1]]
    across[...] += total[:, wide.shape[1] :]
    return jnp.concatenate(columns, 1)


def last_kernel(*refs, group, per, norm, count):
    geo, nbrs, x, lx, val, s_w, back_w, cols, base = refs[:9]
    pieces = refs[9 : 9 + count]
    energy, esum, dx_out, dval_out, dgeo, wide, across, split, g, dg = refs[9 + count :]
    step = pl.program_id(0)

    @pl.when(step == 0)
    def _():
        fill_split(pieces, split)
        wide[...] = jnp.zeros_like(wide)
        across[...] = jnp.zeros_like(across)
        esum[...] = jnp.zeros_like(esum)

    @pl.when(step % per == 0)
    def _():
        energy[...] = base[...]

    chosen = mark_atoms(nbrs, step // per, split.shape[1])
    gathered(split, chosen, g)
    value = val[...]
    s = contracted(geo, group, g, value)
    update, slope = silu_pair(lx[...] + product(s_w[1], s))
    fresh = x[...] + update
    weight = cols[:, 2:3]
    read = jnp.sum(fresh * weight, axis=0, keepdims=True) * norm
    cuts = []
    dgeo[...] = jnp.zeros_like(dgeo)
    for q in range(group):
        cut = geo[0, q : q + 1, :]
        cuts.append(cut)
        energy[...] += read[:, lanes_of(q)] * cut
        dgeo[0, q : q + 1, :] = read[:, lanes_of(q)]

    @pl.when(step % per == per - 1)
    def _():
        esum[0:1, :] += energy[...]

    d_fresh = weight * (jnp.concatenate(cuts, 1) * norm)
    pulled = product(back_w[1], d_fresh * slope)
    dx_out[...] = d_fresh + pulled[:LATENT]
    dval_out[...] = pull_mixed(
        geo, group, g, value, pulled[LATENT:], chosen, dgeo, wide, across, dg
    )


def last_pass(geo, nbrs, pieces, x, lx, val, s_w, back_w, cols, base, slots, group):
    edges = x.shape[1]
    per = slots // group
    rows = HARM * TENSORS
    columns = sum(p.shape[1] for p in pieces)
    return pl.pallas_call(
        partial(
            last_kernel, group=group, per=per, norm=1.0 / math.sqrt(slots), count=len(pieces)
        ),
        grid=(geo.shape[1] // group,),
        out_shape=[
            jax.ShapeDtypeStruct(base.shape, F32),
            edge_shape(8, UNIT),
            edge_shape(LATENT, edges),
            edge_shape(TENSORS, edges),
            jax.ShapeDtypeStruct((HARM,) + geo.shape[1:], F32),
            edge_shape(rows, columns - base.shape[1]),
            edge_shape(rows, base.shape[1]),
        ],
        in_specs=[row_spec(18, group, 0), index_spec(group, 0)]
        + [edge_spec(r, group, 0) for r in (LATENT, LATENT, TENSORS)]
        + [WHOLE] * 3
        + [unit_spec(1, per)]
        + [WHOLE] * len(pieces),
        out_specs=[
            unit_spec(1, per),
            WHOLE,
            edge_spec(LATENT, group, 0),
            edge_spec(TENSORS, group, 0),
            row_spec(HARM, group, 0),
            WHOLE,
            WHOLE,
        ],
        scratch_shapes=[
            pltpu.VMEM((2 * rows, columns), BF16),
            pltpu.VMEM((rows, group * UNIT), F32),
            pltpu.VMEM((2 * rows, group * UNIT), BF16),
        ],
        compiler_params=params(),
        cost_estimate=effort(16 * rows * edges * edges // slots),
        name="last_pass",
    )(geo, nbrs, x, lx, val, s_w, back_w, cols, base, *pieces)


def pull_env(geo, group, total, emb, dgeo, norm):
    columns = []
    for q in range(group):
        part = emb[:, lanes_of(q)]
        cut = geo[0, q : q + 1, :] * norm
        grad = None
        for m in range(HARM):
            source = total[rows_of(m), :]
            if m == 0:
                grad = source
            else:
                grad = grad + source * geo[m, q : q + 1, :]
                dgeo[m, q : q + 1, :] += cut * jnp.sum(source * part, axis=0, keepdims=True)
        dgeo[0, q : q + 1, :] += norm * jnp.sum(grad * part, axis=0, keepdims=True)
        columns.append(grad * cut)
    return jnp.concatenate(columns, 1)


def middle_back_kernel(*refs, group, per, norm, aliased, first):
    geo, nbrs, own, low, high, dgeo_in, dx, dval, emb, g, slope, val, ev_w, back_w = refs[:14]
    wide_in, across_in = refs[14:16] if aliased else (None, None)
    dx_out, dval_out, dgeo, wide, across, total, dg = refs[14 + aliased :]
    step = pl.program_id(0)

    @pl.when(step == 0)
    def _():
        wide[...] = wide_in[...] if aliased else jnp.zeros_like(wide)
        across[...] = across_in[...] if aliased else jnp.zeros_like(across)

    @pl.when(step % per == 0)
    def _():
        total[...] = own[...] + low[...] + high[...]

    chosen = mark_atoms(nbrs, first + step // per, wide.shape[1] + across.shape[1])
    dgeo[...] = dgeo_in[...]
    demb = pull_env(geo, group, total, emb, dgeo, norm)
    d_fresh = dx[...] + product(ev_w[1], jnp.concatenate([demb, dval[...]], 0))
    pulled = product(back_w[0], d_fresh * slope[...])
    dx_out[...] = d_fresh + pulled[:LATENT]
    dval_out[...] = pull_mixed(
        geo, group, g, val[...], pulled[LATENT:], chosen, dgeo, wide, across, dg
    )


def middle_back(
    geo, nbrs, grads, dgeo, dx, dval, emb, g, slope, val, ev_w, back_w, slots, group, span, before
):
    edges = dx.shape[1]
    per = slots // group
    first = span[0] * per
    rows = HARM * TENSORS
    atoms = geo.shape[1] // slots * UNIT
    aliased = len(before)
    shapes = [
        edge_shape(LATENT, edges),
        edge_shape(TENSORS, edges),
        jax.ShapeDtypeStruct((HARM,) + geo.shape[1:], F32),
        edge_shape(rows, 3 * atoms),
        edge_shape(rows, atoms),
    ]
    extra = [*before[3:], *before[:3]]
    return pl.pallas_call(
        partial(
            middle_back_kernel, group=group, per=per, norm=1.0 / math.sqrt(slots), aliased=aliased,
            first=span[0],
        ),
        grid=((span[1] - span[0]) * per,),
        out_shape=shapes,
        in_specs=[row_spec(18, group, first), index_spec(group, first)]
        + [unit_spec(rows, per)] * 3
        + [row_spec(HARM, group, first)]
        + [
            edge_spec(r, group, first)
            for r in (LATENT, TENSORS, TENSORS, rows, LATENT, TENSORS)
        ]
        + [WHOLE] * 2
        + ([WHOLE] * 2 + [pl.BlockSpec(memory_space=pl.ANY)] * 3 if before else []),
        out_specs=[
            edge_spec(LATENT, group, first),
            edge_spec(TENSORS, group, first),
            row_spec(HARM, group, first),
            WHOLE,
            WHOLE,
        ],
        scratch_shapes=[
            pltpu.VMEM((rows, UNIT), F32),
            pltpu.VMEM((2 * rows, group * UNIT), BF16),
        ],
        input_output_aliases={16 + n: n for n in range(3)} if before else {},
        compiler_params=params(),
        cost_estimate=effort(8 * rows * edges * edges // slots),
        name="middle_back",
    )(geo, nbrs, *grads, dgeo, dx, dval, emb, g, slope, val, ev_w, back_w, *extra)


def first_back_kernel(
    geo, own, low, high, dgeo_in, dx, dval, emb, slope, ev_w, rad_w, *rest, group, per, norm
):
    dgeo, total = rest[-2:]
    step = pl.program_id(0)

    @pl.when(step % per == 0)
    def _():
        total[...] = own[...] + low[...] + high[...]

    dgeo[0:HARM] = dgeo_in[...]
    demb = pull_env(geo, group, total, emb, dgeo, norm)
    d_fresh = dx[...] + product(ev_w[0], jnp.concatenate([demb, dval[...]], 0))
    radial = product(rad_w[...], d_fresh * slope[...])
    for q in range(group):
        for n in range(BASIS):
            dgeo[HARM + n, q : q + 1, :] = radial[n : n + 1, lanes_of(q)]


def first_back(
    geo, grads, dgeo, dx, dval, emb, slope, ev_w, rad_w, slots, group, span, before
):
    per = slots // group
    first = span[0] * per
    rows = HARM * TENSORS
    return pl.pallas_call(
        partial(first_back_kernel, group=group, per=per, norm=1.0 / math.sqrt(slots)),
        grid=((span[1] - span[0]) * per,),
        out_shape=jax.ShapeDtypeStruct((HARM + BASIS,) + geo.shape[1:], F32),
        in_specs=[row_spec(18, group, first)]
        + [unit_spec(rows, per)] * 3
        + [row_spec(HARM, group, first)]
        + [edge_spec(r, group, first) for r in (LATENT, TENSORS, TENSORS, LATENT)]
        + [WHOLE] * 2
        + [pl.BlockSpec(memory_space=pl.ANY)] * len(before),
        out_specs=row_spec(HARM + BASIS, group, first),
        scratch_shapes=[pltpu.VMEM((rows, UNIT), F32)],
        input_output_aliases={11 + n: n for n in range(len(before))},
        compiler_params=params(),
        cost_estimate=effort(64 * LATENT * LATENT * dx.shape[1]),
        name="first_back",
    )(geo, *grads, dgeo, dx, dval, emb, slope, ev_w, rad_w, *before)


def geometry_back_kernel(vec, dgeo, nbrs, wide_out, across_out, dvec, *, slots):
    rows_total = vec.shape[1]
    units = rows_total // slots
    for group in range(rows_total // 8):
        up = slice(group * 8, group * 8 + 8)
        vx, vy, vz = (vec[axis, up, :] for axis in range(3))
        inverse, cut, slope, sine, cosine = distances(vx, vy, vz)
        ux, uy, uz = vx * inverse, vy * inverse, vz * inverse
        _, h1, h2, h3, h4, h5, h6, h7, h8 = (dgeo[m, up, :] for m in range(HARM))
        dux = h1 + ROOT3 * (uy * h4 + uz * h7 + ux * h8)
        duy = h2 + ROOT3 * (ux * h4 + uz * h5 - uy * h8)
        duz = h3 + ROOT3 * (uy * h5 + ux * h7) + 3.0 * uz * h6
        along = ux * dux + uy * duy + uz * duz
        scale = math.sqrt(2.0 / CUTOFF) * inverse
        by_wave = jnp.zeros_like(sine)
        by_angle = jnp.zeros_like(sine)
        before, now = jnp.zeros_like(sine), sine
        before_c, now_c = jnp.ones_like(sine), cosine
        for n in range(BASIS):
            pulled = dgeo[HARM + n, up, :]
            by_wave = by_wave + pulled * now
            by_angle = by_angle + (n + 1.0) * (pulled * now_c)
            before, now = now, 2.0 * cosine * now - before
            before_c, now_c = now_c, 2.0 * cosine * now_c - before_c
        d_dist = slope * dgeo[0, up, :] + scale * (
            (math.pi / CUTOFF) * by_angle * cut + by_wave * (slope - inverse * cut)
        )
        dvec[0, up, :] = (dux - ux * along) * inverse + ux * d_dist
        dvec[1, up, :] = (duy - uy * along) * inverse + uy * d_dist
        dvec[2, up, :] = (duz - uz * along) * inverse + uz * d_dist
    total = jnp.zeros((2 * 48, UNIT), F32)
    rows = lax.broadcasted_iota(jnp.int32, (16, UNIT), 0)
    lane = lax.broadcasted_iota(jnp.int32, (UNIT, UNIT), 0)
    for group in range(rows_total // 4):
        spreads, picks = [], []
        for k in range(group * 4, group * 4 + 4):
            index = nbrs[k : k + 1, :]
            here = rows == lax.shift_right_arithmetic(index, 7)
            spreads.append(
                jnp.concatenate(
                    [jnp.where(here, dvec[axis, k : k + 1, :], 0.0) for axis in range(3)], 0
                )
            )
            picks.append((lane == (index & 127)).astype(F32).astype(BF16))
        spread = jnp.concatenate(spreads, 1)
        total = total + dot_nt(stacked(spread), jnp.concatenate(picks, 1))
    total = total[:48] + total[48:]
    wide_out[...] = jnp.zeros_like(wide_out)
    across_out[...] = jnp.zeros_like(across_out)
    for axis in range(3):
        for block in range(4 * units):
            row = axis * 16 + block
            out, place = (wide_out, block) if block < 3 * units else (across_out, block - 3 * units)
            out[axis : axis + 1, lanes_of(place)] = total[row : row + 1]
        for unit in range(units):
            part = dvec[axis, unit * slots : (unit + 1) * slots, :]
            wide_out[axis : axis + 1, lanes_of(unit)] -= jnp.sum(part, axis=0, keepdims=True)


def geometry_back(vec, dgeo, nbrs, slots):
    atoms = vec.shape[1] // slots * UNIT
    return pl.pallas_call(
        partial(geometry_back_kernel, slots=slots),
        out_shape=[edge_shape(8, 3 * atoms), edge_shape(8, atoms)],
        in_specs=[WHOLE] * 3,
        out_specs=[WHOLE] * 2,
        scratch_shapes=[pltpu.VMEM(vec.shape, F32)],
        compiler_params=params(),
        name="geometry_back",
    )(vec, dgeo, nbrs)


def swap_y(rows, face):
    if lax.axis_size("gy") == 2:
        return passed_along(rows, "gy", 1)
    up = passed_along(rows[:, :face], "gy", 1)
    down = passed_along(rows[:, face:], "gy", -1)
    return jnp.concatenate([up, down], 1)


def return_y(rows, face):
    if lax.axis_size("gy") == 2:
        return passed_along(rows, "gy", 1)
    up = passed_along(rows[:, :face], "gy", -1)
    down = passed_along(rows[:, face:], "gy", 1)
    return jnp.concatenate([up, down], 1)


def ghost_rows(parts, wanted, face):
    below, above = [], []
    for part in parts:
        if below:
            part, below[-1], above[-1] = lax.optimization_barrier((part, below[-1], above[-1]))
        below.append(passed_along(part, "gx", 1))
        above.append(passed_along(part, "gx", -1))
    pieces = [*parts, *below, *above]
    return pieces + [swap_y(lend_env(wanted, pieces), face)]


def owned_grads(wide, across, wanted, face, widths, total, steps, hops):
    across, total = lax.optimization_barrier((across, total))
    returned = return_y(across, face)
    for _ in range(hops):
        total = sum_step(total, steps)
    own, below, above = take_back(returned, wanted, wide, widths)
    found = []
    for number in range(len(widths)):
        send = below[number], above[number]
        if found:
            send, found[-1], total = lax.optimization_barrier((send, found[-1], total))
        found.append(
            [own[number], passed_along(send[0], "gx", -1), passed_along(send[1], "gx", 1)]
        )
    return found, total


def sum_steps():
    count = lax.axis_size("gx")
    if count & (count - 1) or lax.axis_size("gy") != 2:
        return None
    return [("gx", 1 << n) for n in range(count.bit_length() - 1)] + [("gy", 1)]


def sum_step(total, steps):
    if steps:
        axis, by = steps.pop(0)
        total = total + passed_along(total, axis, by)
    return total


def per_device(
    positions,
    species,
    neighbours,
    send_x,
    send_y,
    two_weight,
    two_bias,
    env_weight,
    value_weight,
    latent_weight,
    latent_bias,
    out_weight,
    species_shift,
):
    group = 16
    nbrs = neighbours[0, 0]
    atoms = nbrs.shape[1]
    face = send_y.shape[3]
    rows, wanted = pack_rows(positions[0, 0], species[0], send_x[0, 0], send_y[0, 0])
    below = passed_along(rows, "gx", 1)
    above = passed_along(rows, "gx", -1)
    two_w, mix_w, s_w, back_w, ev_w, rad_w, cols = prepare_weights(
        two_weight, two_bias, env_weight, value_weight, latent_weight, latent_bias, out_weight
    )
    lent, wanted = lend_rows(rows, below, above, wanted)
    across = swap_y(lent, face)
    slots = nbrs.shape[0]
    units = atoms // UNIT
    vec, geo, nbrs, base = geometry(rows, below, above, across, nbrs, species_shift, face)
    parts, before = [], []
    for span in ((0, 1), (1, units)):
        *before, part = first_pass(
            geo, rows, two_w, mix_w, cols, slots, group, span, before
        )
        parts.append(part)
    x0, slope_a, emb0, val0, lx0 = before
    pieces = ghost_rows(parts, wanted, face)
    parts, before = [], []
    for span in ((0, units - 1), (units - 1, units)):
        *before, part = middle_pass(
            geo, nbrs, pieces, x0, lx0, val0, s_w, mix_w, cols, slots, group, span, before
        )
        parts.append(part)
    g0, slope0, x1, emb1, val1, lx1 = before
    pieces = ghost_rows(parts, wanted, face)
    energy, total, dx, dval, dgeo, wide, across = last_pass(
        geo, nbrs, pieces, x1, lx1, val1, s_w, back_w, cols, base, slots, group
    )
    steps = sum_steps()
    if steps is None:
        total = lax.psum(total, ("gx", "gy"))
    grads, total = owned_grads(wide, across, wanted, face, (UNIT, atoms - UNIT), total, steps, 1)
    before = []
    for number, span in enumerate(((0, 1), (1, units))):
        before = middle_back(
            geo, nbrs, grads[number], dgeo, dx, dval, emb1, g0, slope0, val0, ev_w, back_w,
            slots, group, span, before,
        )
    dx, dval, dgeo, wide, across = before
    grads, total = owned_grads(wide, across, wanted, face, (atoms - UNIT, UNIT), total, steps, 2)
    before = []
    for number, span in enumerate(((0, units - 1), (units - 1, units))):
        before = [
            first_back(
                geo, grads[number], dgeo, dx, dval, emb0, slope_a, ev_w, rad_w, slots, group,
                span, before,
            )
        ]
    wide, across = geometry_back(vec, before[0], nbrs, slots)
    grads, total = owned_grads(wide, across, wanted, face, (atoms,), total, steps, 1)
    while steps:
        total = sum_step(total, steps)
    mean_energy = jnp.sum(total) / (atoms * lax.axis_size("gx") * lax.axis_size("gy"))
    forces = -(grads[0][0] + grads[0][1] + grads[0][2])[:3]
    return (energy[None], forces[None, None], mean_energy.reshape(1))


def solution(mesh):
    placed = (
        P(("groups", "gx"), "gy", None, None),
        P(("groups", "gx"), "gy", None),
        P(("groups", "gx"), "gy", None, None),
        P(("groups", "gx"), "gy", None, None),
        P(("groups", "gx"), "gy", None, None),
        P(),
        P(),
        P(),
        P(),
        P(),
        P(),
        P(),
        P(),
    )
    return jax.shard_map(
        per_device,
        mesh=mesh,
        in_specs=placed,
        out_specs=(
            P(("groups", "gx"), "gy", None),
            P(("groups", "gx"), "gy", None, None),
            P("groups"),
        ),
        check_vma=False,
    )
```

```python
from functools import partial
import math

import jax
import jax.numpy as jnp
from jax import lax
from jax.experimental import pallas as pl
from jax.experimental.pallas import tpu as pltpu
from jax.sharding import PartitionSpec as P

BASIS = 8
SPECIES = 5
SITES_X = 2
SITES_Y = 16
CUTOFF = 2.5
LATENT = 128
TENSORS = 32
HARM = 9
UNIT = 128
ROOT3 = math.sqrt(3.0)
DEGREE = (0, 1, 1, 1, 2, 2, 2, 2, 2)
F32 = jnp.float32
BF16 = jnp.bfloat16
WHOLE = pl.BlockSpec(memory_space=pltpu.VMEM)
SCALARS = pl.BlockSpec(memory_space=pltpu.SMEM)


def params(mib=28):
    return pltpu.CompilerParams(vmem_limit_bytes=mib << 20)


def passed_along(value, axis, by):
    count = lax.axis_size(axis)
    return lax.ppermute(value, axis, [(i, (i + by) % count) for i in range(count)])


def dot(a, b):
    return jnp.dot(a, b, preferred_element_type=F32)


def dot_nt(a, b):
    return lax.dot_general(a, b, (((1,), (1,)), ((), ())), preferred_element_type=F32)


def halves(value):
    high = value.astype(BF16)
    return high, (value - high.astype(F32)).astype(BF16)


def stacked(value):
    return jnp.concatenate(halves(value), 0)


def product(weights, value):
    rows = weights.shape[0] // 2
    both = dot(weights, stacked(value))
    return both[:rows] + both[rows:]


def rounded(value):
    high = value.astype(BF16).astype(F32)
    return high, value - high


def weights_kernel(two, bias, env, val, lat, lat_bias, out_w, *outs):
    two_out, mix_out, s_out, back_out, ev_out, rad_out, cols = outs

    def depth_stack(piece):
        high, low = rounded(piece)
        top = jnp.concatenate([high, high], 0)
        bottom = jnp.concatenate([low, jnp.zeros_like(low)], 0)
        return top.T, bottom.T

    def lane_stack(piece):
        high, low = rounded(piece)
        top = jnp.concatenate([high, high], 1)
        return top, jnp.concatenate([low, jnp.zeros_like(low)], 1)

    def join(pieces):
        tops, bottoms = zip(*pieces)
        return jnp.concatenate(list(tops) + list(bottoms), 0).astype(BF16)

    def wide_stack(piece):
        return jnp.concatenate(lane_stack(piece), 0).astype(BF16)

    width = two.shape[1]
    first = jnp.concatenate(
        [
            two[0:SPECIES, :],
            bias[...],
            jnp.zeros((2, width), F32),
            two[SPECIES : 2 * SPECIES, :],
            jnp.zeros((3, width), F32),
            two[2 * SPECIES :, :],
        ],
        0,
    )
    two_out[...] = join([depth_stack(first)])
    rad_out[...] = wide_stack(two[2 * SPECIES :, :])
    for layer in range(env.shape[0]):
        latent = lat[layer]
        mix_out[layer] = join(
            [lane_stack(env[layer]), lane_stack(val[layer]), depth_stack(latent[:width])]
        )
        s_out[layer] = join([depth_stack(latent[width:])])
        back_out[layer] = wide_stack(latent)
        high = [rounded(env[layer]), rounded(val[layer])]
        top = jnp.concatenate([high[0][0], high[1][0]] * 2, 0).T
        bottom = jnp.concatenate([high[0][1], high[1][1]] + [jnp.zeros_like(high[0][1])] * 2, 0).T
        ev_out[layer] = jnp.concatenate([top, bottom], 0).astype(BF16)
    columns = jnp.concatenate(
        [lat_bias[...], out_w[...], jnp.zeros((8 - lat_bias.shape[0] - 1, width), F32)], 0
    )
    cols[...] = columns.T


def prepare_weights(two, bias, env, val, lat, lat_bias, out_w):
    layers = env.shape[0]
    shapes = [
        (2 * LATENT, 48),
        (layers, 2 * (LATENT + 2 * TENSORS), 2 * LATENT),
        (layers, 2 * LATENT, 6 * TENSORS),
        (layers, 2 * (LATENT + 3 * TENSORS), 2 * LATENT),
        (layers, 2 * LATENT, 4 * TENSORS),
        (2 * BASIS, 2 * LATENT),
    ]
    out_shape = [jax.ShapeDtypeStruct(s, BF16) for s in shapes]
    out_shape.append(jax.ShapeDtypeStruct((LATENT, 8), F32))
    return pl.pallas_call(
        weights_kernel,
        out_shape=out_shape,
        in_specs=[WHOLE] * 7,
        out_specs=[WHOLE] * 7,
        compiler_params=params(),
        name="prepare_weights",
    )(two, bias[None], env.swapaxes(1, 2), val.swapaxes(1, 2), lat, lat_bias, out_w[None])


def shifted(rows, by_x, by_y):
    lane_row = lax.broadcasted_iota(jnp.int32, rows.shape, 0)
    return rows + jnp.where(lane_row == 0, by_x, jnp.where(lane_row == 1, by_y, 0.0))


def lane_pick(table, row, index, blocks):
    low = index & 127
    high = lax.shift_right_arithmetic(index, 7)
    found = jnp.zeros(index.shape, F32)
    for block in range(blocks):
        span = slice(block * 128, block * 128 + 128)
        source = table[...][:, span] if row is None else table[row : row + 1, span]
        source = jnp.broadcast_to(source, index.shape)
        taken = jnp.take_along_axis(source, low, axis=1)
        found = jnp.where(high == block, taken, found)
    return found


def fill_wide(own, below, above, table, remap):
    atoms = own.shape[1]
    table[:, 0:atoms] = own[...]
    table[:, atoms : 2 * atoms] = shifted(below[...], -float(SITES_X), 0.0)
    table[:, 2 * atoms : 3 * atoms] = shifted(above[...], float(SITES_X), 0.0)
    lanes = lax.broadcasted_iota(jnp.int32, (1, atoms), 1).astype(F32)
    remap[:, 0:atoms] = lanes
    remap[:, atoms : 2 * atoms] = below[5:6, :] + float(atoms)
    remap[:, 2 * atoms : 3 * atoms] = above[4:5, :] + float(2 * atoms)


def lend_kernel(own, below, above, wanted, rows_out, wanted_out, table, remap):
    atoms = own.shape[1]
    blocks = 3 * atoms // 128
    fill_wide(own, below, above, table, remap)
    for tile in range(wanted.shape[1] // 128):
        span = slice(tile * 128, tile * 128 + 128)
        index = jnp.broadcast_to(wanted[:, span], (8, 128))
        place = lane_pick(remap, 0, index, blocks).astype(jnp.int32)
        place = jnp.where(index < 0, -1, place)
        wanted_out[:, span] = place[0:1]
        rows_out[:, span] = lane_pick(table, None, place, blocks)


def pack_kernel(coords, species, lend_x, lend_y, rows, wanted):
    face = lend_y.shape[1]
    rows[...] = jnp.zeros_like(rows)
    rows[0:3, :] = coords[...]
    rows[3:4, :] = species[...].astype(F32)
    rows[4:6, :] = lend_x[...].astype(F32)
    wanted[...] = jnp.full(wanted.shape, -1, jnp.int32)
    wanted[:, 0:face] = lend_y[1:2, :]
    wanted[:, face : 2 * face] = lend_y[0:1, :]


def pack_rows(coords, species, lend_x, lend_y):
    atoms = coords.shape[1]
    return pl.pallas_call(
        pack_kernel,
        out_shape=[edge_shape(8, atoms), jax.ShapeDtypeStruct((1, atoms), jnp.int32)],
        in_specs=[WHOLE] * 4,
        out_specs=[WHOLE] * 2,
        compiler_params=params(),
        name="pack_rows",
    )(coords, species, lend_x, lend_y)


def lend_rows(own, below, above, wanted):
    atoms = own.shape[1]
    return pl.pallas_call(
        lend_kernel,
        out_shape=[
            jax.ShapeDtypeStruct(wanted.shape[:0] + (8, wanted.shape[1]), F32),
            jax.ShapeDtypeStruct(wanted.shape, jnp.int32),
        ],
        in_specs=[WHOLE] * 4,
        out_specs=[WHOLE] * 2,
        scratch_shapes=[pltpu.VMEM((8, 3 * atoms), F32), pltpu.VMEM((1, 3 * atoms), F32)],
        compiler_params=params(),
        name="lend_rows",
    )(own, below, above, wanted)


def distances(vx, vy, vz):
    dist = jnp.sqrt(vx * vx + vy * vy + vz * vz)
    inverse = 1.0 / dist
    scaled = jnp.minimum(dist * (1.0 / CUTOFF), 1.0)
    second = scaled * scaled
    fourth = second * second
    sixth = fourth * second
    cut = 1.0 - 28.0 * sixth + 48.0 * (sixth * scaled) - 21.0 * (sixth * second)
    rest = 1.0 - scaled
    slope = (-168.0 / CUTOFF) * (fourth * scaled) * (rest * rest)
    angle = scaled * math.pi
    return inverse, cut, slope, jnp.sin(angle), jnp.cos(angle)


def geometry_kernel(
    own, below, above, across, nbrs, shift, vec_out, geo_out, nbr_out, base_out, table, remap, face
):
    atoms = own.shape[1]
    slots = nbrs.shape[0]
    blocks = table.shape[1] // 128
    fill_wide(own, below, above, table, remap)
    lanes = lax.broadcasted_iota(jnp.int32, (8, atoms), 1)
    rows = lax.broadcasted_iota(jnp.int32, (8, atoms), 0)
    moved = across[...] + jnp.where(
        rows == 1, jnp.where(lanes < face, -float(SITES_Y), float(SITES_Y)), 0.0
    )
    empty = jnp.where(rows == 2, -1000.0, jnp.where(rows == 3, -1.0, 0.0))
    table[:, 3 * atoms : 4 * atoms] = jnp.where(lanes < 2 * face, moved, empty)
    remap[:, 3 * atoms : 4 * atoms] = (
        lax.broadcasted_iota(jnp.int32, (1, atoms), 1) + 3 * atoms
    ).astype(F32)
    base = jnp.zeros((1, atoms), F32)
    for kind in range(SPECIES):
        base = base + jnp.where(own[3:4, :] == float(kind), shift[kind], 0.0)
    base_out[...] = base
    for group in range(slots // 8):
        for tile in range(atoms // UNIT):
            span = slice(tile * UNIT, tile * UNIT + UNIT)
            index = nbrs[group * 8 : group * 8 + 8, span]
            up = slice(tile * slots + group * 8, tile * slots + group * 8 + 8)
            index = lane_pick(remap, 0, index, blocks).astype(jnp.int32)
            nbr_out[up, :] = index
            vx = lane_pick(table, 0, index, blocks) - own[0:1, span]
            vy = lane_pick(table, 1, index, blocks) - own[1:2, span]
            vz = lane_pick(table, 2, index, blocks) - own[2:3, span]
            kind = lane_pick(table, 3, index, blocks)
            vec_out[0, up, :] = vx
            vec_out[1, up, :] = vy
            vec_out[2, up, :] = vz
            inverse, cut, _, sine, cosine = distances(vx, vy, vz)
            ux, uy, uz = vx * inverse, vy * inverse, vz * inverse
            harm = [
                ux,
                uy,
                uz,
                ROOT3 * ux * uy,
                ROOT3 * uy * uz,
                0.5 * (3.0 * uz * uz - 1.0),
                ROOT3 * ux * uz,
                0.5 * ROOT3 * (ux * ux - uy * uy),
            ]
            geo_out[0, up, :] = cut
            for number, value in enumerate(harm):
                geo_out[1 + number, up, :] = value
            scale = math.sqrt(2.0 / CUTOFF) * inverse * cut
            before, now = jnp.zeros_like(sine), sine
            for number in range(BASIS):
                geo_out[9 + number, up, :] = now * scale
                before, now = now, 2.0 * cosine * now - before
            geo_out[17, up, :] = kind


def geometry(own, below, above, across, nbrs, shift, face):
    slots, atoms = nbrs.shape
    return pl.pallas_call(
        partial(geometry_kernel, face=face),
        out_shape=[
            jax.ShapeDtypeStruct((3, slots * atoms // UNIT, UNIT), F32),
            jax.ShapeDtypeStruct((18, slots * atoms // UNIT, UNIT), F32),
            jax.ShapeDtypeStruct((slots * atoms // UNIT, UNIT), jnp.int32),
            jax.ShapeDtypeStruct((1, atoms), F32),
        ],
        in_specs=[WHOLE] * 5 + [SCALARS],
        out_specs=[WHOLE] * 4,
        scratch_shapes=[pltpu.VMEM((8, 4 * atoms), F32), pltpu.VMEM((1, 4 * atoms), F32)],
        compiler_params=params(),
        name="geometry",
    )(own, below, above, across, nbrs, shift)


def silu_pair(pre):
    gate = 1.0 / (1.0 + jnp.exp(-pre))
    value = pre * gate
    return value, gate + value * (1.0 - gate)


def row_spec(count, group, first):
    return pl.BlockSpec((count, group, UNIT), lambda i: (0, first + i, 0))


def index_spec(group, first):
    return pl.BlockSpec((group, UNIT), lambda i: (first + i, 0))


def edge_spec(rows, group, first):
    return pl.BlockSpec((rows, group * UNIT), lambda i: (0, first + i))


def unit_spec(rows, per):
    return pl.BlockSpec((rows, UNIT), lambda i: (0, i // per))


def edge_shape(rows, edges):
    return jax.ShapeDtypeStruct((rows, edges), F32)


def lanes_of(q):
    return slice(q * UNIT, (q + 1) * UNIT)


def rows_of(m):
    return slice(m * TENSORS, (m + 1) * TENSORS)


def add_env(geo, step, per, group, embed, env_out, norm):
    @pl.when(step % per == 0)
    def _():
        env_out[...] = jnp.zeros_like(env_out)

    cuts = [geo[0, q : q + 1, :] * norm for q in range(group)]
    for m in range(HARM):
        total = env_out[rows_of(m), :]
        for q in range(group):
            factor = cuts[q] if m == 0 else cuts[q] * geo[m, q : q + 1, :]
            total = total + embed[:TENSORS, lanes_of(q)] * factor
        env_out[rows_of(m), :] = total


def first_kernel(
    geo, own, two_w, mix_w, cols, *outs, group, per, norm
):
    x_out, slope_out, emb_out, val_out, lx_out, env_out = outs[-6:]
    step = pl.program_id(0)
    kinds = lax.broadcasted_iota(jnp.int32, (8, UNIT), 0)
    kinds_f = kinds.astype(F32)
    centre = jnp.where((own[3:4, :] == kinds_f) & (kinds < SPECIES), 1.0, 0.0)
    centre = jnp.where(kinds == SPECIES, 1.0, centre)
    parts = []
    for q in range(group):
        other = jnp.where(geo[17, q : q + 1, :] == kinds_f, 1.0, 0.0)
        radial = [geo[9 + n, q : q + 1, :] for n in range(BASIS)]
        parts.append(jnp.concatenate([centre, other] + radial, 0))
    features = jnp.concatenate(parts, 1)
    x, slope = silu_pair(product(two_w[...], features))
    x_out[...] = x
    slope_out[...] = slope
    mixed = product(mix_w[0], x)
    emb_out[...] = mixed[:TENSORS]
    val_out[...] = mixed[TENSORS : 2 * TENSORS]
    lx_out[...] = mixed[2 * TENSORS :] + cols[:, 0:1]
    add_env(geo, step, per, group, mixed, env_out, norm)


def wide_unit_spec(rows, per, first):
    return pl.BlockSpec((rows, UNIT), lambda i: (0, first + i // per))


def first_pass(geo, own, two_w, mix_w, cols, slots, group, span, before):
    edges = geo.shape[1] * UNIT
    per = slots // group
    first = span[0] * per
    rows = (LATENT, LATENT, TENSORS, TENSORS, LATENT)
    return pl.pallas_call(
        partial(first_kernel, group=group, per=per, norm=1.0 / math.sqrt(slots)),
        grid=((span[1] - span[0]) * per,),
        out_shape=[edge_shape(r, edges) for r in rows]
        + [edge_shape(HARM * TENSORS, (span[1] - span[0]) * UNIT)],
        in_specs=[row_spec(18, group, first), wide_unit_spec(8, per, span[0])]
        + [WHOLE] * 3
        + [pl.BlockSpec(memory_space=pl.ANY)] * len(before),
        out_specs=[edge_spec(r, group, first) for r in rows]
        + [unit_spec(HARM * TENSORS, per)],
        input_output_aliases={5 + n: n for n in range(len(before))},
        compiler_params=params(),
        cost_estimate=effort(64 * LATENT * LATENT * edges),
        name="first_pass",
    )(geo, own, two_w, mix_w, cols, *before)


def chosen_rows(index, columns, start):
    rows = lax.broadcasted_iota(jnp.int32, (columns, index.shape[1]), 0) + start
    return (rows == index).astype(F32).astype(BF16)


def mark_atoms(nbrs, unit, columns):
    own = columns // 4
    centre = lax.broadcasted_iota(jnp.int32, (1, UNIT), 1) + unit * UNIT
    here = lax.broadcasted_iota(jnp.int32, (own, UNIT), 0)
    away = lax.broadcasted_iota(jnp.int32, (columns - own, UNIT), 0) + own
    parts = []
    for q in range(nbrs.shape[0]):
        index = nbrs[q : q + 1, :]
        top = (here == index).astype(F32) + (here == centre).astype(F32)
        rest = (away == index).astype(F32)
        parts.append(jnp.concatenate([top, rest], 0).astype(BF16))
    return jnp.concatenate(parts, 1)


def lend_env_kernel(wanted, *refs):
    out = refs[-1]
    rows = out.shape[0]
    total = jnp.zeros((2 * rows, out.shape[1]), F32)
    start = 0
    for block in refs[:-1]:
        chosen = chosen_rows(wanted[...], block.shape[1], start)
        total = total + dot(stacked(block[...]), chosen)
        start += block.shape[1]
    out[...] = total[:rows] + total[rows:]


def lend_env(wanted, pieces):
    return pl.pallas_call(
        lend_env_kernel,
        out_shape=jax.ShapeDtypeStruct((HARM * TENSORS, wanted.shape[1]), F32),
        in_specs=[WHOLE] * (1 + len(pieces)),
        out_specs=WHOLE,
        compiler_params=params(),
        name="lend_env",
    )(wanted, *pieces)


def take_back_kernel(returned, wanted, wide, *outs, widths):
    atoms = wide.shape[1] // 3
    rows = returned.shape[0]
    value = stacked(returned[...])
    for place in range(3):
        chosen = chosen_rows(wanted[...], atoms, place * atoms)
        both = dot_nt(value, chosen)
        total = wide[:, place * atoms : (place + 1) * atoms] + both[:rows] + both[rows:]
        start = 0
        for number, width in enumerate(widths):
            outs[place * len(widths) + number][...] = total[:, start : start + width]
            start += width


def take_back(returned, wanted, wide, widths):
    outs = pl.pallas_call(
        partial(take_back_kernel, widths=widths),
        out_shape=[edge_shape(wide.shape[0], w) for w in widths] * 3,
        in_specs=[WHOLE] * 3,
        out_specs=[WHOLE] * (3 * len(widths)),
        compiler_params=params(),
        name="take_back",
    )(returned, wanted, wide)
    count = len(widths)
    return [list(outs[place * count : (place + 1) * count]) for place in range(3)]


def fill_split(pieces, split):
    rows = pieces[0].shape[0]
    start = 0
    for block in pieces:
        span = slice(start, start + block.shape[1])
        high, low = halves(block[...])
        split[:rows, span] = high
        split[rows:, span] = low
        start += block.shape[1]


def gathered(split, chosen, g):
    rows = HARM * TENSORS
    both = dot(split[...], chosen)
    g[...] = both[:rows] + both[rows:]


def contracted(geo, group, g, value):
    columns = []
    for q in range(group):
        span = lanes_of(q)
        sums = [g[0:TENSORS, span], None, None]
        for m in range(1, HARM):
            term = g[rows_of(m), span] * geo[m, q : q + 1, :]
            d = DEGREE[m]
            sums[d] = term if sums[d] is None else sums[d] + term
        columns.append(jnp.concatenate([part * value[:, span] for part in sums], 0))
    return jnp.concatenate(columns, 1)


def middle_kernel(*refs, group, per, norm, count, aliased, first):
    geo, nbrs, x, lx, val, s_w, mix_w, cols = refs[:8]
    pieces = refs[8 : 8 + count]
    g, slope_out, x_out, emb_out, val_out, lx_out, env_out, split = refs[
        8 + count + aliased :
    ]
    step = pl.program_id(0)

    @pl.when(step == 0)
    def _():
        fill_split(pieces, split)

    chosen = mark_atoms(nbrs, first + step // per, split.shape[1])
    gathered(split, chosen, g)
    s = contracted(geo, group, g, val[...])
    update, slope = silu_pair(lx[...] + product(s_w[0], s))
    slope_out[...] = slope
    fresh = x[...] + update
    x_out[...] = fresh
    mixed = product(mix_w[1], fresh)
    emb_out[...] = mixed[:TENSORS]
    val_out[...] = mixed[TENSORS : 2 * TENSORS]
    lx_out[...] = mixed[2 * TENSORS :] + cols[:, 1:2]
    add_env(geo, step, per, group, mixed, env_out, norm)


def middle_pass(geo, nbrs, pieces, x, lx, val, s_w, mix_w, cols, slots, group, span, before):
    edges = x.shape[1]
    per = slots // group
    first = span[0] * per
    rows = (HARM * TENSORS, LATENT, LATENT, TENSORS, TENSORS, LATENT)
    ins = 8 + len(pieces)
    columns = sum(p.shape[1] for p in pieces)
    return pl.pallas_call(
        partial(
            middle_kernel, group=group, per=per, norm=1.0 / math.sqrt(slots),
            count=len(pieces), aliased=len(before), first=span[0],
        ),
        grid=((span[1] - span[0]) * per,),
        out_shape=[edge_shape(r, edges) for r in rows]
        + [edge_shape(HARM * TENSORS, (span[1] - span[0]) * UNIT)],
        in_specs=[row_spec(18, group, first), index_spec(group, first)]
        + [edge_spec(r, group, first) for r in (LATENT, LATENT, TENSORS)]
        + [WHOLE] * (3 + len(pieces))
        + [pl.BlockSpec(memory_space=pl.ANY)] * len(before),
        out_specs=[edge_spec(r, group, first) for r in rows]
        + [unit_spec(HARM * TENSORS, per)],
        scratch_shapes=[
            pltpu.VMEM((2 * HARM * TENSORS, columns), BF16),
        ],
        input_output_aliases={ins + n: n for n in range(len(before))},
        compiler_params=params(44),
        cost_estimate=effort(8 * HARM * TENSORS * edges * edges // slots),
        name="middle_pass",
    )(geo, nbrs, x, lx, val, s_w, mix_w, cols, *pieces, *before)


def effort(flops):
    return pl.CostEstimate(flops=flops, transcendentals=0, bytes_accessed=flops // 512)


def pull_mixed(geo, group, g, value, ds, chosen, dgeo, wide, across, dg):
    columns = []
    for q in range(group):
        span = lanes_of(q)
        part = value[:, span]
        pulled = [ds[rows_of(d), span] for d in range(3)]
        scaled = [p * part for p in pulled]
        total = None
        for m in range(HARM):
            d = DEGREE[m]
            source = g[rows_of(m), span]
            if m == 0:
                total = source * pulled[0]
                grad = scaled[0]
            else:
                harm = geo[m, q : q + 1, :]
                total = total + source * pulled[d] * harm
                dgeo[m, q : q + 1, :] += jnp.sum(source * scaled[d], axis=0, keepdims=True)
                grad = scaled[d] * harm
            high, low = halves(grad)
            dg[rows_of(m), span] = high
            dg[rows_of(HARM + m), span] = low
        columns.append(total)
    both = dot_nt(dg[...], chosen)
    rows = HARM * TENSORS
    total = both[:rows] + both[rows:]
    wide[...] += total[:, : wide.shape[1]]
    across[...] += total[:, wide.shape[1] :]
    return jnp.concatenate(columns, 1)


def last_kernel(*refs, group, per, norm, count):
    geo, nbrs, x, lx, val, s_w, back_w, cols, base = refs[:9]
    pieces = refs[9 : 9 + count]
    energy, esum, dx_out, dval_out, dgeo, wide, across, split, g, dg = refs[9 + count :]
    step = pl.program_id(0)

    @pl.when(step == 0)
    def _():
        fill_split(pieces, split)
        wide[...] = jnp.zeros_like(wide)
        across[...] = jnp.zeros_like(across)
        esum[...] = jnp.zeros_like(esum)

    @pl.when(step % per == 0)
    def _():
        energy[...] = base[...]

    chosen = mark_atoms(nbrs, step // per, split.shape[1])
    gathered(split, chosen, g)
    value = val[...]
    s = contracted(geo, group, g, value)
    update, slope = silu_pair(lx[...] + product(s_w[1], s))
    fresh = x[...] + update
    weight = cols[:, 2:3]
    read = jnp.sum(fresh * weight, axis=0, keepdims=True) * norm
    cuts = []
    dgeo[...] = jnp.zeros_like(dgeo)
    for q in range(group):
        cut = geo[0, q : q + 1, :]
        cuts.append(cut)
        energy[...] += read[:, lanes_of(q)] * cut
        dgeo[0, q : q + 1, :] = read[:, lanes_of(q)]

    @pl.when(step % per == per - 1)
    def _():
        esum[0:1, :] += energy[...]

    d_fresh = weight * (jnp.concatenate(cuts, 1) * norm)
    pulled = product(back_w[1], d_fresh * slope)
    dx_out[...] = d_fresh + pulled[:LATENT]
    dval_out[...] = pull_mixed(
        geo, group, g, value, pulled[LATENT:], chosen, dgeo, wide, across, dg
    )


def last_pass(geo, nbrs, pieces, x, lx, val, s_w, back_w, cols, base, slots, group):
    edges = x.shape[1]
    per = slots // group
    rows = HARM * TENSORS
    columns = sum(p.shape[1] for p in pieces)
    return pl.pallas_call(
        partial(
            last_kernel, group=group, per=per, norm=1.0 / math.sqrt(slots), count=len(pieces)
        ),
        grid=(geo.shape[1] // group,),
        out_shape=[
            jax.ShapeDtypeStruct(base.shape, F32),
            edge_shape(8, UNIT),
            edge_shape(LATENT, edges),
            edge_shape(TENSORS, edges),
            jax.ShapeDtypeStruct((HARM,) + geo.shape[1:], F32),
            edge_shape(rows, columns - base.shape[1]),
            edge_shape(rows, base.shape[1]),
        ],
        in_specs=[row_spec(18, group, 0), index_spec(group, 0)]
        + [edge_spec(r, group, 0) for r in (LATENT, LATENT, TENSORS)]
        + [WHOLE] * 3
        + [unit_spec(1, per)]
        + [WHOLE] * len(pieces),
        out_specs=[
            unit_spec(1, per),
            WHOLE,
            edge_spec(LATENT, group, 0),
            edge_spec(TENSORS, group, 0),
            row_spec(HARM, group, 0),
            WHOLE,
            WHOLE,
        ],
        scratch_shapes=[
            pltpu.VMEM((2 * rows, columns), BF16),
            pltpu.VMEM((rows, group * UNIT), F32),
            pltpu.VMEM((2 * rows, group * UNIT), BF16),
        ],
        compiler_params=params(44),
        cost_estimate=effort(16 * rows * edges * edges // slots),
        name="last_pass",
    )(geo, nbrs, x, lx, val, s_w, back_w, cols, base, *pieces)


def pull_env(geo, group, total, emb, dgeo, norm):
    columns = []
    for q in range(group):
        part = emb[:, lanes_of(q)]
        cut = geo[0, q : q + 1, :] * norm
        grad = None
        for m in range(HARM):
            source = total[rows_of(m), :]
            if m == 0:
                grad = source
            else:
                grad = grad + source * geo[m, q : q + 1, :]
                dgeo[m, q : q + 1, :] += cut * jnp.sum(source * part, axis=0, keepdims=True)
        dgeo[0, q : q + 1, :] += norm * jnp.sum(grad * part, axis=0, keepdims=True)
        columns.append(grad * cut)
    return jnp.concatenate(columns, 1)


def middle_back_kernel(*refs, group, per, norm, aliased, first):
    geo, nbrs, own, low, high, dgeo_in, dx, dval, emb, g, slope, val, ev_w, back_w = refs[:14]
    wide_in, across_in = refs[14:16] if aliased else (None, None)
    dx_out, dval_out, dgeo, wide, across, total, dg = refs[14 + aliased :]
    step = pl.program_id(0)

    @pl.when(step == 0)
    def _():
        wide[...] = wide_in[...] if aliased else jnp.zeros_like(wide)
        across[...] = across_in[...] if aliased else jnp.zeros_like(across)

    @pl.when(step % per == 0)
    def _():
        total[...] = own[...] + low[...] + high[...]

    chosen = mark_atoms(nbrs, first + step // per, wide.shape[1] + across.shape[1])
    dgeo[...] = dgeo_in[...]
    demb = pull_env(geo, group, total, emb, dgeo, norm)
    d_fresh = dx[...] + product(ev_w[1], jnp.concatenate([demb, dval[...]], 0))
    pulled = product(back_w[0], d_fresh * slope[...])
    dx_out[...] = d_fresh + pulled[:LATENT]
    dval_out[...] = pull_mixed(
        geo, group, g, val[...], pulled[LATENT:], chosen, dgeo, wide, across, dg
    )


def middle_back(
    geo, nbrs, grads, dgeo, dx, dval, emb, g, slope, val, ev_w, back_w, slots, group, span, before
):
    edges = dx.shape[1]
    per = slots // group
    first = span[0] * per
    rows = HARM * TENSORS
    atoms = geo.shape[1] // slots * UNIT
    aliased = len(before)
    shapes = [
        edge_shape(LATENT, edges),
        edge_shape(TENSORS, edges),
        jax.ShapeDtypeStruct((HARM,) + geo.shape[1:], F32),
        edge_shape(rows, 3 * atoms),
        edge_shape(rows, atoms),
    ]
    extra = [*before[3:], *before[:3]]
    return pl.pallas_call(
        partial(
            middle_back_kernel, group=group, per=per, norm=1.0 / math.sqrt(slots), aliased=aliased,
            first=span[0],
        ),
        grid=((span[1] - span[0]) * per,),
        out_shape=shapes,
        in_specs=[row_spec(18, group, first), index_spec(group, first)]
        + [unit_spec(rows, per)] * 3
        + [row_spec(HARM, group, first)]
        + [
            edge_spec(r, group, first)
            for r in (LATENT, TENSORS, TENSORS, rows, LATENT, TENSORS)
        ]
        + [WHOLE] * 2
        + ([WHOLE] * 2 + [pl.BlockSpec(memory_space=pl.ANY)] * 3 if before else []),
        out_specs=[
            edge_spec(LATENT, group, first),
            edge_spec(TENSORS, group, first),
            row_spec(HARM, group, first),
            WHOLE,
            WHOLE,
        ],
        scratch_shapes=[
            pltpu.VMEM((rows, UNIT), F32),
            pltpu.VMEM((2 * rows, group * UNIT), BF16),
        ],
        input_output_aliases={16 + n: n for n in range(3)} if before else {},
        compiler_params=params(44),
        cost_estimate=effort(8 * rows * edges * edges // slots),
        name="middle_back",
    )(geo, nbrs, *grads, dgeo, dx, dval, emb, g, slope, val, ev_w, back_w, *extra)


def first_back_kernel(
    geo, own, low, high, dgeo_in, dx, dval, emb, slope, ev_w, rad_w, *rest, group, per, norm
):
    dgeo, total = rest[-2:]
    step = pl.program_id(0)

    @pl.when(step % per == 0)
    def _():
        total[...] = own[...] + low[...] + high[...]

    dgeo[0:HARM] = dgeo_in[...]
    demb = pull_env(geo, group, total, emb, dgeo, norm)
    d_fresh = dx[...] + product(ev_w[0], jnp.concatenate([demb, dval[...]], 0))
    radial = product(rad_w[...], d_fresh * slope[...])
    for q in range(group):
        for n in range(BASIS):
            dgeo[HARM + n, q : q + 1, :] = radial[n : n + 1, lanes_of(q)]


def first_back(
    geo, grads, dgeo, dx, dval, emb, slope, ev_w, rad_w, slots, group, span, before
):
    per = slots // group
    first = span[0] * per
    rows = HARM * TENSORS
    return pl.pallas_call(
        partial(first_back_kernel, group=group, per=per, norm=1.0 / math.sqrt(slots)),
        grid=((span[1] - span[0]) * per,),
        out_shape=jax.ShapeDtypeStruct((HARM + BASIS,) + geo.shape[1:], F32),
        in_specs=[row_spec(18, group, first)]
        + [unit_spec(rows, per)] * 3
        + [row_spec(HARM, group, first)]
        + [edge_spec(r, group, first) for r in (LATENT, TENSORS, TENSORS, LATENT)]
        + [WHOLE] * 2
        + [pl.BlockSpec(memory_space=pl.ANY)] * len(before),
        out_specs=row_spec(HARM + BASIS, group, first),
        scratch_shapes=[pltpu.VMEM((rows, UNIT), F32)],
        input_output_aliases={11 + n: n for n in range(len(before))},
        compiler_params=params(),
        cost_estimate=effort(64 * LATENT * LATENT * dx.shape[1]),
        name="first_back",
    )(geo, *grads, dgeo, dx, dval, emb, slope, ev_w, rad_w, *before)


def geometry_back_kernel(vec, dgeo, nbrs, wide_out, across_out, dvec, *, slots):
    rows_total = vec.shape[1]
    units = rows_total // slots
    for group in range(rows_total // 8):
        up = slice(group * 8, group * 8 + 8)
        vx, vy, vz = (vec[axis, up, :] for axis in range(3))
        inverse, cut, slope, sine, cosine = distances(vx, vy, vz)
        ux, uy, uz = vx * inverse, vy * inverse, vz * inverse
        _, h1, h2, h3, h4, h5, h6, h7, h8 = (dgeo[m, up, :] for m in range(HARM))
        dux = h1 + ROOT3 * (uy * h4 + uz * h7 + ux * h8)
        duy = h2 + ROOT3 * (ux * h4 + uz * h5 - uy * h8)
        duz = h3 + ROOT3 * (uy * h5 + ux * h7) + 3.0 * uz * h6
        along = ux * dux + uy * duy + uz * duz
        scale = math.sqrt(2.0 / CUTOFF) * inverse
        by_wave = jnp.zeros_like(sine)
        by_angle = jnp.zeros_like(sine)
        before, now = jnp.zeros_like(sine), sine
        before_c, now_c = jnp.ones_like(sine), cosine
        for n in range(BASIS):
            pulled = dgeo[HARM + n, up, :]
            by_wave = by_wave + pulled * now
            by_angle = by_angle + (n + 1.0) * (pulled * now_c)
            before, now = now, 2.0 * cosine * now - before
            before_c, now_c = now_c, 2.0 * cosine * now_c - before_c
        d_dist = slope * dgeo[0, up, :] + scale * (
            (math.pi / CUTOFF) * by_angle * cut + by_wave * (slope - inverse * cut)
        )
        dvec[0, up, :] = (dux - ux * along) * inverse + ux * d_dist
        dvec[1, up, :] = (duy - uy * along) * inverse + uy * d_dist
        dvec[2, up, :] = (duz - uz * along) * inverse + uz * d_dist
    total = jnp.zeros((2 * 48, UNIT), F32)
    rows = lax.broadcasted_iota(jnp.int32, (16, UNIT), 0)
    lane = lax.broadcasted_iota(jnp.int32, (UNIT, UNIT), 0)
    for group in range(rows_total // 4):
        spreads, picks = [], []
        for k in range(group * 4, group * 4 + 4):
            index = nbrs[k : k + 1, :]
            here = rows == lax.shift_right_arithmetic(index, 7)
            spreads.append(
                jnp.concatenate(
                    [jnp.where(here, dvec[axis, k : k + 1, :], 0.0) for axis in range(3)], 0
                )
            )
            picks.append((lane == (index & 127)).astype(F32).astype(BF16))
        spread = jnp.concatenate(spreads, 1)
        total = total + dot_nt(stacked(spread), jnp.concatenate(picks, 1))
    total = total[:48] + total[48:]
    wide_out[...] = jnp.zeros_like(wide_out)
    across_out[...] = jnp.zeros_like(across_out)
    for axis in range(3):
        for block in range(4 * units):
            row = axis * 16 + block
            out, place = (wide_out, block) if block < 3 * units else (across_out, block - 3 * units)
            out[axis : axis + 1, lanes_of(place)] = total[row : row + 1]
        for unit in range(units):
            part = dvec[axis, unit * slots : (unit + 1) * slots, :]
            wide_out[axis : axis + 1, lanes_of(unit)] -= jnp.sum(part, axis=0, keepdims=True)


def geometry_back(vec, dgeo, nbrs, slots):
    atoms = vec.shape[1] // slots * UNIT
    return pl.pallas_call(
        partial(geometry_back_kernel, slots=slots),
        out_shape=[edge_shape(8, 3 * atoms), edge_shape(8, atoms)],
        in_specs=[WHOLE] * 3,
        out_specs=[WHOLE] * 2,
        scratch_shapes=[pltpu.VMEM(vec.shape, F32)],
        compiler_params=params(),
        name="geometry_back",
    )(vec, dgeo, nbrs)


def swap_y(rows, face):
    if lax.axis_size("gy") == 2:
        return passed_along(rows, "gy", 1)
    up = passed_along(rows[:, :face], "gy", 1)
    down = passed_along(rows[:, face:], "gy", -1)
    return jnp.concatenate([up, down], 1)


def return_y(rows, face):
    if lax.axis_size("gy") == 2:
        return passed_along(rows, "gy", 1)
    up = passed_along(rows[:, :face], "gy", -1)
    down = passed_along(rows[:, face:], "gy", 1)
    return jnp.concatenate([up, down], 1)


def ghost_rows(parts, wanted, face):
    below, above = [], []
    for part in parts:
        if below:
            part, below[-1], above[-1] = lax.optimization_barrier((part, below[-1], above[-1]))
        below.append(passed_along(part, "gx", 1))
        above.append(passed_along(part, "gx", -1))
    pieces = [*parts, *below, *above]
    return pieces + [swap_y(lend_env(wanted, pieces), face)]


def owned_grads(wide, across, wanted, face, widths, total, steps, hops):
    across, total = lax.optimization_barrier((across, total))
    returned = return_y(across, face)
    for _ in range(hops):
        total = sum_step(total, steps)
    own, below, above = take_back(returned, wanted, wide, widths)
    found = []
    for number in range(len(widths)):
        send = below[number], above[number]
        if found:
            send, found[-1], total = lax.optimization_barrier((send, found[-1], total))
        found.append(
            [own[number], passed_along(send[0], "gx", -1), passed_along(send[1], "gx", 1)]
        )
    return found, total


def sum_steps():
    count = lax.axis_size("gx")
    if count & (count - 1) or lax.axis_size("gy") != 2:
        return None
    return [("gx", 1 << n) for n in range(count.bit_length() - 1)] + [("gy", 1)]


def sum_step(total, steps):
    if steps:
        axis, by = steps.pop(0)
        total = total + passed_along(total, axis, by)
    return total


def per_device(
    positions,
    species,
    neighbours,
    send_x,
    send_y,
    two_weight,
    two_bias,
    env_weight,
    value_weight,
    latent_weight,
    latent_bias,
    out_weight,
    species_shift,
):
    group = 16
    nbrs = neighbours[0, 0]
    atoms = nbrs.shape[1]
    face = send_y.shape[3]
    rows, wanted = pack_rows(positions[0, 0], species[0], send_x[0, 0], send_y[0, 0])
    below = passed_along(rows, "gx", 1)
    above = passed_along(rows, "gx", -1)
    two_w, mix_w, s_w, back_w, ev_w, rad_w, cols = prepare_weights(
        two_weight, two_bias, env_weight, value_weight, latent_weight, latent_bias, out_weight
    )
    lent, wanted = lend_rows(rows, below, above, wanted)
    across = swap_y(lent, face)
    slots = nbrs.shape[0]
    units = atoms // UNIT
    vec, geo, nbrs, base = geometry(rows, below, above, across, nbrs, species_shift, face)
    parts, before = [], []
    for span in ((0, 1), (1, units)):
        *before, part = first_pass(
            geo, rows, two_w, mix_w, cols, slots, group, span, before
        )
        parts.append(part)
    x0, slope_a, emb0, val0, lx0 = before
    pieces = ghost_rows(parts, wanted, face)
    parts, before = [], []
    for span in ((0, units - 1), (units - 1, units)):
        *before, part = middle_pass(
            geo, nbrs, pieces, x0, lx0, val0, s_w, mix_w, cols, slots, group, span, before
        )
        parts.append(part)
    g0, slope0, x1, emb1, val1, lx1 = before
    pieces = ghost_rows(parts, wanted, face)
    energy, total, dx, dval, dgeo, wide, across = last_pass(
        geo, nbrs, pieces, x1, lx1, val1, s_w, back_w, cols, base, slots, group
    )
    steps = sum_steps()
    if steps is None:
        total = lax.psum(total, ("gx", "gy"))
    grads, total = owned_grads(wide, across, wanted, face, (UNIT, atoms - UNIT), total, steps, 1)
    before = []
    for number, span in enumerate(((0, 1), (1, units))):
        before = middle_back(
            geo, nbrs, grads[number], dgeo, dx, dval, emb1, g0, slope0, val0, ev_w, back_w,
            slots, group, span, before,
        )
    dx, dval, dgeo, wide, across = before
    grads, total = owned_grads(wide, across, wanted, face, (atoms - UNIT, UNIT), total, steps, 2)
    before = []
    for number, span in enumerate(((0, units - 1), (units - 1, units))):
        before = [
            first_back(
                geo, grads[number], dgeo, dx, dval, emb0, slope_a, ev_w, rad_w, slots, group,
                span, before,
            )
        ]
    wide, across = geometry_back(vec, before[0], nbrs, slots)
    grads, total = owned_grads(wide, across, wanted, face, (atoms,), total, steps, 1)
    while steps:
        total = sum_step(total, steps)
    mean_energy = jnp.sum(total) / (atoms * lax.axis_size("gx") * lax.axis_size("gy"))
    forces = -(grads[0][0] + grads[0][1] + grads[0][2])[:3]
    return (energy[None], forces[None, None], mean_energy.reshape(1))


def solution(mesh):
    placed = (
        P(("groups", "gx"), "gy", None, None),
        P(("groups", "gx"), "gy", None),
        P(("groups", "gx"), "gy", None, None),
        P(("groups", "gx"), "gy", None, None),
        P(("groups", "gx"), "gy", None, None),
        P(),
        P(),
        P(),
        P(),
        P(),
        P(),
        P(),
        P(),
    )
    return jax.shard_map(
        per_device,
        mesh=mesh,
        in_specs=placed,
        out_specs=(
            P(("groups", "gx"), "gy", None),
            P(("groups", "gx"), "gy", None, None),
            P("groups"),
        ),
        check_vma=False,
    )
```
